512 devices in a mesh: src: 16 (over z_lo, core), slab: 32 (over z_hi, x, y).
Axes of the slice: x: 4, y: 4, z: 16 (z_hi: 2, z_lo: 8; z = z_hi * 8 + z_lo), core: 2. Of those that a mesh axis runs over, the one named last changes fastest.
Arguments:
- conductivity: float32 [128, 32, 128], P('slab'), may hold values from 0.2 to 5
- forward_fields: float32 [16, 128, 32, 128], P('src', 'slab'), may hold values from -6 to 6
- receiver_pairs: int32 [16, 2000, 2], P('src'), may hold values from 0 to 524287
- observed: float32 [16, 2000], replicated, may hold values from -12 to 12
Outputs:
- gradient: float32 [128, 32, 128], P('slab', 'src')
- misfit: float32 [], replicated
The draws below stay inside these ranges and needn't reach their ends.
All inputs are finite; a program needn't handle non-finite values.
Results may differ from the reference program's by a relative error of at most 0.0003.
Values sent between devices are 32-bit elements; how exact they have to be, the bound alone decides.
A program may use at most 64 MiB of HBM per device.

```python
import math
import jax
import jax.numpy as jnp
from jax import lax

NY = 32
NX = 128
RX = 2000
DEG = 2
GROUPS = 16
NZ = 128
NODES = 524288


def draw_observed(key, part):
    key = jax.random.fold_in(key, 7)
    ramp = jnp.arange(GROUPS, dtype=jnp.float32)[:, None] / (GROUPS - 1)
    values = jnp.clip(jax.random.normal(key, (GROUPS, RX), jnp.float32), -4.0, 4.0)
    return values * (1.0 + 2.0 * ramp)


def place_ends(entries, key, smallest, high):
    index_at = [jax.random.randint(jax.random.fold_in(key, axis), (), 0, length) for axis, length in enumerate(entries.shape)]
    widest = entries.shape.index(max(entries.shape))
    beside = index_at[:widest] + [(index_at[widest] + 1) % entries.shape[widest]] + index_at[widest + 1:]
    return entries.at[tuple(index_at)].set(smallest).at[tuple(beside)].set(high)


def shard_levels(stream_key, dims, pieces, least, high):
    level = 1.0
    for position, blocks in pieces:
        heights = jax.random.uniform(jax.random.fold_in(jax.random.fold_in(stream_key, 6), position), (blocks,), jnp.float32, least / len(pieces), high / len(pieces))
        level = level * jnp.repeat(jnp.exp(heights), dims[position] // blocks).reshape((-1,) + (1,) * (len(dims) - 1 - position))
    return level


def noise(key, dims, deviation, most, split=(), kind=jnp.bfloat16):
    level = shard_levels(key, dims, split, -0.22, 0.18) if split else 1.0
    entries = jax.random.normal(key, dims, jnp.float32) * deviation * level
    return jnp.minimum(jnp.maximum(entries, -most), most).astype(kind)


def setup_inputs(seed: int = 0) -> dict:
    seeds = jax.random.split(jax.random.key(seed), 5)
    conductivity = jnp.clip(jnp.exp(math.log(5.0) - 3.218876 * jax.random.uniform(seeds[0], (NZ, NY, NX), jnp.float32) ** shard_levels(seeds[0], (NZ, NY, NX), ((0, 32),), -0.2, 0.2)), 0.2, 5.0)
    forward_fields = noise(seeds[1], (GROUPS, NZ, NY, NX), 1.0, 6.0, ((0, 16), (1, 32)), jnp.float32)
    receiver_pairs = place_ends(jax.random.randint(seeds[2], (GROUPS, RX, 2), 0, NODES), jax.random.fold_in(seeds[2], 1), 0, NODES - 1).astype(jnp.int32)
    observed = draw_observed(jax.random.fold_in(seeds[4], 71), 0)
    return dict(conductivity=conductivity, forward_fields=forward_fields, receiver_pairs=receiver_pairs, observed=observed)


LOWER = 0.3
UPPER = 2.0
OMEGA = 0.6
MASS = (1.0 / 3.0, 1.0 / 6.0, 1.0 / 6.0, 1.0 / 3.0)
STIFF = (1.0, -1.0, -1.0, 1.0)


def mix_pair(matrix, lead, trail):
    return (matrix[0] * lead + matrix[1] * trail, matrix[2] * lead + matrix[3] * trail)


def along_axis(matrix, arrays, stride):
    result = list(arrays)
    for corner in range(8):
        if (corner // stride) % 2 == 0:
            result[corner], result[corner + stride] = mix_pair(matrix, arrays[corner], arrays[corner + stride])
    return result


def element_apply(corners):
    mass_x = along_axis(MASS, corners, 1)
    stiff_x = along_axis(STIFF, corners, 1)
    mass_mass = along_axis(MASS, mass_x, 2)
    stiff_mass = along_axis(STIFF, mass_x, 2)
    mass_stiff = along_axis(MASS, stiff_x, 2)
    joined = [left + right for left, right in zip(stiff_mass, mass_stiff)]
    z_stiff = along_axis(STIFF, mass_mass, 4)
    z_mass = along_axis(MASS, joined, 4)
    return [left + right for left, right in zip(z_stiff, z_mass)]


def assemble(parts):
    depth, rows, cols = parts[0].shape
    total = jnp.zeros_like(parts[0])
    for corner in range(8):
        a_z, b_y, c_x = corner // 4, (corner // 2) % 2, corner % 2
        padded = jnp.pad(parts[corner], ((1, 0), (1, 0), (1, 0)))
        total = total + padded[1 - a_z:1 - a_z + depth, 1 - b_y:1 - b_y + rows, 1 - c_x:1 - c_x + cols]
    return total


def corners_of(field):
    depth, rows, cols = field.shape
    padded = jnp.pad(field, ((0, 1), (0, 1), (0, 1)))
    return [padded[corner // 4:corner // 4 + depth, (corner // 2) % 2:(corner // 2) % 2 + rows,
                   corner % 2:corner % 2 + cols] for corner in range(8)]


def coarse_cells(cells):
    depth, rows, cols = cells.shape
    blocks = cells.reshape(depth // 2, 2, rows // 2, 2, cols // 2, 2)
    return jnp.sum(blocks, axis=(1, 3, 5)) * 0.125


def restrict_axis(field, axis, below):
    length = field.shape[axis]
    even = lax.slice_in_dim(field, 0, length, 2, axis)
    odd = lax.slice_in_dim(field, 1, length, 2, axis)
    before = jnp.concatenate([below, lax.slice_in_dim(odd, 0, odd.shape[axis] - 1, 1, axis)], axis)
    return even + 0.5 * (odd + before)


def prolong_axis(coarse, axis, above):
    length = coarse.shape[axis]
    following = jnp.concatenate([lax.slice_in_dim(coarse, 1, length, 1, axis), above], axis)
    middle = 0.5 * (coarse + following)
    shape = list(coarse.shape)
    shape[axis] = 2 * length
    return jnp.stack([coarse, middle], axis + 1).reshape(shape)


def sweep(lam, resid, diagonal, operate, finish):
    theta = 0.5 * (UPPER + LOWER)
    delta = 0.5 * (UPPER - LOWER)
    ratio = theta / delta
    rho_now = 1.0 / ratio
    direction = resid / theta
    for step in range(DEG):
        lam = lam + direction
        if step < DEG - 1 or finish:
            resid = resid - operate(direction) / diagonal
        if step < DEG - 1:
            rho_next = 1.0 / (2.0 * ratio - rho_now)
            direction = (rho_next * rho_now) * direction + (2.0 * rho_next / delta) * resid
            rho_now = rho_next
    return lam, resid


def solve(rhs, diagonal, coarse_diag, operate, from_below, from_above):
    lam = jnp.zeros_like(rhs)
    resid = rhs / diagonal
    lam, resid = sweep(lam, resid, diagonal, operate, True)
    fine = diagonal * resid
    coarse = restrict_axis(fine, 2, jnp.zeros_like(fine[:, :, :1]))
    coarse = restrict_axis(coarse, 1, jnp.zeros_like(coarse[:, :1, :]))
    coarse = restrict_axis(coarse, 0, from_below(coarse[-1:]))
    correction = OMEGA * coarse / coarse_diag
    refined = prolong_axis(correction, 0, from_above(correction[:1]))
    refined = prolong_axis(refined, 1, jnp.zeros_like(refined[:, :1, :]))
    refined = prolong_axis(refined, 2, jnp.zeros_like(refined[:, :, :1]))
    lam = lam + refined
    resid = resid - operate(refined) / diagonal
    lam, resid = sweep(lam, resid, diagonal, operate, False)
    return lam


def products(lam_corners, field_corners):
    applied = element_apply(field_corners)
    total = lam_corners[0] * applied[0]
    for corner in range(1, 8):
        total = total + lam_corners[corner] * applied[corner]
    return -total


def reference(conductivity, forward_fields, receiver_pairs, observed):
    diagonal = assemble([conductivity * (1.0 / 3.0) for corner in range(8)])
    coarse_cond = coarse_cells(conductivity)
    coarse_diag = assemble([coarse_cond * (2.0 / 3.0) for corner in range(8)])

    def operate(vector):
        return assemble([conductivity * part for part in element_apply(corners_of(vector))])

    def group_step(carry, inputs):
        grad_sum, misfit_sum = carry
        field, pairs, target = inputs
        flat = field.reshape(-1)
        resid_data = flat[pairs[:, 0]] - flat[pairs[:, 1]] - target
        rhs = jnp.zeros(flat.shape, jnp.float32).at[pairs[:, 0]].add(resid_data)
        rhs = rhs.at[pairs[:, 1]].add(-resid_data).reshape(field.shape)
        lam = solve(rhs, diagonal, coarse_diag, operate, jnp.zeros_like, jnp.zeros_like)
        grad = products(corners_of(lam), corners_of(field))
        return (grad_sum + grad, misfit_sum + jnp.sum(0.5 * resid_data * resid_data)), None

    start = (jnp.zeros(conductivity.shape, jnp.float32), jnp.zeros((), jnp.float32))
    (gradient, total), unused = lax.scan(group_step, start, (forward_fields, receiver_pairs, observed))
    return gradient, total / (GROUPS * RX)
```

```python
import functools

import jax
import jax.numpy as jnp
from jax import lax
from jax.experimental import pallas as pl
from jax.experimental.pallas import tpu as pltpu
from jax.sharding import PartitionSpec as P

LOWER = 0.3
UPPER = 2.0
OMEGA = 0.6
THETA = 0.5 * (UPPER + LOWER)
DELTA = 0.5 * (UPPER - LOWER)
RATIO = THETA / DELTA
RHO_A = 1.0 / RATIO
RHO_B = 1.0 / (2.0 * RATIO - RHO_A)
ALPHA = RHO_B * RHO_A
BETA = 2.0 * RHO_B / DELTA

NY, NX = 32, 128
DEPTH = 4
BELOW = 5
PLANES = 15
CELLS = 16
RX = 2000
RROWS = 16
IDX = 2 * RROWS
GROUPS = 16
NZ = 128
MESH = pl.DeviceIdType.MESH
F32 = jnp.float32
ONE, TWO, THREE = 1.0 / 16.0, 1.0 / 24.0, 1.0 / 48.0


def lanes():
    return lax.broadcasted_iota(jnp.int32, (NY, NX), 1)


def rows():
    return lax.broadcasted_iota(jnp.int32, (NY, NX), 0)


def next_x(v):
    return jnp.where(lanes() < NX - 1, pltpu.roll(v, NX - 1, 1), 0.0)


def prev_x(v):
    return jnp.where(lanes() > 0, pltpu.roll(v, 1, 1), 0.0)


def next_y(v):
    return jnp.where(rows() < NY - 1, pltpu.roll(v, NY - 1, 0), 0.0)


def prev_y(v):
    return jnp.where(rows() > 0, pltpu.roll(v, 1, 0), 0.0)


def prev2_x(v):
    return jnp.where(lanes() > 1, pltpu.roll(v, 2, 1), 0.0)


def prev2_y(v):
    return jnp.where(rows() > 1, pltpu.roll(v, 2, 0), 0.0)


def forward(v):
    moved = next_x(v)
    sx, dx = v + moved, v - moved
    ms, md = next_y(sx), next_y(dx)
    return sx + ms, sx - ms, dx + md, dx - md


def cell_terms(low, high):
    ss, ds, sd, dd = low
    ss2, ds2, sd2, dd2 = high
    return (ss - ss2, ds + ds2, ds - ds2, sd + sd2, sd - sd2, dd + dd2, dd - dd2)


def scatter_cell(low, high, c1, c2, c3):
    zss, sds, zds, ssd, zsd, sdd, zdd = cell_terms(low, high)
    zss = zss * c1
    sds, zds = sds * c1, zds * c2
    ssd, zsd = ssd * c1, zsd * c2
    sdd, zdd = sdd * c2, zdd * c3
    lower = (zss, sds + zds, ssd + zsd, sdd + zdd)
    upper = (-zss, sds - zds, ssd - zsd, sdd - zdd)
    return lower, upper


def backward(parts):
    ss, ds, sd, dd = parts
    os = (ss + ds) + prev_y(ss - ds)
    od = (sd + dd) + prev_y(sd - dd)
    return (os + od) + prev_x(os - od)


def apply_planes(v_ref, coef, first, last, sink):
    low = forward(v_ref[first - 1])
    mid = forward(v_ref[first])
    _, upper = scatter_cell(low, mid, coef[0, first - 1], coef[1, first - 1], coef[2, first - 1])

    def body(p, carry):
        here, above = carry[:4], carry[4:]
        ahead = forward(v_ref[p + 1])
        lower, upper = scatter_cell(here, ahead, coef[0, p], coef[1, p], coef[2, p])
        sink(p, backward([a + b for a, b in zip(lower, above)]))
        return (*ahead, *upper)

    lax.fori_loop(first, last + 1, body, (*mid, *upper))


def kernel(
    cond_hbm, field_hbm, pairs_hbm, obs_hbm,
    grad_ref, misfit_ref,
    cext, fext, pairs, obs, index, target,
    part, recv_xy, zsum, recv_z,
    row_at, lane_at, res_at, row_hot, lane_res, coef, diag, invd, cinv, hu,
    resid, direct, work, lam, pe, fine,
    mis, recv_mis, chunks, recv_core, merged, recv_src,
    in_sem, send_sem, halo_sem, xy_sem, z_sem, mis_sem, core_sem, src_sem,
):
    src = lax.axis_index("src")
    slab = lax.axis_index("slab")
    zl, core = src // 2, src % 2
    zh, px, py = slab // 16, (slab // 4) % 4, slab % 4
    plane_peers = [
        (src, zh * 16 + ((px + i) % 4) * 4 + (py + j) % 4)
        for i in range(4)
        for j in range(4)
        if i + j
    ]
    z_peer = (src, (1 - zh) * 16 + px * 4 + py)
    ups = [(src, (slab + k) % 32) for k in (1, 2)]
    downs = [(src, (slab + 32 - k) % 32) for k in (1, 2)]
    src_peers = [(((zl + i) % 8) * 2 + (core + j) % 2, slab) for i in range(8) for j in range(2) if i + j]
    sibling = (zl * 2 + 1 - core, slab)
    run_peers = [(zl + i) % 8 for i in range(1, 8)]

    barrier = pltpu.get_barrier_semaphore()
    greeted = plane_peers + [z_peer] + ups + downs + src_peers
    for peer in greeted:
        pl.semaphore_signal(barrier, inc=1, device_id=peer, device_id_type=MESH)

    loads = [
        pltpu.make_async_copy(field_hbm, fext.at[pl.ds(0, DEPTH)], in_sem.at[0]),
        pltpu.make_async_copy(pairs_hbm, pairs, in_sem.at[1]),
        pltpu.make_async_copy(cond_hbm, cext.at[pl.ds(6, DEPTH)], in_sem.at[2]),
        pltpu.make_async_copy(obs_hbm, obs, in_sem.at[3]),
    ]
    for load in loads:
        load.start()
    for load in loads:
        load.wait()

    index[...] = jnp.full((IDX, NX), 1 << 24, jnp.int32)
    target[...] = jnp.zeros((RROWS, NX), F32)
    for j in range(RROWS):
        width = min(NX, RX - j * NX)
        span = pl.ds(j * NX, width)
        for at, end in ((j, 0), (RROWS + j, 1)):
            index[at : at + 1, 0:width] = pairs[end : end + 1, span]
        mine = lax.broadcasted_iota(jnp.int32, (GROUPS, width), 0) == src
        target[j : j + 1, 0:width] = jnp.sum(
            jnp.where(mine, obs[:, span], 0.0), axis=0, keepdims=True
        )

    lane = jnp.bitwise_and(index[...], NX - 1)
    line = jnp.right_shift(index[...], 7) - slab * (DEPTH * NY)

    def pick(block, acc):
        values = fext[block // 4, pl.ds((block % 4) * 8, 8), :]
        for k in range(8):
            spread = jnp.broadcast_to(values[k : k + 1, :], (IDX, NX))
            found = jnp.take_along_axis(spread, lane, axis=1, mode="promise_in_bounds")
            acc = jnp.where(line == block * 8 + k, found, acc)
        return acc

    picked = lax.fori_loop(0, DEPTH * NY // 8, pick, jnp.zeros((IDX, NX), F32))
    part[...] = picked[:RROWS] - picked[RROWS:]
    here = px * 4 + py
    recv_xy[here] = part[...]

    pl.semaphore_wait(barrier, len(greeted))

    def remote(source, dest, arrival, peer):
        return pltpu.make_async_remote_copy(
            src_ref=source, dst_ref=dest, send_sem=send_sem, recv_sem=arrival,
            device_id=peer, device_id_type=MESH,
        )

    sent = []

    def send(source, dest, arrival, peer):
        copy = remote(source, dest, arrival, peer)
        copy.start()
        sent.append(copy)

    def arrived(buffer, arrival):
        pltpu.make_async_copy(buffer, buffer, arrival).wait()

    for peer in plane_peers:
        send(part, recv_xy.at[here], xy_sem, peer)
    own = cext.at[pl.ds(6, DEPTH)]
    send(own, cext.at[pl.ds(2, DEPTH)], halo_sem.at[0], ups[0])
    send(own, cext.at[pl.ds(10, DEPTH)], halo_sem.at[1], downs[0])
    send(cext.at[pl.ds(8, 2)], cext.at[pl.ds(0, 2)], halo_sem.at[2], ups[1])
    send(cext.at[pl.ds(6, 2)], cext.at[pl.ds(14, 2)], halo_sem.at[3], downs[1])
    send(fext.at[pl.ds(0, 1)], fext.at[pl.ds(DEPTH, 1)], halo_sem.at[4], downs[0])

    place = jnp.right_shift(index[...], 7) - (slab * DEPTH - BELOW) * NY
    for j in range(IDX):
        row_at[j] = place[j : j + 1, :].astype(F32)
        lane_at[j] = lane[j : j + 1, :].astype(F32)

    def hot(j, carry):
        spread = jnp.broadcast_to(row_at[j], (PLANES * NY, NX))
        line_id = lax.broadcasted_iota(jnp.int32, (PLANES * NY, NX), 0).astype(F32)
        row_hot[j] = jnp.where(spread == line_id, 1.0, 0.0).astype(jnp.bfloat16)
        return carry

    lax.fori_loop(0, IDX, hot, 0)

    arrived(recv_xy.at[pl.ds(0, 15)], xy_sem)

    def add_xy(k, acc):
        return acc + recv_xy[k]

    zsum[...] = lax.fori_loop(1, 16, add_xy, recv_xy[0])
    send(zsum, recv_z, z_sem, z_peer)

    arrived(cext.at[pl.ds(2, DEPTH)], halo_sem.at[0])
    arrived(cext.at[pl.ds(10, DEPTH)], halo_sem.at[1])
    arrived(cext.at[pl.ds(0, 2)], halo_sem.at[2])
    arrived(cext.at[pl.ds(14, 2)], halo_sem.at[3])
    arrived(fext.at[pl.ds(DEPTH, 1)], halo_sem.at[4])

    def inside(plane):
        z = slab * DEPTH + plane
        return jnp.logical_and(z >= 0, z < NZ)

    def masked_cells(e):
        return jnp.where(inside(e - 6), cext[e], 0.0)

    def around(cells):
        along = cells + prev_x(cells)
        return along + prev_y(along)

    def diagonals(p, below):
        cells = masked_cells(p + 1)
        coef[0, p] = cells * ONE
        coef[1, p] = cells * TWO
        coef[2, p] = cells * THREE
        boxed = around(cells)
        value = (boxed + below) * (1.0 / 3.0)
        keep = inside(p - BELOW)
        diag[p] = jnp.where(keep, value, 0.0)
        invd[p] = jnp.where(keep, 1.0 / jnp.where(keep, value, 1.0), 0.0)
        return boxed

    lax.fori_loop(0, PLANES, diagonals, around(masked_cells(0)))

    even = jnp.logical_and(lanes() % 2 == 0, rows() % 2 == 0)

    def coarse_box(j):
        pair = masked_cells(2 * j + 2) + masked_cells(2 * j + 3)
        pair = pair + next_y(pair)
        pair = jnp.where(even, pair + next_x(pair), 0.0)
        pair = pair + prev2_x(pair)
        return pair + prev2_y(pair)

    def coarse(j, below):
        boxed = coarse_box(j)
        value = (boxed + below) * (0.125 * 2.0 / 3.0)
        keep = jnp.logical_and(even, inside(2 * (j - 2)))
        cinv[j - 1] = jnp.where(keep, OMEGA / jnp.where(keep, value, 1.0), 0.0)
        return boxed

    lax.fori_loop(1, 6, coarse, coarse_box(0))

    def field_terms(p, low):
        plane = jnp.where(inside(p + 1), fext[p + 1], 0.0)
        high = forward(plane)
        scales = (-ONE, -ONE, -TWO, -ONE, -TWO, -TWO, -THREE)
        for k, (term, scale) in enumerate(zip(cell_terms(low, high), scales)):
            hu[p, k] = term * scale
        return high

    lax.fori_loop(0, DEPTH, field_terms, forward(fext[0]))

    arrived(recv_z, z_sem)
    res = (zsum[...] + recv_z[...]) - target[...]
    half = jnp.sum(jnp.sum(0.5 * res * res, axis=0, keepdims=True), axis=1, keepdims=True)
    mis[...] = jnp.broadcast_to(half, (1, NX))
    recv_mis[src] = mis[...]
    for peer in src_peers:
        send(mis, recv_mis.at[src], mis_sem, peer)

    for j in range(RROWS):
        res_at[j] = res[j : j + 1, :]
        res_at[RROWS + j] = -res[j : j + 1, :]

    def spread_res(j, carry):
        value = jnp.broadcast_to(res_at[j], (NX, NX))
        at = jnp.broadcast_to(lane_at[j], (NX, NX))
        lane_id = lax.broadcasted_iota(jnp.int32, (NX, NX), 0).astype(F32)
        value = jnp.where(at == lane_id, value, 0.0)
        high = value.astype(jnp.bfloat16)
        lane_res[j, 0:NX, :] = high
        lane_res[j, NX:, :] = (value - high.astype(F32)).astype(jnp.bfloat16)
        return carry

    lax.fori_loop(0, IDX, spread_res, 0)

    def product(j, acc):
        both = lax.dot_general(
            row_hot[j], lane_res[j], (((1,), (1,)), ((), ())), preferred_element_type=F32
        )
        fine[...] += both
        return acc

    fine[...] = jnp.zeros_like(fine)
    lax.fori_loop(0, IDX, product, 0)

    def start_resid(p, carry):
        block = fine[pl.ds(pl.multiple_of(p * NY, NY), NY), :]
        resid[p] = (block[:, :NX] + block[:, NX:]) * invd[p]
        return carry

    lax.fori_loop(0, PLANES, start_resid, 0)

    def first_step(p, applied):
        r = resid[p]
        r1 = r - (applied * (1.0 / THETA)) * invd[p]
        d2 = (ALPHA / THETA) * r + BETA * r1
        resid[p] = r1
        direct[p] = d2
        lam[p] = r * (1.0 / THETA) + d2

    apply_planes(resid, coef, 1, 13, first_step)

    def second_step(p, applied):
        r2 = resid[p] - applied * invd[p]
        resid[p] = r2
        f = diag[p] * r2
        f = f + 0.5 * (prev_x(f) + next_x(f))
        work[p] = f + 0.5 * (prev_y(f) + next_y(f))

    apply_planes(direct, coef, 2, 12, second_step)

    def correct(j):
        p = 2 * j + 3
        c = (work[p] + 0.5 * (work[p - 1] + work[p + 1])) * cinv[j]
        c = c + 0.5 * (prev_y(c) + next_y(c))
        return c + 0.5 * (prev_x(c) + next_x(c))

    def prolong(j, below):
        c = correct(j)
        pe[2 * j + 3] = c
        pe[2 * j + 2] = 0.5 * (below + c)
        return c

    first = correct(0)
    pe[3] = first
    lax.fori_loop(1, 5, prolong, first)

    def third_step(p, applied):
        r3 = resid[p] - applied * invd[p]
        resid[p] = r3
        lam[p] = lam[p] + pe[p] + r3 * (1.0 / THETA)

    apply_planes(pe, coef, 4, 10, third_step)

    def fourth_step(p, applied):
        r3 = resid[p]
        r4 = r3 - (applied * (1.0 / THETA)) * invd[p]
        lam[p] = lam[p] + (ALPHA / THETA) * r3 + BETA * r4

    apply_planes(resid, coef, 5, 9, fourth_step)

    low = forward(lam[BELOW])
    for p in range(DEPTH):
        high = forward(lam[BELOW + p + 1])
        total = None
        for k, term in enumerate(cell_terms(low, high)):
            piece = term * hu[p, k]
            total = piece if total is None else total + piece
        low = high
        for z in range(8):
            for c in range(2):
                at = 4 * z + 2 * c
                chunks[c, z, 2 * p : 2 * p + 2, :] = total[at : at + 2, :]

    send(chunks.at[1 - core], recv_core, core_sem, sibling)
    arrived(recv_core, core_sem)
    merged[...] = chunks[core] + recv_core[...]
    for z in run_peers:
        send(merged.at[z], recv_src.at[zl], src_sem, (z * 2 + core, slab))
    recv_src[zl] = merged[zl]
    arrived(recv_mis.at[pl.ds(0, 15)], mis_sem)
    misfit = recv_mis[0]
    for k in range(1, GROUPS):
        misfit = misfit + recv_mis[k]
    misfit_ref[...] = misfit * (1.0 / (GROUPS * RX))
    arrived(recv_src.at[pl.ds(0, 7)], src_sem)
    total = recv_src[0]
    for k in range(1, 8):
        total = total + recv_src[k]
    grad_ref[...] = total
    for copy in sent:
        copy.wait_send()


def on_device(conductivity, forward_fields, receiver_pairs, observed):
    field = forward_fields.reshape(DEPTH, NY, NX)
    pairs = jnp.transpose(receiver_pairs[0])
    plane = (NY, NX)
    any_spec = pl.BlockSpec(memory_space=pl.ANY)
    vmem = pl.BlockSpec(memory_space=pltpu.VMEM)
    dma = pltpu.SemaphoreType.DMA
    grad, misfit = pl.pallas_call(
        kernel,
        name="adjoint_gradient",
        out_shape=(jax.ShapeDtypeStruct((8, NX), F32), jax.ShapeDtypeStruct((1, NX), F32)),
        in_specs=[any_spec] * 4,
        out_specs=(vmem, vmem),
        scratch_shapes=[
            pltpu.VMEM((CELLS, *plane), F32),
            pltpu.VMEM((DEPTH + 1, *plane), F32),
            pltpu.VMEM((2, RX), jnp.int32),
            pltpu.VMEM((GROUPS, RX), F32),
            pltpu.VMEM((IDX, NX), jnp.int32),
            pltpu.VMEM((RROWS, NX), F32),
            pltpu.VMEM((RROWS, NX), F32),
            pltpu.VMEM((16, RROWS, NX), F32),
            pltpu.VMEM((RROWS, NX), F32),
            pltpu.VMEM((RROWS, NX), F32),
            pltpu.VMEM((IDX, 1, NX), F32),
            pltpu.VMEM((IDX, 1, NX), F32),
            pltpu.VMEM((IDX, 1, NX), F32),
            pltpu.VMEM((IDX, PLANES * NY, NX), jnp.bfloat16),
            pltpu.VMEM((IDX, 2 * NX, NX), jnp.bfloat16),
            pltpu.VMEM((3, PLANES, *plane), F32),
            pltpu.VMEM((PLANES, *plane), F32),
            pltpu.VMEM((PLANES, *plane), F32),
            pltpu.VMEM((5, *plane), F32),
            pltpu.VMEM((DEPTH, 7, *plane), F32),
            pltpu.VMEM((PLANES, *plane), F32),
            pltpu.VMEM((PLANES, *plane), F32),
            pltpu.VMEM((PLANES, *plane), F32),
            pltpu.VMEM((PLANES, *plane), F32),
            pltpu.VMEM((PLANES, *plane), F32),
            pltpu.VMEM((PLANES * NY, 2 * NX), F32),
            pltpu.VMEM((1, NX), F32),
            pltpu.VMEM((GROUPS, 1, NX), F32),
            pltpu.VMEM((2, 8, 8, NX), F32),
            pltpu.VMEM((8, 8, NX), F32),
            pltpu.VMEM((8, 8, NX), F32),
            pltpu.VMEM((8, 8, NX), F32),
            dma((4,)), dma, dma((5,)), dma, dma, dma, dma, dma,
        ],
        compiler_params=pltpu.CompilerParams(
            collective_id=0, has_side_effects=True, vmem_limit_bytes=32 * 1024 * 1024
        ),
    )(conductivity, field, pairs, observed)
    return grad.reshape(DEPTH, 2, NX), misfit[0, 0]


def solution(mesh):
    in_specs = (P("slab", None, None), P("src", "slab", None, None), P("src", None, None), P())
    out_specs = (P("slab", "src", None), P())
    return jax.shard_map(
        on_device, mesh=mesh, in_specs=in_specs, out_specs=out_specs, check_vma=False
    )
```

```python
import functools

import jax
import jax.numpy as jnp
from jax import lax
from jax.experimental import pallas as pl
from jax.experimental.pallas import tpu as pltpu
from jax.sharding import PartitionSpec as P

LOWER = 0.3
UPPER = 2.0
OMEGA = 0.6
THETA = 0.5 * (UPPER + LOWER)
DELTA = 0.5 * (UPPER - LOWER)
RATIO = THETA / DELTA
RHO_A = 1.0 / RATIO
RHO_B = 1.0 / (2.0 * RATIO - RHO_A)
ALPHA = RHO_B * RHO_A
BETA = 2.0 * RHO_B / DELTA

NY, NX = 32, 128
DEPTH = 4
BELOW = 5
BLOCK = 15
PLANES = 15
CELLS = 16
RX = 2000
RROWS = 16
IDX = 2 * RROWS
GROUPS = 16
NZ = 128
MESH = pl.DeviceIdType.MESH
F32 = jnp.float32
ONE, TWO, THREE = 1.0 / 16.0, 1.0 / 24.0, 1.0 / 48.0


def lanes():
    return lax.broadcasted_iota(jnp.int32, (NY, NX), 1)


def rows():
    return lax.broadcasted_iota(jnp.int32, (NY, NX), 0)


def next_x(v):
    return jnp.where(lanes() < NX - 1, pltpu.roll(v, NX - 1, 1), 0.0)


def prev_x(v):
    return jnp.where(lanes() > 0, pltpu.roll(v, 1, 1), 0.0)


def next_y(v):
    return jnp.where(rows() < NY - 1, pltpu.roll(v, NY - 1, 0), 0.0)


def prev_y(v):
    return jnp.where(rows() > 0, pltpu.roll(v, 1, 0), 0.0)


def prev2_x(v):
    return jnp.where(lanes() > 1, pltpu.roll(v, 2, 1), 0.0)


def prev2_y(v):
    return jnp.where(rows() > 1, pltpu.roll(v, 2, 0), 0.0)


def forward(v):
    moved = next_x(v)
    sx, dx = v + moved, v - moved
    ms, md = next_y(sx), next_y(dx)
    return sx + ms, sx - ms, dx + md, dx - md


def cell_terms(low, high):
    ss, ds, sd, dd = low
    ss2, ds2, sd2, dd2 = high
    return (ss - ss2, ds + ds2, ds - ds2, sd + sd2, sd - sd2, dd + dd2, dd - dd2)


def scatter_cell(low, high, c1, c2, c3):
    zss, sds, zds, ssd, zsd, sdd, zdd = cell_terms(low, high)
    zss = zss * c1
    sds, zds = sds * c1, zds * c2
    ssd, zsd = ssd * c1, zsd * c2
    sdd, zdd = sdd * c2, zdd * c3
    lower = (zss, sds + zds, ssd + zsd, sdd + zdd)
    upper = (-zss, sds - zds, ssd - zsd, sdd - zdd)
    return lower, upper


def backward(parts):
    ss, ds, sd, dd = parts
    os = (ss + ds) + prev_y(ss - ds)
    od = (sd + dd) + prev_y(sd - dd)
    return (os + od) + prev_x(os - od)


def apply_planes(v_ref, coef, first, last, sink):
    low = forward(v_ref[first - 1])
    mid = forward(v_ref[first])
    _, upper = scatter_cell(low, mid, coef[0, first - 1], coef[1, first - 1], coef[2, first - 1])

    def body(p, carry):
        here, above = carry[:4], carry[4:]
        ahead = forward(v_ref[p + 1])
        lower, upper = scatter_cell(here, ahead, coef[0, p], coef[1, p], coef[2, p])
        sink(p, backward([a + b for a, b in zip(lower, above)]))
        return (*ahead, *upper)

    lax.fori_loop(first, last + 1, body, (*mid, *upper), unroll=True)


def read_pairs(pairs, index, place_row, lane_row, slab):
    index[...] = jnp.full((IDX, NX), 1 << 24, jnp.int32)
    for j in range(RROWS):
        width = min(NX, RX - j * NX)
        for at, end in ((j, 0), (RROWS + j, 1)):
            index[at : at + 1, 0:width] = pairs[end : end + 1, pl.ds(j * NX, width)]
    lane = jnp.bitwise_and(index[...], NX - 1).astype(F32)
    place = (jnp.right_shift(index[...], 7) - (slab * DEPTH - BELOW) * NY).astype(F32)
    for j in range(IDX):
        place_row[j] = place[j : j + 1, :]
        lane_row[j] = lane[j : j + 1, :]


def read_target(obs, target, src):
    target[...] = jnp.zeros((RROWS, NX), F32)
    for j in range(RROWS):
        width = min(NX, RX - j * NX)
        mine = lax.broadcasted_iota(jnp.int32, (GROUPS, width), 0) == src
        target[j : j + 1, 0:width] = jnp.sum(
            jnp.where(mine, obs[:, pl.ds(j * NX, width)], 0.0), axis=0, keepdims=True
        )


def gather(fext, index, part, slab):
    lane = jnp.bitwise_and(index[...], NX - 1)
    line = jnp.right_shift(index[...], 7) - slab * (DEPTH * NY)

    def pick(block, acc):
        values = fext[block // 4, pl.ds((block % 4) * 8, 8), :]
        for k in range(8):
            spread = jnp.broadcast_to(values[k : k + 1, :], (IDX, NX))
            found = jnp.take_along_axis(spread, lane, axis=1, mode="promise_in_bounds")
            acc = jnp.where(line == block * 8 + k, found, acc)
        return acc

    picked = lax.fori_loop(0, DEPTH * NY // 8, pick, jnp.zeros((IDX, NX), F32))
    part[...] = picked[:RROWS] - picked[RROWS:]


def one_hot_rows(place_row, row_hot):
    def hot(j, carry):
        spread = jnp.broadcast_to(place_row[j], (PLANES * NY, NX))
        line_id = lax.broadcasted_iota(jnp.int32, (PLANES * NY, NX), 0).astype(F32)
        row_hot[:, pl.ds(pl.multiple_of(j * NX, NX), NX)] = jnp.where(spread == line_id, 1.0, 0.0).astype(jnp.bfloat16)
        return carry

    lax.fori_loop(0, IDX, hot, 0)


def inside(plane, slab):
    z = slab * DEPTH + plane
    return jnp.logical_and(z >= 0, z < NZ)


def conductivity_terms(cext, coef, diag, invd, cinv, slab):
    def masked_cells(e):
        return jnp.where(inside(e - 6, slab), cext[e], 0.0)

    def around(cells):
        along = cells + prev_x(cells)
        return along + prev_y(along)

    def diagonals(p, below):
        cells = masked_cells(p + 1)
        coef[0, p] = cells * ONE
        coef[1, p] = cells * TWO
        coef[2, p] = cells * THREE
        boxed = around(cells)
        value = (boxed + below) * (1.0 / 3.0)
        keep = inside(p - BELOW, slab)
        diag[p] = jnp.where(keep, value, 0.0)
        invd[p] = jnp.where(keep, 1.0 / jnp.where(keep, value, 1.0), 0.0)
        return boxed

    lax.fori_loop(0, PLANES, diagonals, around(masked_cells(0)))

    even = jnp.logical_and(lanes() % 2 == 0, rows() % 2 == 0)

    def coarse_box(j):
        pair = masked_cells(2 * j + 2) + masked_cells(2 * j + 3)
        pair = pair + next_y(pair)
        pair = jnp.where(even, pair + next_x(pair), 0.0)
        pair = pair + prev2_x(pair)
        return pair + prev2_y(pair)

    def coarse(j, below):
        boxed = coarse_box(j)
        value = (boxed + below) * (0.125 * 2.0 / 3.0)
        keep = jnp.logical_and(even, inside(2 * (j - 2), slab))
        cinv[j - 1] = jnp.where(keep, OMEGA / jnp.where(keep, value, 1.0), 0.0)
        return boxed

    lax.fori_loop(1, 6, coarse, coarse_box(0))


def field_terms(fext, hu, slab):
    def terms(p, low):
        high = forward(jnp.where(inside(p + 1, slab), fext[p + 1], 0.0))
        scales = (-ONE, -ONE, -TWO, -ONE, -TWO, -TWO, -THREE)
        for k, (term, scale) in enumerate(zip(cell_terms(low, high), scales)):
            hu[p, k] = term * scale
        return high

    lax.fori_loop(0, DEPTH, terms, forward(fext[0]))


def spread_residual(res_row, lane_row, lane_res):
    def spread(j, carry):
        value = jnp.broadcast_to(res_row[j], (NX, NX))
        at = jnp.broadcast_to(lane_row[j], (NX, NX))
        lane_id = lax.broadcasted_iota(jnp.int32, (NX, NX), 0).astype(F32)
        value = jnp.where(at == lane_id, value, 0.0)
        high = value.astype(jnp.bfloat16)
        columns = pl.ds(pl.multiple_of(j * NX, NX), NX)
        lane_res[0:NX, columns] = high
        lane_res[NX:, columns] = (value - high.astype(F32)).astype(jnp.bfloat16)
        return carry

    lax.fori_loop(0, IDX, spread, 0)


def scatter(row_hot, lane_res, invd, resid):
    def product(q, carry):
        span = pl.ds(pl.multiple_of(q * (BLOCK * NY), BLOCK * NY), BLOCK * NY)
        both = lax.dot_general(
            row_hot[span, :], lane_res[...], (((1,), (1,)), ((), ())), preferred_element_type=F32
        )
        rhs = (both[:, :NX] + both[:, NX:]).reshape(BLOCK, NY, NX)
        planes = pl.ds(q * BLOCK, BLOCK)
        resid[planes] = rhs * invd[planes]
        return carry

    lax.fori_loop(0, PLANES // BLOCK, product, 0)


def solve(coef, diag, invd, cinv, resid, direct, work, pe, lam):
    def first_step(p, applied):
        r = resid[p]
        r1 = r - (applied * (1.0 / THETA)) * invd[p]
        d2 = (ALPHA / THETA) * r + BETA * r1
        resid[p] = r1
        direct[p] = d2
        lam[p] = r * (1.0 / THETA) + d2

    apply_planes(resid, coef, 1, 13, first_step)

    def second_step(p, applied):
        r2 = resid[p] - applied * invd[p]
        resid[p] = r2
        f = diag[p] * r2
        f = f + 0.5 * (prev_x(f) + next_x(f))
        work[p] = f + 0.5 * (prev_y(f) + next_y(f))

    apply_planes(direct, coef, 2, 12, second_step)

    def correct(j):
        p = 2 * j + 3
        c = (work[p] + 0.5 * (work[p - 1] + work[p + 1])) * cinv[j]
        c = c + 0.5 * (prev_y(c) + next_y(c))
        return c + 0.5 * (prev_x(c) + next_x(c))

    def prolong(j, below):
        c = correct(j)
        pe[2 * j + 3] = c
        pe[2 * j + 2] = 0.5 * (below + c)
        return c

    first = correct(0)
    pe[3] = first
    lax.fori_loop(1, 5, prolong, first)

    def third_step(p, applied):
        r3 = resid[p] - applied * invd[p]
        resid[p] = r3
        lam[p] = lam[p] + pe[p] + r3 * (1.0 / THETA)

    apply_planes(pe, coef, 4, 10, third_step)

    def fourth_step(p, applied):
        r3 = resid[p]
        r4 = r3 - (applied * (1.0 / THETA)) * invd[p]
        lam[p] = lam[p] + (ALPHA / THETA) * r3 + BETA * r4

    apply_planes(resid, coef, 5, 9, fourth_step)


def cell_products(lam, hu, chunks):
    low = forward(lam[BELOW])
    for p in range(DEPTH):
        high = forward(lam[BELOW + p + 1])
        total = None
        for k, term in enumerate(cell_terms(low, high)):
            piece = term * hu[p, k]
            total = piece if total is None else total + piece
        low = high
        for z in range(8):
            for c in range(2):
                at = 4 * z + 2 * c
                chunks[c, z, 2 * p : 2 * p + 2, :] = total[at : at + 2, :]


def kernel(
    cond_hbm, field_hbm, pairs_hbm, obs_hbm,
    grad_ref, misfit_ref,
    cext, fext, pairs, obs, index, target,
    part, recv_xy, zsum, recv_z,
    place_row, lane_row, res_row, row_hot, lane_res, coef, diag, invd, cinv, hu,
    resid, direct, work, lam, pe,
    mis, recv_mis, chunks, recv_core, merged, recv_src,
    in_sem, send_sem, halo_sem, xy_sem, z_sem, mis_sem, core_sem, src_sem,
):
    src = lax.axis_index("src")
    slab = lax.axis_index("slab")
    zl, core = src // 2, src % 2
    zh, px, py = slab // 16, (slab // 4) % 4, slab % 4
    here = px * 4 + py
    plane_peers = [
        (src, zh * 16 + ((px + i) % 4) * 4 + (py + j) % 4)
        for i in range(4)
        for j in range(4)
        if i + j
    ]
    z_peer = (src, (1 - zh) * 16 + px * 4 + py)
    ups = [(src, (slab + k) % 32) for k in (1, 2)]
    downs = [(src, (slab + 32 - k) % 32) for k in (1, 2)]
    src_peers = [(((zl + i) % 8) * 2 + (core + j) % 2, slab) for i in range(8) for j in range(2) if i + j]
    sibling = (zl * 2 + 1 - core, slab)
    run_peers = [(zl + i) % 8 for i in range(1, 8)]

    barrier = pltpu.get_barrier_semaphore()
    greeted = plane_peers + [z_peer] + ups + downs + src_peers
    for peer in greeted:
        pl.semaphore_signal(barrier, inc=1, device_id=peer, device_id_type=MESH)

    loads = [
        pltpu.make_async_copy(pairs_hbm, pairs, in_sem.at[0]),
        pltpu.make_async_copy(field_hbm, fext.at[pl.ds(0, DEPTH)], in_sem.at[1]),
        pltpu.make_async_copy(cond_hbm, cext.at[pl.ds(6, DEPTH)], in_sem.at[2]),
        pltpu.make_async_copy(obs_hbm, obs, in_sem.at[3]),
    ]
    for load in loads:
        load.start()
    loads[0].wait()
    read_pairs(pairs, index, place_row, lane_row, slab)
    loads[1].wait()
    gather(fext, index, part, slab)
    recv_xy[here] = part[...]
    loads[2].wait()

    sent = []

    def send(source, dest, arrival, peer):
        copy = pltpu.make_async_remote_copy(
            src_ref=source, dst_ref=dest, send_sem=send_sem, recv_sem=arrival,
            device_id=peer, device_id_type=MESH,
        )
        copy.start()
        sent.append(copy)

    def arrived(buffer, arrival):
        pltpu.make_async_copy(buffer, buffer, arrival).wait()

    pl.semaphore_wait(barrier, len(greeted))
    for peer in plane_peers:
        send(part, recv_xy.at[here], xy_sem, peer)
    own = cext.at[pl.ds(6, DEPTH)]
    send(own, cext.at[pl.ds(2, DEPTH)], halo_sem.at[0], ups[0])
    send(own, cext.at[pl.ds(10, DEPTH)], halo_sem.at[1], downs[0])
    send(cext.at[pl.ds(8, 2)], cext.at[pl.ds(0, 2)], halo_sem.at[2], ups[1])
    send(cext.at[pl.ds(6, 2)], cext.at[pl.ds(14, 2)], halo_sem.at[3], downs[1])
    send(fext.at[pl.ds(0, 1)], fext.at[pl.ds(DEPTH, 1)], halo_sem.at[4], downs[0])
    loads[3].wait()
    read_target(obs, target, src)
    one_hot_rows(place_row, row_hot)

    arrived(recv_xy.at[pl.ds(0, 15)], xy_sem)
    zsum[...] = lax.fori_loop(1, 16, lambda k, acc: acc + recv_xy[k], recv_xy[0])
    send(zsum, recv_z, z_sem, z_peer)

    arrived(cext.at[pl.ds(2, DEPTH)], halo_sem.at[0])
    arrived(cext.at[pl.ds(10, DEPTH)], halo_sem.at[1])
    arrived(cext.at[pl.ds(0, 2)], halo_sem.at[2])
    arrived(cext.at[pl.ds(14, 2)], halo_sem.at[3])
    arrived(fext.at[pl.ds(DEPTH, 1)], halo_sem.at[4])
    conductivity_terms(cext, coef, diag, invd, cinv, slab)
    field_terms(fext, hu, slab)

    arrived(recv_z, z_sem)
    res = (zsum[...] + recv_z[...]) - target[...]
    for j in range(RROWS):
        res_row[j] = res[j : j + 1, :]
        res_row[RROWS + j] = -res[j : j + 1, :]
    half = jnp.sum(jnp.sum(0.5 * res * res, axis=0, keepdims=True), axis=1, keepdims=True)
    mis[...] = jnp.broadcast_to(half, (1, NX))
    recv_mis[src] = mis[...]
    for peer in src_peers:
        send(mis, recv_mis.at[src], mis_sem, peer)

    spread_residual(res_row, lane_row, lane_res)
    scatter(row_hot, lane_res, invd, resid)
    solve(coef, diag, invd, cinv, resid, direct, work, pe, lam)
    cell_products(lam, hu, chunks)

    send(chunks.at[1 - core], recv_core, core_sem, sibling)
    arrived(recv_core, core_sem)
    merged[...] = chunks[core] + recv_core[...]
    for z in run_peers:
        send(merged.at[z], recv_src.at[zl], src_sem, (z * 2 + core, slab))
    recv_src[zl] = merged[zl]
    arrived(recv_mis.at[pl.ds(0, 15)], mis_sem)
    misfit = recv_mis[0]
    for k in range(1, GROUPS):
        misfit = misfit + recv_mis[k]
    misfit_ref[...] = misfit * (1.0 / (GROUPS * RX))
    arrived(recv_src.at[pl.ds(0, 7)], src_sem)
    total = recv_src[0]
    for k in range(1, 8):
        total = total + recv_src[k]
    grad_ref[...] = total
    for copy in sent:
        copy.wait_send()


def on_device(conductivity, forward_fields, receiver_pairs, observed):
    field = forward_fields.reshape(DEPTH, NY, NX)
    pairs = jnp.transpose(receiver_pairs[0])
    conductivity, field, pairs, observed = (
        pltpu.with_memory_space_constraint(a, pltpu.HBM) for a in (conductivity, field, pairs, observed)
    )
    plane = (NY, NX)
    any_spec = pl.BlockSpec(memory_space=pltpu.HBM)
    vmem = pl.BlockSpec(memory_space=pltpu.VMEM)
    dma = pltpu.SemaphoreType.DMA
    grad, misfit = pl.pallas_call(
        kernel,
        name="adjoint_gradient",
        out_shape=(jax.ShapeDtypeStruct((8, NX), F32), jax.ShapeDtypeStruct((1, NX), F32)),
        in_specs=[any_spec] * 4,
        out_specs=(vmem, vmem),
        scratch_shapes=[
            pltpu.VMEM((CELLS, *plane), F32),
            pltpu.VMEM((DEPTH + 1, *plane), F32),
            pltpu.VMEM((2, RX), jnp.int32),
            pltpu.VMEM((GROUPS, RX), F32),
            pltpu.VMEM((IDX, NX), jnp.int32),
            pltpu.VMEM((RROWS, NX), F32),
            pltpu.VMEM((RROWS, NX), F32),
            pltpu.VMEM((16, RROWS, NX), F32),
            pltpu.VMEM((RROWS, NX), F32),
            pltpu.VMEM((RROWS, NX), F32),
            pltpu.VMEM((IDX, 1, NX), F32),
            pltpu.VMEM((IDX, 1, NX), F32),
            pltpu.VMEM((IDX, 1, NX), F32),
            pltpu.VMEM((PLANES * NY, IDX * NX), jnp.bfloat16),
            pltpu.VMEM((2 * NX, IDX * NX), jnp.bfloat16),
            pltpu.VMEM((3, PLANES, *plane), F32),
            pltpu.VMEM((PLANES, *plane), F32),
            pltpu.VMEM((PLANES, *plane), F32),
            pltpu.VMEM((5, *plane), F32),
            pltpu.VMEM((DEPTH, 7, *plane), F32),
            pltpu.VMEM((PLANES, *plane), F32),
            pltpu.VMEM((PLANES, *plane), F32),
            pltpu.VMEM((PLANES, *plane), F32),
            pltpu.VMEM((PLANES, *plane), F32),
            pltpu.VMEM((PLANES, *plane), F32),
            pltpu.VMEM((1, NX), F32),
            pltpu.VMEM((GROUPS, 1, NX), F32),
            pltpu.VMEM((2, 8, 8, NX), F32),
            pltpu.VMEM((8, 8, NX), F32),
            pltpu.VMEM((8, 8, NX), F32),
            pltpu.VMEM((8, 8, NX), F32),
            dma((4,)), dma, dma((5,)), dma, dma, dma, dma, dma,
        ],
        compiler_params=pltpu.CompilerParams(
            collective_id=0, has_side_effects=True, vmem_limit_bytes=32 * 1024 * 1024
        ),
    )(conductivity, field, pairs, observed)
    return grad.reshape(DEPTH, 2, NX), misfit[0, 0]


def solution(mesh):
    in_specs = (P("slab", None, None), P("src", "slab", None, None), P("src", None, None), P())
    out_specs = (P("slab", "src", None), P())
    return jax.shard_map(
        on_device, mesh=mesh, in_specs=in_specs, out_specs=out_specs, check_vma=False
    )
```

```python
import functools

import jax
import jax.numpy as jnp
from jax import lax
from jax.experimental import pallas as pl
from jax.experimental.pallas import tpu as pltpu
from jax.sharding import PartitionSpec as P

LOWER = 0.3
UPPER = 2.0
OMEGA = 0.6
THETA = 0.5 * (UPPER + LOWER)
DELTA = 0.5 * (UPPER - LOWER)
RATIO = THETA / DELTA
RHO_A = 1.0 / RATIO
RHO_B = 1.0 / (2.0 * RATIO - RHO_A)
ALPHA = RHO_B * RHO_A
BETA = 2.0 * RHO_B / DELTA

NY, NX = 32, 128
DEPTH = 4
BELOW = 5
BLOCK = 15
PLANES = 15
CELLS = 16
RX = 2000
RROWS = 16
IDX = 2 * RROWS
GROUPS = 16
CROSSING = ((14, 16), (15, 16), (15, 17))
NZ = 128
MESH = pl.DeviceIdType.MESH
F32 = jnp.float32
ONE, TWO, THREE = 1.0 / 16.0, 1.0 / 24.0, 1.0 / 48.0


def lanes():
    return lax.broadcasted_iota(jnp.int32, (NY, NX), 1)


def rows():
    return lax.broadcasted_iota(jnp.int32, (NY, NX), 0)


def next_x(v):
    return jnp.where(lanes() < NX - 1, pltpu.roll(v, NX - 1, 1), 0.0)


def prev_x(v):
    return jnp.where(lanes() > 0, pltpu.roll(v, 1, 1), 0.0)


def next_y(v):
    return jnp.where(rows() < NY - 1, pltpu.roll(v, NY - 1, 0), 0.0)


def prev_y(v):
    return jnp.where(rows() > 0, pltpu.roll(v, 1, 0), 0.0)


def prev2_x(v):
    return jnp.where(lanes() > 1, pltpu.roll(v, 2, 1), 0.0)


def prev2_y(v):
    return jnp.where(rows() > 1, pltpu.roll(v, 2, 0), 0.0)


def forward(v):
    moved = next_x(v)
    sx, dx = v + moved, v - moved
    ms, md = next_y(sx), next_y(dx)
    return sx + ms, sx - ms, dx + md, dx - md


def cell_terms(low, high):
    ss, ds, sd, dd = low
    ss2, ds2, sd2, dd2 = high
    return (ss - ss2, ds + ds2, ds - ds2, sd + sd2, sd - sd2, dd + dd2, dd - dd2)


def scatter_cell(low, high, c1, c2, c3):
    zss, sds, zds, ssd, zsd, sdd, zdd = cell_terms(low, high)
    zss = zss * c1
    sds, zds = sds * c1, zds * c2
    ssd, zsd = ssd * c1, zsd * c2
    sdd, zdd = sdd * c2, zdd * c3
    lower = (zss, sds + zds, ssd + zsd, sdd + zdd)
    upper = (-zss, sds - zds, ssd - zsd, sdd - zdd)
    return lower, upper


def backward(parts):
    ss, ds, sd, dd = parts
    os = (ss + ds) + prev_y(ss - ds)
    od = (sd + dd) + prev_y(sd - dd)
    return (os + od) + prev_x(os - od)


def apply_planes(v_ref, coef, first, last, sink):
    low = forward(v_ref[first - 1])
    mid = forward(v_ref[first])
    _, upper = scatter_cell(low, mid, coef[0, first - 1], coef[1, first - 1], coef[2, first - 1])

    def body(p, carry):
        here, above = carry[:4], carry[4:]
        ahead = forward(v_ref[p + 1])
        lower, upper = scatter_cell(here, ahead, coef[0, p], coef[1, p], coef[2, p])
        sink(p, backward([a + b for a, b in zip(lower, above)]))
        return (*ahead, *upper)

    lax.fori_loop(first, last + 1, body, (*mid, *upper), unroll=True)


def read_pairs(pairs, index, place_row, lane_row, slab):
    index[...] = jnp.full((IDX, NX), 1 << 24, jnp.int32)
    for j in range(RROWS):
        width = min(NX, RX - j * NX)
        for at, end in ((j, 0), (RROWS + j, 1)):
            index[at : at + 1, 0:width] = pairs[end : end + 1, pl.ds(j * NX, width)]
    lane = jnp.bitwise_and(index[...], NX - 1).astype(F32)
    place = (jnp.right_shift(index[...], 7) - (slab * DEPTH - BELOW) * NY).astype(F32)
    for j in range(IDX):
        place_row[j] = place[j : j + 1, :]
        lane_row[j] = lane[j : j + 1, :]


def read_target(obs, target, src):
    target[...] = jnp.zeros((RROWS, NX), F32)
    for j in range(RROWS):
        width = min(NX, RX - j * NX)
        mine = lax.broadcasted_iota(jnp.int32, (GROUPS, width), 0) == src
        target[j : j + 1, 0:width] = jnp.sum(
            jnp.where(mine, obs[:, pl.ds(j * NX, width)], 0.0), axis=0, keepdims=True
        )


def gather(fext, index, part, slab):
    lane = jnp.bitwise_and(index[...], NX - 1)
    line = jnp.right_shift(index[...], 7) - slab * (DEPTH * NY)

    def pick(block, acc):
        values = fext[block // 4, pl.ds((block % 4) * 8, 8), :]
        for k in range(8):
            spread = jnp.broadcast_to(values[k : k + 1, :], (IDX, NX))
            found = jnp.take_along_axis(spread, lane, axis=1, mode="promise_in_bounds")
            acc = jnp.where(line == block * 8 + k, found, acc)
        return acc

    picked = lax.fori_loop(0, DEPTH * NY // 8, pick, jnp.zeros((IDX, NX), F32), unroll=True)
    part[...] = picked[:RROWS] - picked[RROWS:]


def one_hots(place_row, lane_row, row_hot, lane_hot):
    def hot(j, carry):
        columns = pl.ds(pl.multiple_of(j * NX, NX), NX)
        for at, out, size in ((place_row, row_hot, PLANES * NY), (lane_row, lane_hot, NX)):
            spread = jnp.broadcast_to(at[j], (size, NX))
            line_id = lax.broadcasted_iota(jnp.int32, (size, NX), 0).astype(F32)
            out[:, columns] = jnp.where(spread == line_id, 1.0, 0.0).astype(jnp.bfloat16)
        return carry

    lax.fori_loop(0, IDX, hot, 0)


def inside(plane, slab):
    z = slab * DEPTH + plane
    return jnp.logical_and(z >= 0, z < NZ)


def conductivity_terms(cext, coef, diag, invd, cinv, slab):
    def masked_cells(e):
        return jnp.where(inside(e - 6, slab), cext[e], 0.0)

    def around(cells):
        along = cells + prev_x(cells)
        return along + prev_y(along)

    def diagonals(p, below):
        cells = masked_cells(p + 1)
        coef[0, p] = cells * ONE
        coef[1, p] = cells * TWO
        coef[2, p] = cells * THREE
        boxed = around(cells)
        value = (boxed + below) * (1.0 / 3.0)
        keep = inside(p - BELOW, slab)
        diag[p] = jnp.where(keep, value, 0.0)
        invd[p] = jnp.where(keep, 1.0 / jnp.where(keep, value, 1.0), 0.0)
        return boxed

    lax.fori_loop(0, PLANES, diagonals, around(masked_cells(0)), unroll=5)

    even = jnp.logical_and(lanes() % 2 == 0, rows() % 2 == 0)

    def coarse_box(j):
        pair = masked_cells(2 * j + 2) + masked_cells(2 * j + 3)
        pair = pair + next_y(pair)
        pair = jnp.where(even, pair + next_x(pair), 0.0)
        pair = pair + prev2_x(pair)
        return pair + prev2_y(pair)

    def coarse(j, below):
        boxed = coarse_box(j)
        value = (boxed + below) * (0.125 * 2.0 / 3.0)
        keep = jnp.logical_and(even, inside(2 * (j - 2), slab))
        cinv[j - 1] = jnp.where(keep, OMEGA / jnp.where(keep, value, 1.0), 0.0)
        return boxed

    lax.fori_loop(1, 6, coarse, coarse_box(0), unroll=True)


def field_terms(fext, hu, slab):
    def terms(p, low):
        high = forward(jnp.where(inside(p + 1, slab), fext[p + 1], 0.0))
        scales = (-ONE, -ONE, -TWO, -ONE, -TWO, -TWO, -THREE)
        for k, (term, scale) in enumerate(zip(cell_terms(low, high), scales)):
            hu[p, k] = term * scale
        return high

    lax.fori_loop(0, DEPTH, terms, forward(fext[0]), unroll=True)


def spread_residual(res_row, lane_hot, lane_res):
    def spread(j, carry):
        columns = pl.ds(pl.multiple_of(j * NX, NX), NX)
        value = jnp.broadcast_to(res_row[j], (16, NX))
        high = value.astype(jnp.bfloat16)
        low = (value - high.astype(F32)).astype(jnp.bfloat16)
        hot = lane_hot[:, columns].reshape(NX // 16, 16, NX)
        lane_res[0:NX, columns] = (hot * high[None]).reshape(NX, NX)
        lane_res[NX:, columns] = (hot * low[None]).reshape(NX, NX)
        return carry

    lax.fori_loop(0, IDX, spread, 0, unroll=4)


def scatter(row_hot, lane_res, invd, resid):
    def product(q, carry):
        span = pl.ds(pl.multiple_of(q * (BLOCK * NY), BLOCK * NY), BLOCK * NY)
        both = lax.dot_general(
            row_hot[span, :], lane_res[...], (((1,), (1,)), ((), ())), preferred_element_type=F32
        )
        rhs = (both[:, :NX] + both[:, NX:]).reshape(BLOCK, NY, NX)
        planes = pl.ds(q * BLOCK, BLOCK)
        resid[planes] = rhs * invd[planes]
        return carry

    lax.fori_loop(0, PLANES // BLOCK, product, 0)


def solve(coef, diag, invd, cinv, resid, direct, work, pe, lam):
    def first_step(p, applied):
        r = resid[p]
        r1 = r - (applied * (1.0 / THETA)) * invd[p]
        d2 = (ALPHA / THETA) * r + BETA * r1
        resid[p] = r1
        direct[p] = d2
        lam[p] = r * (1.0 / THETA) + d2

    apply_planes(resid, coef, 1, 13, first_step)

    def second_step(p, applied):
        r2 = resid[p] - applied * invd[p]
        resid[p] = r2
        f = diag[p] * r2
        f = f + 0.5 * (prev_x(f) + next_x(f))
        work[p] = f + 0.5 * (prev_y(f) + next_y(f))

    apply_planes(direct, coef, 2, 12, second_step)

    def correct(j):
        p = 2 * j + 3
        c = (work[p] + 0.5 * (work[p - 1] + work[p + 1])) * cinv[j]
        c = c + 0.5 * (prev_y(c) + next_y(c))
        return c + 0.5 * (prev_x(c) + next_x(c))

    def prolong(j, below):
        c = correct(j)
        pe[2 * j + 3] = c
        pe[2 * j + 2] = 0.5 * (below + c)
        return c

    first = correct(0)
    pe[3] = first
    lax.fori_loop(1, 5, prolong, first, unroll=True)

    def third_step(p, applied):
        r3 = resid[p] - applied * invd[p]
        resid[p] = r3
        lam[p] = lam[p] + pe[p] + r3 * (1.0 / THETA)

    apply_planes(pe, coef, 4, 10, third_step)

    def fourth_step(p, applied):
        r3 = resid[p]
        r4 = r3 - (applied * (1.0 / THETA)) * invd[p]
        lam[p] = lam[p] + (ALPHA / THETA) * r3 + BETA * r4

    apply_planes(resid, coef, 5, 9, fourth_step)


def cell_products(lam, hu, chunks):
    low = forward(lam[BELOW])
    for p in range(DEPTH):
        high = forward(lam[BELOW + p + 1])
        total = None
        for k, term in enumerate(cell_terms(low, high)):
            piece = term * hu[p, k]
            total = piece if total is None else total + piece
        low = high
        for z in range(8):
            for c in range(2):
                at = 4 * z + 2 * c
                chunks[c, z, 2 * p : 2 * p + 2, :] = total[at : at + 2, :]


def kernel(
    cond_hbm, field_hbm, pairs_hbm, obs_hbm,
    recv_src, recv_mis,
    cext, fext, pairs, obs, index, target,
    part, recv_xy, zsum, recv_z,
    place_row, lane_row, res_row, row_hot, lane_hot, lane_res, coef, diag, invd, cinv, hu,
    resid, direct, work, lam, pe,
    mis, mis_core, mis_sum, chunks, recv_core, merged,
    in_sem, send_sem, halo_sem, xy_sem, z_sem, mis_sem, core_sem, src_sem,
    ready_z, ready_halo, ready_core, ready_src,
):
    src = lax.axis_index("src")
    slab = lax.axis_index("slab")
    zl, core = src // 2, src % 2
    zh, px, py = slab // 16, (slab // 4) % 4, slab % 4
    here = px * 4 + py
    plane_peers = [
        (src, zh * 16 + ((px + i) % 4) * 4 + (py + j) % 4)
        for i in range(4)
        for j in range(4)
        if i + j
    ]
    z_peer = (src, (1 - zh) * 16 + here)
    sibling = (zl * 2 + 1 - core, slab)
    low_half, high_half = zh == 0, zh == 1

    loads = [
        pltpu.make_async_copy(pairs_hbm, pairs, in_sem.at[0]),
        pltpu.make_async_copy(field_hbm, fext.at[pl.ds(0, DEPTH)], in_sem.at[1]),
        pltpu.make_async_copy(cond_hbm, cext.at[pl.ds(6, DEPTH)], in_sem.at[2]),
        pltpu.make_async_copy(obs_hbm, obs, in_sem.at[3]),
    ]
    for load in loads:
        load.start()

    barrier = pltpu.get_barrier_semaphore()

    def signal(sem, peer):
        pl.semaphore_signal(sem, inc=1, device_id=peer, device_id_type=MESH)

    for peer in plane_peers:
        signal(barrier, peer)

    @pl.when(low_half)
    def _():
        signal(barrier, z_peer)

    for at, to in CROSSING:

        @pl.when(slab == at)
        def _():
            signal(barrier, (src, to))

    for z in range(8):
        after = jnp.where(low_half, z > zl, z < zl)

        @pl.when(after)
        def _():
            signal(barrier, (z * 2 + core, slab))

    @pl.when(core == 1)
    def _():
        signal(barrier, sibling)

    loads[0].wait()
    read_pairs(pairs, index, place_row, lane_row, slab)
    loads[1].wait()
    gather(fext, index, part, slab)
    recv_xy[here] = part[...]

    sent = []

    def send(source, dest, arrival, peer, when=None):
        copy = pltpu.make_async_remote_copy(
            src_ref=source, dst_ref=dest, send_sem=send_sem, recv_sem=arrival,
            device_id=peer, device_id_type=MESH,
        )
        sent.append((copy.wait_send, when))
        if when is None:
            copy.start()
        else:
            pl.when(when)(copy.start)

    def arrived(buffer, arrival):
        pltpu.make_async_copy(buffer, buffer, arrival).wait()

    def wait_for(sem, count):
        @pl.when(count > 0)
        def _():
            pl.semaphore_wait(sem, count)

    def number(flag):
        return flag.astype(jnp.int32)

    crossed = sum(number(slab == to) for _, to in CROSSING)
    crossing = sum(number(slab == at) for at, _ in CROSSING)
    before = jnp.where(low_half, zl, 7 - zl)
    pl.semaphore_wait(barrier, 15 + zh + crossed + before + (1 - core))
    for peer in plane_peers:
        send(part, recv_xy.at[here], xy_sem, peer)

    @pl.when(high_half)
    def _():
        signal(ready_z, z_peer)

    for at, to in CROSSING:

        @pl.when(slab == to)
        def _():
            signal(ready_halo, (src, at))

    for z in range(8):
        earlier = jnp.where(low_half, z < zl, z > zl)

        @pl.when(earlier)
        def _():
            signal(ready_src, (z * 2 + core, slab))

    @pl.when(core == 0)
    def _():
        signal(ready_core, sibling)

    loads[2].wait()
    own = cext.at[pl.ds(6, DEPTH)]
    own_low, own_high = cext.at[pl.ds(6, 2)], cext.at[pl.ds(8, 2)]
    at_1, at_2 = slab == 15, jnp.logical_or(slab == 14, slab == 15)
    up_1 = (own, cext.at[pl.ds(2, DEPTH)], halo_sem.at[0], (src, (slab + 1) % 32))
    up_2 = (own_high, cext.at[pl.ds(0, 2)], halo_sem.at[2], (src, (slab + 2) % 32))
    down_1, down_2 = (src, (slab + 31) % 32), (src, (slab + 30) % 32)
    send(own, cext.at[pl.ds(10, DEPTH)], halo_sem.at[1], down_1, slab > 0)
    send(fext.at[pl.ds(0, 1)], fext.at[pl.ds(DEPTH, 1)], halo_sem.at[4], down_1, slab > 0)
    send(own_low, cext.at[pl.ds(14, 2)], halo_sem.at[3], down_2, slab > 1)
    send(*up_1, jnp.logical_and(slab < 31, jnp.logical_not(at_1)))
    send(*up_2, jnp.logical_and(slab < 30, jnp.logical_not(at_2)))
    loads[3].wait()
    read_target(obs, target, src)
    one_hots(place_row, lane_row, row_hot, lane_hot)

    arrived(recv_xy.at[pl.ds(0, 15)], xy_sem)
    zsum[...] = lax.fori_loop(1, 16, lambda k, acc: acc + recv_xy[k], recv_xy[0], unroll=True)
    wait_for(ready_z, 1 - zh)
    send(zsum, recv_z, z_sem, z_peer)
    wait_for(ready_halo, crossing)
    send(*up_1, at_1)
    send(*up_2, at_2)

    @pl.when(slab > 0)
    def _():
        arrived(cext.at[pl.ds(2, DEPTH)], halo_sem.at[0])

    @pl.when(slab > 1)
    def _():
        arrived(cext.at[pl.ds(0, 2)], halo_sem.at[2])

    @pl.when(slab < 31)
    def _():
        arrived(cext.at[pl.ds(10, DEPTH)], halo_sem.at[1])
        arrived(fext.at[pl.ds(DEPTH, 1)], halo_sem.at[4])

    @pl.when(slab < 30)
    def _():
        arrived(cext.at[pl.ds(14, 2)], halo_sem.at[3])

    conductivity_terms(cext, coef, diag, invd, cinv, slab)
    field_terms(fext, hu, slab)
    wait_for(ready_core, core)
    wait_for(ready_src, 7 - before)

    arrived(recv_z, z_sem)
    res = (zsum[...] + recv_z[...]) - target[...]
    for j in range(RROWS):
        res_row[j] = res[j : j + 1, :]
        res_row[RROWS + j] = -res[j : j + 1, :]
    half = jnp.sum(jnp.sum(0.5 * res * res, axis=0, keepdims=True), axis=1, keepdims=True)
    mis[...] = jnp.broadcast_to(half, (1, NX))
    send(mis, mis_core, mis_sem.at[0], sibling)

    spread_residual(res_row, lane_hot, lane_res)
    scatter(row_hot, lane_res, invd, resid)

    arrived(mis_core, mis_sem.at[0])
    mis_sum[...] = mis[...] + mis_core[...]
    recv_mis[zl] = mis_sum[...]
    for k in range(1, 8):
        z = (zl + k) % 8
        send(mis_sum, recv_mis.at[zl], mis_sem.at[1], (z * 2 + core, slab))

    solve(coef, diag, invd, cinv, resid, direct, work, pe, lam)
    cell_products(lam, hu, chunks)

    send(chunks.at[1 - core], recv_core, core_sem, sibling)
    arrived(recv_core, core_sem)
    merged[...] = chunks[core] + recv_core[...]
    for k in range(1, 8):
        z = (zl + k) % 8
        send(merged.at[z], recv_src.at[zl], src_sem, (z * 2 + core, slab))
    recv_src[zl] = merged[zl]
    arrived(recv_mis.at[pl.ds(0, 7)], mis_sem.at[1])
    arrived(recv_src.at[pl.ds(0, 7)], src_sem)
    for wait, when in sent:
        if when is None:
            wait()
        else:
            pl.when(when)(wait)


def finish(recv_src, recv_mis, grad_ref, misfit_ref):
    total, misfit = recv_src[0], recv_mis[0]
    for k in range(1, 8):
        total, misfit = total + recv_src[k], misfit + recv_mis[k]
    grad_ref[...] = total
    misfit_ref[...] = misfit * (1.0 / (GROUPS * RX))


def on_device(conductivity, forward_fields, receiver_pairs, observed):
    field = forward_fields.reshape(DEPTH, NY, NX)
    pairs = jnp.transpose(receiver_pairs[0])
    conductivity, field, pairs, observed = (
        pltpu.with_memory_space_constraint(a, pltpu.HBM) for a in (conductivity, field, pairs, observed)
    )
    plane = (NY, NX)
    any_spec = pl.BlockSpec(memory_space=pltpu.HBM)
    vmem = pl.BlockSpec(memory_space=pltpu.VMEM)
    dma, regular = pltpu.SemaphoreType.DMA, pltpu.SemaphoreType.REGULAR
    received = pl.pallas_call(
        kernel,
        name="adjoint_gradient",
        out_shape=(
            jax.ShapeDtypeStruct((8, 8, NX), F32),
            jax.ShapeDtypeStruct((8, 1, NX), F32),
        ),
        in_specs=[any_spec] * 4,
        out_specs=(vmem, vmem),
        scratch_shapes=[
            pltpu.VMEM((CELLS, *plane), F32),
            pltpu.VMEM((DEPTH + 1, *plane), F32),
            pltpu.VMEM((2, RX), jnp.int32),
            pltpu.VMEM((GROUPS, RX), F32),
            pltpu.VMEM((IDX, NX), jnp.int32),
            pltpu.VMEM((RROWS, NX), F32),
            pltpu.VMEM((RROWS, NX), F32),
            pltpu.VMEM((16, RROWS, NX), F32),
            pltpu.VMEM((RROWS, NX), F32),
            pltpu.VMEM((RROWS, NX), F32),
            pltpu.VMEM((IDX, 1, NX), F32),
            pltpu.VMEM((IDX, 1, NX), F32),
            pltpu.VMEM((IDX, 1, NX), F32),
            pltpu.VMEM((PLANES * NY, IDX * NX), jnp.bfloat16),
            pltpu.VMEM((NX, IDX * NX), jnp.bfloat16),
            pltpu.VMEM((2 * NX, IDX * NX), jnp.bfloat16),
            pltpu.VMEM((3, PLANES, *plane), F32),
            pltpu.VMEM((PLANES, *plane), F32),
            pltpu.VMEM((PLANES, *plane), F32),
            pltpu.VMEM((5, *plane), F32),
            pltpu.VMEM((DEPTH, 7, *plane), F32),
            pltpu.VMEM((PLANES, *plane), F32),
            pltpu.VMEM((PLANES, *plane), F32),
            pltpu.VMEM((PLANES, *plane), F32),
            pltpu.VMEM((PLANES, *plane), F32),
            pltpu.VMEM((PLANES, *plane), F32),
            pltpu.VMEM((1, NX), F32),
            pltpu.VMEM((1, NX), F32),
            pltpu.VMEM((1, NX), F32),
            pltpu.VMEM((2, 8, 8, NX), F32),
            pltpu.VMEM((8, 8, NX), F32),
            pltpu.VMEM((8, 8, NX), F32),
            dma((4,)), dma, dma((5,)), dma, dma, dma((2,)), dma, dma,
            regular, regular, regular, regular,
        ],
        compiler_params=pltpu.CompilerParams(
            collective_id=0, has_side_effects=True, vmem_limit_bytes=32 * 1024 * 1024
        ),
    )(conductivity, field, pairs, observed)
    grad, misfit = pl.pallas_call(
        finish,
        name="add_groups",
        out_shape=(jax.ShapeDtypeStruct((8, NX), F32), jax.ShapeDtypeStruct((1, NX), F32)),
        in_specs=[vmem] * 2,
        out_specs=(vmem, vmem),
    )(*received)
    return grad.reshape(DEPTH, 2, NX), misfit[0, 0]


def solution(mesh):
    in_specs = (P("slab", None, None), P("src", "slab", None, None), P("src", None, None), P())
    out_specs = (P("slab", "src", None), P())
    return jax.shard_map(
        on_device, mesh=mesh, in_specs=in_specs, out_specs=out_specs, check_vma=False
    )
```

```python
import functools

import jax
import jax.numpy as jnp
from jax import lax
from jax.experimental import pallas as pl
from jax.experimental.pallas import tpu as pltpu
from jax.sharding import PartitionSpec as P

LOWER = 0.3
UPPER = 2.0
OMEGA = 0.6
THETA = 0.5 * (UPPER + LOWER)
DELTA = 0.5 * (UPPER - LOWER)
RATIO = THETA / DELTA
RHO_A = 1.0 / RATIO
RHO_B = 1.0 / (2.0 * RATIO - RHO_A)
ALPHA = RHO_B * RHO_A
BETA = 2.0 * RHO_B / DELTA

NY, NX = 32, 128
DEPTH = 4
BELOW = 5
BLOCK = 15
PLANES = 15
CELLS = 16
RX = 2000
RROWS = 16
IDX = 2 * RROWS
GROUPS = 16
UPWARD = ((14, 16, 8, 0, 0), (15, 16, 6, 2, 1), (15, 16, 8, 4, 2), (15, 17, 8, 0, 0))
DOWNWARD = ((16, 15, 6, 10, 0), (16, 15, 8, 12, 1), (17, 15, 6, 14, 2), (16, 14, 6, 14, 0))
CROSSING = ((14, 16), (15, 16), (15, 17))
NZ = 128
MESH = pl.DeviceIdType.MESH
F32 = jnp.float32
ONE, TWO, THREE = 1.0 / 16.0, 1.0 / 24.0, 1.0 / 48.0


def lanes():
    return lax.broadcasted_iota(jnp.int32, (NY, NX), 1)


def rows():
    return lax.broadcasted_iota(jnp.int32, (NY, NX), 0)


def next_x(v):
    return jnp.where(lanes() < NX - 1, pltpu.roll(v, NX - 1, 1), 0.0)


def prev_x(v):
    return jnp.where(lanes() > 0, pltpu.roll(v, 1, 1), 0.0)


def next_y(v):
    return jnp.where(rows() < NY - 1, pltpu.roll(v, NY - 1, 0), 0.0)


def prev_y(v):
    return jnp.where(rows() > 0, pltpu.roll(v, 1, 0), 0.0)


def prev2_x(v):
    return jnp.where(lanes() > 1, pltpu.roll(v, 2, 1), 0.0)


def prev2_y(v):
    return jnp.where(rows() > 1, pltpu.roll(v, 2, 0), 0.0)


def forward(v):
    moved = next_x(v)
    sx, dx = v + moved, v - moved
    ms, md = next_y(sx), next_y(dx)
    return sx + ms, sx - ms, dx + md, dx - md


def cell_terms(low, high):
    ss, ds, sd, dd = low
    ss2, ds2, sd2, dd2 = high
    return (ss - ss2, ds + ds2, ds - ds2, sd + sd2, sd - sd2, dd + dd2, dd - dd2)


def scatter_cell(low, high, c1, c2, c3):
    zss, sds, zds, ssd, zsd, sdd, zdd = cell_terms(low, high)
    zss = zss * c1
    sds, zds = sds * c1, zds * c2
    ssd, zsd = ssd * c1, zsd * c2
    sdd, zdd = sdd * c2, zdd * c3
    lower = (zss, sds + zds, ssd + zsd, sdd + zdd)
    upper = (-zss, sds - zds, ssd - zsd, sdd - zdd)
    return lower, upper


def backward(parts):
    ss, ds, sd, dd = parts
    os = (ss + ds) + prev_y(ss - ds)
    od = (sd + dd) + prev_y(sd - dd)
    return (os + od) + prev_x(os - od)


def apply_planes(v_ref, coef, first, last, sink):
    low = forward(v_ref[first - 1])
    mid = forward(v_ref[first])
    _, upper = scatter_cell(low, mid, coef[0, first - 1], coef[1, first - 1], coef[2, first - 1])

    def body(p, carry):
        here, above = carry[:4], carry[4:]
        ahead = forward(v_ref[p + 1])
        lower, upper = scatter_cell(here, ahead, coef[0, p], coef[1, p], coef[2, p])
        sink(p, backward([a + b for a, b in zip(lower, above)]))
        return (*ahead, *upper)

    lax.fori_loop(first, last + 1, body, (*mid, *upper), unroll=True)


def read_pairs(pairs, index, place_row, lane_row, slab):
    index[...] = jnp.full((IDX, NX), 1 << 24, jnp.int32)
    for j in range(RROWS):
        width = min(NX, RX - j * NX)
        for at, end in ((j, 0), (RROWS + j, 1)):
            index[at : at + 1, 0:width] = pairs[end : end + 1, pl.ds(j * NX, width)]
    lane = jnp.bitwise_and(index[...], NX - 1).astype(F32)
    place = (jnp.right_shift(index[...], 7) - (slab * DEPTH - BELOW) * NY).astype(F32)
    for j in range(IDX):
        place_row[j] = place[j : j + 1, :]
        lane_row[j] = lane[j : j + 1, :]


def read_target(obs, target, src):
    target[...] = jnp.zeros((RROWS, NX), F32)
    for j in range(RROWS):
        width = min(NX, RX - j * NX)
        mine = lax.broadcasted_iota(jnp.int32, (GROUPS, width), 0) == src
        target[j : j + 1, 0:width] = jnp.sum(
            jnp.where(mine, obs[:, pl.ds(j * NX, width)], 0.0), axis=0, keepdims=True
        )


def gather(fext, index, part, slab):
    lane = jnp.bitwise_and(index[...], NX - 1)
    line = jnp.right_shift(index[...], 7) - slab * (DEPTH * NY)

    def pick(block, acc):
        values = fext[block // 4, pl.ds((block % 4) * 8, 8), :]
        for k in range(8):
            spread = jnp.broadcast_to(values[k : k + 1, :], (IDX, NX))
            found = jnp.take_along_axis(spread, lane, axis=1, mode="promise_in_bounds")
            acc = jnp.where(line == block * 8 + k, found, acc)
        return acc

    picked = lax.fori_loop(0, DEPTH * NY // 8, pick, jnp.zeros((IDX, NX), F32), unroll=True)
    part[...] = picked[:RROWS] - picked[RROWS:]


def one_hots(place_row, lane_row, row_hot, lane_hot):
    def hot(j, carry):
        columns = pl.ds(pl.multiple_of(j * NX, NX), NX)
        for at, out, size in ((place_row, row_hot, PLANES * NY), (lane_row, lane_hot, NX)):
            spread = jnp.broadcast_to(at[j], (size, NX))
            line_id = lax.broadcasted_iota(jnp.int32, (size, NX), 0).astype(F32)
            out[:, columns] = jnp.where(spread == line_id, 1.0, 0.0).astype(jnp.bfloat16)
        return carry

    lax.fori_loop(0, IDX, hot, 0)


def inside(plane, slab):
    z = slab * DEPTH + plane
    return jnp.logical_and(z >= 0, z < NZ)


def conductivity_terms(cext, coef, diag, invd, cinv, slab):
    def masked_cells(e):
        return jnp.where(inside(e - 6, slab), cext[e], 0.0)

    def around(cells):
        along = cells + prev_x(cells)
        return along + prev_y(along)

    def diagonals(p, below):
        cells = masked_cells(p + 1)
        coef[0, p] = cells * ONE
        coef[1, p] = cells * TWO
        coef[2, p] = cells * THREE
        boxed = around(cells)
        value = (boxed + below) * (1.0 / 3.0)
        keep = inside(p - BELOW, slab)
        diag[p] = jnp.where(keep, value, 0.0)
        invd[p] = jnp.where(keep, 1.0 / jnp.where(keep, value, 1.0), 0.0)
        return boxed

    lax.fori_loop(0, PLANES, diagonals, around(masked_cells(0)), unroll=5)

    even = jnp.logical_and(lanes() % 2 == 0, rows() % 2 == 0)

    def coarse_box(j):
        pair = masked_cells(2 * j + 2) + masked_cells(2 * j + 3)
        pair = pair + next_y(pair)
        pair = jnp.where(even, pair + next_x(pair), 0.0)
        pair = pair + prev2_x(pair)
        return pair + prev2_y(pair)

    def coarse(j, below):
        boxed = coarse_box(j)
        value = (boxed + below) * (0.125 * 2.0 / 3.0)
        keep = jnp.logical_and(even, inside(2 * (j - 2), slab))
        cinv[j - 1] = jnp.where(keep, OMEGA / jnp.where(keep, value, 1.0), 0.0)
        return boxed

    lax.fori_loop(1, 6, coarse, coarse_box(0), unroll=True)


def field_terms(fext, hu, slab):
    def terms(p, low):
        high = forward(jnp.where(inside(p + 1, slab), fext[p + 1], 0.0))
        scales = (-ONE, -ONE, -TWO, -ONE, -TWO, -TWO, -THREE)
        for k, (term, scale) in enumerate(zip(cell_terms(low, high), scales)):
            hu[p, k] = term * scale
        return high

    lax.fori_loop(0, DEPTH, terms, forward(fext[0]), unroll=True)


def spread_residual(res_row, lane_hot, lane_res):
    def spread(j, carry):
        columns = pl.ds(pl.multiple_of(j * NX, NX), NX)
        value = jnp.broadcast_to(res_row[j], (16, NX))
        high = value.astype(jnp.bfloat16)
        low = (value - high.astype(F32)).astype(jnp.bfloat16)
        hot = lane_hot[:, columns].reshape(NX // 16, 16, NX)
        lane_res[0:NX, columns] = (hot * high[None]).reshape(NX, NX)
        lane_res[NX:, columns] = (hot * low[None]).reshape(NX, NX)
        return carry

    lax.fori_loop(0, IDX, spread, 0, unroll=4)


def scatter(row_hot, lane_res, invd, resid):
    def product(q, carry):
        span = pl.ds(pl.multiple_of(q * (BLOCK * NY), BLOCK * NY), BLOCK * NY)
        both = lax.dot_general(
            row_hot[span, :], lane_res[...], (((1,), (1,)), ((), ())), preferred_element_type=F32
        )
        rhs = (both[:, :NX] + both[:, NX:]).reshape(BLOCK, NY, NX)
        planes = pl.ds(q * BLOCK, BLOCK)
        resid[planes] = rhs * invd[planes]
        return carry

    lax.fori_loop(0, PLANES // BLOCK, product, 0)


def solve(coef, diag, invd, cinv, resid, direct, work, pe, lam):
    def first_step(p, applied):
        r = resid[p]
        r1 = r - (applied * (1.0 / THETA)) * invd[p]
        d2 = (ALPHA / THETA) * r + BETA * r1
        resid[p] = r1
        direct[p] = d2
        lam[p] = r * (1.0 / THETA) + d2

    apply_planes(resid, coef, 1, 13, first_step)

    def second_step(p, applied):
        r2 = resid[p] - applied * invd[p]
        resid[p] = r2
        f = diag[p] * r2
        f = f + 0.5 * (prev_x(f) + next_x(f))
        work[p] = f + 0.5 * (prev_y(f) + next_y(f))

    apply_planes(direct, coef, 2, 12, second_step)

    def correct(j):
        p = 2 * j + 3
        c = (work[p] + 0.5 * (work[p - 1] + work[p + 1])) * cinv[j]
        c = c + 0.5 * (prev_y(c) + next_y(c))
        return c + 0.5 * (prev_x(c) + next_x(c))

    def prolong(j, below):
        c = correct(j)
        pe[2 * j + 3] = c
        pe[2 * j + 2] = 0.5 * (below + c)
        return c

    first = correct(0)
    pe[3] = first
    lax.fori_loop(1, 5, prolong, first, unroll=True)

    def third_step(p, applied):
        r3 = resid[p] - applied * invd[p]
        resid[p] = r3
        lam[p] = lam[p] + pe[p] + r3 * (1.0 / THETA)

    apply_planes(pe, coef, 4, 10, third_step)

    def fourth_step(p, applied):
        r3 = resid[p]
        r4 = r3 - (applied * (1.0 / THETA)) * invd[p]
        lam[p] = lam[p] + (ALPHA / THETA) * r3 + BETA * r4

    apply_planes(resid, coef, 5, 9, fourth_step)


def cell_products(lam, hu, chunks):
    low = forward(lam[BELOW])
    for p in range(DEPTH):
        high = forward(lam[BELOW + p + 1])
        total = None
        for k, term in enumerate(cell_terms(low, high)):
            piece = term * hu[p, k]
            total = piece if total is None else total + piece
        low = high
        for z in range(8):
            for c in range(2):
                at = 4 * z + 2 * c
                chunks[c, z, 2 * p : 2 * p + 2, :] = total[at : at + 2, :]


def kernel(
    cond_hbm, field_hbm, pairs_hbm, obs_hbm,
    recv_src, recv_mis,
    cext, fext, pairs, obs, index, target,
    part, recv_xy, zsum, recv_z,
    place_row, lane_row, res_row, row_hot, lane_hot, lane_res, coef, diag, invd, cinv, hu,
    resid, direct, work, lam, pe,
    mis, mis_core, mis_sum, chunks, recv_core, merged,
    in_sem, send_sem, halo_sem, xy_sem, z_sem, mis_sem, core_sem, src_sem,
    cross_sem, swap_sem, ready_z, ready_halo, ready_core, ready_src, ready_field,
):
    src = lax.axis_index("src")
    slab = lax.axis_index("slab")
    zl, core = src // 2, src % 2
    zh, px, py = slab // 16, (slab // 4) % 4, slab % 4
    here = px * 4 + py
    plane_peers = [
        (src, zh * 16 + ((px + i) % 4) * 4 + (py + j) % 4)
        for i in range(4)
        for j in range(4)
        if i + j
    ]
    z_peer = (src, (1 - zh) * 16 + here)
    sibling = (zl * 2 + 1 - core, slab)
    low_half, high_half = zh == 0, zh == 1
    first = jnp.where(zl < 4, zh, 1 - zh) == 0
    second = jnp.logical_not(first)
    edge = jnp.logical_or(zl == 0, zl == 7)
    beyond = (7 - zl) * 2 + core
    greets_field = jnp.logical_and(first, jnp.logical_or(slab == 15, slab == 16))
    hears_field = jnp.logical_and(second, jnp.logical_or(slab == 15, slab == 16))
    across = (src, 31 - slab)

    loads = [
        pltpu.make_async_copy(pairs_hbm, pairs, in_sem.at[0]),
        pltpu.make_async_copy(field_hbm, fext.at[pl.ds(0, DEPTH)], in_sem.at[1]),
        pltpu.make_async_copy(cond_hbm, cext.at[pl.ds(6, DEPTH)], in_sem.at[2]),
        pltpu.make_async_copy(obs_hbm, obs, in_sem.at[3]),
    ]
    for load in loads:
        load.start()

    barrier = pltpu.get_barrier_semaphore()

    def signal(sem, peer):
        pl.semaphore_signal(sem, inc=1, device_id=peer, device_id_type=MESH)

    for peer in plane_peers:
        signal(barrier, peer)

    @pl.when(first)
    def _():
        signal(barrier, z_peer)

    for at, to in CROSSING:

        @pl.when(jnp.logical_and(edge, slab == at))
        def _():
            signal(barrier, (beyond, to))

    @pl.when(greets_field)
    def _():
        signal(barrier, across)

    for z in range(8):
        after = jnp.where(low_half, z > zl, z < zl)

        @pl.when(after)
        def _():
            signal(barrier, (z * 2 + core, slab))

    @pl.when(core == 1)
    def _():
        signal(barrier, sibling)

    loads[0].wait()
    read_pairs(pairs, index, place_row, lane_row, slab)
    loads[1].wait()
    gather(fext, index, part, slab)
    recv_xy[here] = part[...]

    sent = []

    def send(source, dest, arrival, peer, when=None):
        copy = pltpu.make_async_remote_copy(
            src_ref=source, dst_ref=dest, send_sem=send_sem, recv_sem=arrival,
            device_id=peer, device_id_type=MESH,
        )
        sent.append((copy.wait_send, when))
        if when is None:
            copy.start()
        else:
            pl.when(when)(copy.start)

    def arrived(buffer, arrival):
        pltpu.make_async_copy(buffer, buffer, arrival).wait()

    def wait_for(sem, count):
        @pl.when(count > 0)
        def _():
            pl.semaphore_wait(sem, count)

    def number(flag):
        return flag.astype(jnp.int32)

    crossed = sum(number(slab == to) for _, to in CROSSING) * number(edge)
    crossing = sum(number(slab == at) for at, _ in CROSSING) * number(edge)
    before = jnp.where(low_half, zl, 7 - zl)
    heard = 15 + number(second) + crossed + number(hears_field) + before + (1 - core)
    pl.semaphore_wait(barrier, heard)
    for peer in plane_peers:
        send(part, recv_xy.at[here], xy_sem, peer)

    @pl.when(second)
    def _():
        signal(ready_z, z_peer)

    for at, to in CROSSING:

        @pl.when(jnp.logical_and(edge, slab == to))
        def _():
            signal(ready_halo, (beyond, at))

    @pl.when(jnp.logical_and(hears_field, slab == 15))
    def _():
        signal(ready_field, across)

    for z in range(8):
        earlier = jnp.where(low_half, z < zl, z > zl)

        @pl.when(earlier)
        def _():
            signal(ready_src, (z * 2 + core, slab))

    @pl.when(core == 0)
    def _():
        signal(ready_core, sibling)

    loads[2].wait()
    def cross(blocks):
        for at, to, take, put, k in blocks:
            send(
                cext.at[take + core], cext.at[put + core], cross_sem.at[k], (beyond, to),
                jnp.logical_and(edge, slab == at),
            )

    own = cext.at[pl.ds(6, DEPTH)]
    own_low, own_high = cext.at[pl.ds(6, 2)], cext.at[pl.ds(8, 2)]
    from_1, from_2 = cext.at[pl.ds(2, DEPTH)], cext.at[pl.ds(0, 2)]
    to_1, to_2 = cext.at[pl.ds(10, DEPTH)], cext.at[pl.ds(14, 2)]
    up_1, up_2 = (src, (slab + 1) % 32), (src, (slab + 2) % 32)
    down_1, down_2 = (src, (slab + 31) % 32), (src, (slab + 30) % 32)

    def among(*slabs):
        found = slab == slabs[0]
        for other in slabs[1:]:
            found = jnp.logical_or(found, slab == other)
        return found

    sends_up_1, sends_up_2 = (jnp.logical_not(among(*t)) for t in ((15, 31), (14, 15, 30, 31)))
    sends_down_1, sends_down_2 = (jnp.logical_not(among(*t)) for t in ((0, 16), (0, 1, 16, 17)))
    top = fext.at[pl.ds(DEPTH, 1)]
    bottom = fext.at[pl.ds(0, 1)]
    send(own, to_1, halo_sem.at[1], down_1, sends_down_1)
    send(bottom, top, halo_sem.at[4], down_1, sends_down_1)
    send(bottom, top, halo_sem.at[4], down_1, jnp.logical_and(slab == 16, second))
    send(own_low, to_2, halo_sem.at[3], down_2, sends_down_2)
    send(own, from_1, halo_sem.at[0], up_1, sends_up_1)
    send(own_high, from_2, halo_sem.at[2], up_2, sends_up_2)
    cross(DOWNWARD)
    loads[3].wait()
    read_target(obs, target, src)
    one_hots(place_row, lane_row, row_hot, lane_hot)

    arrived(recv_xy.at[pl.ds(0, 15)], xy_sem)
    zsum[...] = lax.fori_loop(1, 16, lambda k, acc: acc + recv_xy[k], recv_xy[0], unroll=True)
    wait_for(ready_halo, crossing)
    cross(UPWARD)
    wait_for(ready_z, number(first))
    send(zsum, recv_z, z_sem, z_peer)

    held_field = jnp.logical_and(slab == 16, first)
    wait_for(ready_field, number(held_field))
    send(bottom, top, halo_sem.at[4], down_1, held_field)
    wait_for(ready_core, core)
    wait_for(ready_src, 7 - before)

    for _, to, _, put, k in UPWARD + DOWNWARD:
        block = cext.at[put + core]

        @pl.when(slab == to)
        def _():
            arrived(block, cross_sem.at[k])

        send(block, block, swap_sem.at[k], sibling, slab == to)
        for step in range(1, 4):
            z = jnp.where(zl == 0, step, 7 - step)
            send(block, block, cross_sem.at[k], (z * 2 + core, slab), jnp.logical_and(edge, slab == to))
    for _, to, _, put, k in UPWARD + DOWNWARD:

        @pl.when(slab == to)
        def _():
            arrived(cext.at[put + 1 - core], swap_sem.at[k])

    for buffer, arrival, when in (
        (from_1, halo_sem.at[0], jnp.logical_not(among(0, 16))),
        (to_1, halo_sem.at[1], jnp.logical_not(among(15, 31))),
        (from_2, halo_sem.at[2], jnp.logical_not(among(0, 1, 16, 17))),
        (to_2, halo_sem.at[3], jnp.logical_not(among(14, 15, 30, 31))),
        (top, halo_sem.at[4], slab < 31),
    ):

        @pl.when(when)
        def _():
            arrived(buffer, arrival)

    conductivity_terms(cext, coef, diag, invd, cinv, slab)
    field_terms(fext, hu, slab)
    arrived(recv_z, z_sem)
    res = (zsum[...] + recv_z[...]) - target[...]
    for j in range(RROWS):
        res_row[j] = res[j : j + 1, :]
        res_row[RROWS + j] = -res[j : j + 1, :]
    half = jnp.sum(jnp.sum(0.5 * res * res, axis=0, keepdims=True), axis=1, keepdims=True)
    mis[...] = jnp.broadcast_to(half, (1, NX))
    send(mis, mis_core, mis_sem.at[0], sibling)

    spread_residual(res_row, lane_hot, lane_res)
    scatter(row_hot, lane_res, invd, resid)

    arrived(mis_core, mis_sem.at[0])
    mis_sum[...] = mis[...] + mis_core[...]
    recv_mis[zl] = mis_sum[...]
    for k in range(1, 8):
        z = (zl + k) % 8
        send(mis_sum, recv_mis.at[zl], mis_sem.at[1], (z * 2 + core, slab))

    solve(coef, diag, invd, cinv, resid, direct, work, pe, lam)
    cell_products(lam, hu, chunks)

    send(chunks.at[1 - core], recv_core, core_sem, sibling)
    arrived(recv_core, core_sem)
    merged[...] = chunks[core] + recv_core[...]
    for k in range(1, 8):
        z = (zl + k) % 8
        send(merged.at[z], recv_src.at[zl], src_sem, (z * 2 + core, slab))
    recv_src[zl] = merged[zl]
    arrived(recv_mis.at[pl.ds(0, 7)], mis_sem.at[1])
    arrived(recv_src.at[pl.ds(0, 7)], src_sem)
    for wait, when in sent:
        if when is None:
            wait()
        else:
            pl.when(when)(wait)


def finish(recv_src, recv_mis, grad_ref, misfit_ref):
    total, misfit = recv_src[0], recv_mis[0]
    for k in range(1, 8):
        total, misfit = total + recv_src[k], misfit + recv_mis[k]
    grad_ref[...] = total
    misfit_ref[...] = misfit * (1.0 / (GROUPS * RX))


def on_device(conductivity, forward_fields, receiver_pairs, observed):
    field = forward_fields.reshape(DEPTH, NY, NX)
    pairs = jnp.transpose(receiver_pairs[0])
    conductivity, field, pairs, observed = (
        pltpu.with_memory_space_constraint(a, pltpu.HBM) for a in (conductivity, field, pairs, observed)
    )
    plane = (NY, NX)
    any_spec = pl.BlockSpec(memory_space=pltpu.HBM)
    vmem = pl.BlockSpec(memory_space=pltpu.VMEM)
    dma, regular = pltpu.SemaphoreType.DMA, pltpu.SemaphoreType.REGULAR
    received = pl.pallas_call(
        kernel,
        name="adjoint_gradient",
        out_shape=(
            jax.ShapeDtypeStruct((8, 8, NX), F32),
            jax.ShapeDtypeStruct((8, 1, NX), F32),
        ),
        in_specs=[any_spec] * 4,
        out_specs=(vmem, vmem),
        scratch_shapes=[
            pltpu.VMEM((CELLS, *plane), F32),
            pltpu.VMEM((DEPTH + 1, *plane), F32),
            pltpu.VMEM((2, RX), jnp.int32),
            pltpu.VMEM((GROUPS, RX), F32),
            pltpu.VMEM((IDX, NX), jnp.int32),
            pltpu.VMEM((RROWS, NX), F32),
            pltpu.VMEM((RROWS, NX), F32),
            pltpu.VMEM((16, RROWS, NX), F32),
            pltpu.VMEM((RROWS, NX), F32),
            pltpu.VMEM((RROWS, NX), F32),
            pltpu.VMEM((IDX, 1, NX), F32),
            pltpu.VMEM((IDX, 1, NX), F32),
            pltpu.VMEM((IDX, 1, NX), F32),
            pltpu.VMEM((PLANES * NY, IDX * NX), jnp.bfloat16),
            pltpu.VMEM((NX, IDX * NX), jnp.bfloat16),
            pltpu.VMEM((2 * NX, IDX * NX), jnp.bfloat16),
            pltpu.VMEM((3, PLANES, *plane), F32),
            pltpu.VMEM((PLANES, *plane), F32),
            pltpu.VMEM((PLANES, *plane), F32),
            pltpu.VMEM((5, *plane), F32),
            pltpu.VMEM((DEPTH, 7, *plane), F32),
            pltpu.VMEM((PLANES, *plane), F32),
            pltpu.VMEM((PLANES, *plane), F32),
            pltpu.VMEM((PLANES, *plane), F32),
            pltpu.VMEM((PLANES, *plane), F32),
            pltpu.VMEM((PLANES, *plane), F32),
            pltpu.VMEM((1, NX), F32),
            pltpu.VMEM((1, NX), F32),
            pltpu.VMEM((1, NX), F32),
            pltpu.VMEM((2, 8, 8, NX), F32),
            pltpu.VMEM((8, 8, NX), F32),
            pltpu.VMEM((8, 8, NX), F32),
            dma((4,)), dma, dma((5,)), dma, dma, dma((2,)), dma, dma,
            dma((3,)), dma((3,)), regular, regular, regular, regular, regular,
        ],
        compiler_params=pltpu.CompilerParams(
            collective_id=0, has_side_effects=True, vmem_limit_bytes=32 * 1024 * 1024
        ),
    )(conductivity, field, pairs, observed)
    grad, misfit = pl.pallas_call(
        finish,
        name="add_groups",
        out_shape=(jax.ShapeDtypeStruct((8, NX), F32), jax.ShapeDtypeStruct((1, NX), F32)),
        in_specs=[vmem] * 2,
        out_specs=(vmem, vmem),
        compiler_params=pltpu.CompilerParams(vmem_limit_bytes=1024 * 1024),
    )(*received)
    return grad.reshape(DEPTH, 2, NX), misfit[0, 0]


def solution(mesh):
    in_specs = (P("slab", None, None), P("src", "slab", None, None), P("src", None, None), P())
    out_specs = (P("slab", "src", None), P())
    return jax.shard_map(
        on_device, mesh=mesh, in_specs=in_specs, out_specs=out_specs, check_vma=False
    )
```

```python
import functools

import jax
import jax.numpy as jnp
from jax import lax
from jax.experimental import pallas as pl
from jax.experimental.pallas import tpu as pltpu
from jax.sharding import PartitionSpec as P

LOWER = 0.3
UPPER = 2.0
OMEGA = 0.6
THETA = 0.5 * (UPPER + LOWER)
DELTA = 0.5 * (UPPER - LOWER)
RATIO = THETA / DELTA
RHO_A = 1.0 / RATIO
RHO_B = 1.0 / (2.0 * RATIO - RHO_A)
ALPHA = RHO_B * RHO_A
BETA = 2.0 * RHO_B / DELTA

NY, NX = 32, 128
DEPTH = 4
BELOW = 5
BLOCK = 15
PLANES = 15
CELLS = 16
RX = 2000
RROWS = 16
IDX = 2 * RROWS
GROUPS = 16
UPWARD = ((14, 16, 8, 0, 0), (15, 16, 6, 2, 1), (15, 16, 8, 4, 2), (15, 17, 8, 0, 0))
DOWNWARD = ((16, 15, 6, 10, 0), (16, 15, 8, 12, 1), (17, 15, 6, 14, 2), (16, 14, 6, 14, 0))
CROSSING = ((14, 16), (15, 16), (15, 17))
NZ = 128
MESH = pl.DeviceIdType.MESH
F32 = jnp.float32
ONE, TWO, THREE = 1.0 / 16.0, 1.0 / 24.0, 1.0 / 48.0


def lanes():
    return lax.broadcasted_iota(jnp.int32, (NY, NX), 1)


def rows():
    return lax.broadcasted_iota(jnp.int32, (NY, NX), 0)


def next_x(v):
    return jnp.where(lanes() < NX - 1, pltpu.roll(v, NX - 1, 1), 0.0)


def prev_x(v):
    return jnp.where(lanes() > 0, pltpu.roll(v, 1, 1), 0.0)


def next_y(v):
    return jnp.where(rows() < NY - 1, pltpu.roll(v, NY - 1, 0), 0.0)


def prev_y(v):
    return jnp.where(rows() > 0, pltpu.roll(v, 1, 0), 0.0)


def prev2_x(v):
    return jnp.where(lanes() > 1, pltpu.roll(v, 2, 1), 0.0)


def prev2_y(v):
    return jnp.where(rows() > 1, pltpu.roll(v, 2, 0), 0.0)


def forward(v):
    moved = next_x(v)
    sx, dx = v + moved, v - moved
    ms, md = next_y(sx), next_y(dx)
    return sx + ms, sx - ms, dx + md, dx - md


def cell_terms(low, high):
    ss, ds, sd, dd = low
    ss2, ds2, sd2, dd2 = high
    return (ss - ss2, ds + ds2, ds - ds2, sd + sd2, sd - sd2, dd + dd2, dd - dd2)


def scatter_cell(low, high, c1, c2, c3):
    zss, sds, zds, ssd, zsd, sdd, zdd = cell_terms(low, high)
    zss = zss * c1
    sds, zds = sds * c1, zds * c2
    ssd, zsd = ssd * c1, zsd * c2
    sdd, zdd = sdd * c2, zdd * c3
    lower = (zss, sds + zds, ssd + zsd, sdd + zdd)
    upper = (-zss, sds - zds, ssd - zsd, sdd - zdd)
    return lower, upper


def backward(parts):
    ss, ds, sd, dd = parts
    os = (ss + ds) + prev_y(ss - ds)
    od = (sd + dd) + prev_y(sd - dd)
    return (os + od) + prev_x(os - od)


def apply_planes(v_ref, coef, first, last, sink):
    low = forward(v_ref[first - 1])
    mid = forward(v_ref[first])
    _, upper = scatter_cell(low, mid, coef[0, first - 1], coef[1, first - 1], coef[2, first - 1])

    def body(p, carry):
        here, above = carry[:4], carry[4:]
        ahead = forward(v_ref[p + 1])
        lower, upper = scatter_cell(here, ahead, coef[0, p], coef[1, p], coef[2, p])
        sink(p, backward([a + b for a, b in zip(lower, above)]))
        return (*ahead, *upper)

    lax.fori_loop(first, last + 1, body, (*mid, *upper), unroll=True)


def read_pairs(pairs, index, place_row, lane_row, slab):
    index[...] = jnp.full((IDX, NX), 1 << 24, jnp.int32)
    for j in range(RROWS):
        width = min(NX, RX - j * NX)
        for at, end in ((j, 0), (RROWS + j, 1)):
            index[at : at + 1, 0:width] = pairs[end : end + 1, pl.ds(j * NX, width)]
    lane = jnp.bitwise_and(index[...], NX - 1).astype(F32)
    place = (jnp.right_shift(index[...], 7) - (slab * DEPTH - BELOW) * NY).astype(F32)
    for j in range(IDX):
        place_row[j] = place[j : j + 1, :]
        lane_row[j] = lane[j : j + 1, :]


def read_target(obs, target, src):
    target[...] = jnp.zeros((RROWS, NX), F32)
    for j in range(RROWS):
        width = min(NX, RX - j * NX)
        mine = lax.broadcasted_iota(jnp.int32, (GROUPS, width), 0) == src
        target[j : j + 1, 0:width] = jnp.sum(
            jnp.where(mine, obs[:, pl.ds(j * NX, width)], 0.0), axis=0, keepdims=True
        )


def gather(fext, index, part, slab):
    lane = jnp.bitwise_and(index[...], NX - 1)
    line = jnp.right_shift(index[...], 7) - slab * (DEPTH * NY)

    def pick(block, acc):
        values = fext[block // 4, pl.ds((block % 4) * 8, 8), :]
        for k in range(8):
            spread = jnp.broadcast_to(values[k : k + 1, :], (IDX, NX))
            found = jnp.take_along_axis(spread, lane, axis=1, mode="promise_in_bounds")
            acc = jnp.where(line == block * 8 + k, found, acc)
        return acc

    picked = lax.fori_loop(0, DEPTH * NY // 8, pick, jnp.zeros((IDX, NX), F32), unroll=True)
    part[...] = picked[:RROWS] - picked[RROWS:]


def one_hots(place_row, lane_row, row_hot, lane_hot):
    def hot(j, carry):
        columns = pl.ds(pl.multiple_of(j * NX, NX), NX)
        for at, out, size in ((place_row, row_hot, PLANES * NY), (lane_row, lane_hot, NX)):
            spread = jnp.broadcast_to(at[j], (size, NX))
            line_id = lax.broadcasted_iota(jnp.int32, (size, NX), 0).astype(F32)
            out[:, columns] = jnp.where(spread == line_id, 1.0, 0.0).astype(jnp.bfloat16)
        return carry

    lax.fori_loop(0, IDX, hot, 0)


def inside(plane, slab):
    z = slab * DEPTH + plane
    return jnp.logical_and(z >= 0, z < NZ)


def conductivity_terms(cext, coef, diag, invd, cinv, slab):
    def masked_cells(e):
        return jnp.where(inside(e - 6, slab), cext[e], 0.0)

    def around(cells):
        along = cells + prev_x(cells)
        return along + prev_y(along)

    def diagonals(p, below):
        cells = masked_cells(p + 1)
        coef[0, p] = cells * ONE
        coef[1, p] = cells * TWO
        coef[2, p] = cells * THREE
        boxed = around(cells)
        value = (boxed + below) * (1.0 / 3.0)
        keep = inside(p - BELOW, slab)
        diag[p] = jnp.where(keep, value, 0.0)
        invd[p] = jnp.where(keep, 1.0 / jnp.where(keep, value, 1.0), 0.0)
        return boxed

    lax.fori_loop(0, PLANES, diagonals, around(masked_cells(0)), unroll=5)

    even = jnp.logical_and(lanes() % 2 == 0, rows() % 2 == 0)

    def coarse_box(j):
        pair = masked_cells(2 * j + 2) + masked_cells(2 * j + 3)
        pair = pair + next_y(pair)
        pair = jnp.where(even, pair + next_x(pair), 0.0)
        pair = pair + prev2_x(pair)
        return pair + prev2_y(pair)

    def coarse(j, below):
        boxed = coarse_box(j)
        value = (boxed + below) * (0.125 * 2.0 / 3.0)
        keep = jnp.logical_and(even, inside(2 * (j - 2), slab))
        cinv[j - 1] = jnp.where(keep, OMEGA / jnp.where(keep, value, 1.0), 0.0)
        return boxed

    lax.fori_loop(1, 6, coarse, coarse_box(0), unroll=True)


def field_terms(fext, hu, slab, start, stop):
    def terms(p, low):
        high = forward(jnp.where(inside(p + 1, slab), fext[p + 1], 0.0))
        scales = (-ONE, -ONE, -TWO, -ONE, -TWO, -TWO, -THREE)
        for k, (term, scale) in enumerate(zip(cell_terms(low, high), scales)):
            hu[p, k] = term * scale
        return high

    lax.fori_loop(start, stop, terms, forward(fext[start]), unroll=True)


def spread_residual(res_row, lane_hot, lane_res):
    def spread(j, carry):
        columns = pl.ds(pl.multiple_of(j * NX, NX), NX)
        value = jnp.broadcast_to(res_row[j], (16, NX))
        high = value.astype(jnp.bfloat16)
        low = (value - high.astype(F32)).astype(jnp.bfloat16)
        hot = lane_hot[:, columns].reshape(NX // 16, 16, NX)
        lane_res[0:NX, columns] = (hot * high[None]).reshape(NX, NX)
        lane_res[NX:, columns] = (hot * low[None]).reshape(NX, NX)
        return carry

    lax.fori_loop(0, IDX, spread, 0, unroll=4)


def scatter(row_hot, lane_res, invd, resid):
    def product(q, carry):
        span = pl.ds(pl.multiple_of(q * (BLOCK * NY), BLOCK * NY), BLOCK * NY)
        both = lax.dot_general(
            row_hot[span, :], lane_res[...], (((1,), (1,)), ((), ())), preferred_element_type=F32
        )
        rhs = (both[:, :NX] + both[:, NX:]).reshape(BLOCK, NY, NX)
        planes = pl.ds(q * BLOCK, BLOCK)
        resid[planes] = rhs * invd[planes]
        return carry

    lax.fori_loop(0, PLANES // BLOCK, product, 0)


def solve(coef, diag, invd, cinv, resid, direct, work, pe, lam):
    def first_step(p, applied):
        r = resid[p]
        r1 = r - (applied * (1.0 / THETA)) * invd[p]
        d2 = (ALPHA / THETA) * r + BETA * r1
        resid[p] = r1
        direct[p] = d2
        lam[p] = r * (1.0 / THETA) + d2

    apply_planes(resid, coef, 1, 13, first_step)

    def second_step(p, applied):
        r2 = resid[p] - applied * invd[p]
        resid[p] = r2
        f = diag[p] * r2
        f = f + 0.5 * (prev_x(f) + next_x(f))
        work[p] = f + 0.5 * (prev_y(f) + next_y(f))

    apply_planes(direct, coef, 2, 12, second_step)

    def correct(j):
        p = 2 * j + 3
        c = (work[p] + 0.5 * (work[p - 1] + work[p + 1])) * cinv[j]
        c = c + 0.5 * (prev_y(c) + next_y(c))
        return c + 0.5 * (prev_x(c) + next_x(c))

    def prolong(j, below):
        c = correct(j)
        pe[2 * j + 3] = c
        pe[2 * j + 2] = 0.5 * (below + c)
        return c

    first = correct(0)
    pe[3] = first
    lax.fori_loop(1, 5, prolong, first, unroll=True)

    def third_step(p, applied):
        r3 = resid[p] - applied * invd[p]
        resid[p] = r3
        lam[p] = lam[p] + pe[p] + r3 * (1.0 / THETA)

    apply_planes(pe, coef, 4, 10, third_step)

    def fourth_step(p, applied):
        r3 = resid[p]
        r4 = r3 - (applied * (1.0 / THETA)) * invd[p]
        lam[p] = lam[p] + (ALPHA / THETA) * r3 + BETA * r4

    apply_planes(resid, coef, 5, 9, fourth_step)


def cell_products(lam, hu, chunks):
    low = forward(lam[BELOW])
    for p in range(DEPTH):
        high = forward(lam[BELOW + p + 1])
        total = None
        for k, term in enumerate(cell_terms(low, high)):
            piece = term * hu[p, k]
            total = piece if total is None else total + piece
        low = high
        for z in range(8):
            for c in range(2):
                at = 4 * z + 2 * c
                chunks[c, z, 2 * p : 2 * p + 2, :] = total[at : at + 2, :]


def kernel(
    cond_hbm, field_hbm, pairs_hbm, obs_hbm,
    recv_src, recv_mis,
    cext, fext, pairs, obs, index, target,
    part, recv_xy, zsum, recv_z,
    place_row, lane_row, res_row, row_hot, lane_hot, lane_res, coef, diag, invd, cinv, hu,
    resid, direct, work, lam, pe,
    mis, mis_core, mis_sum, chunks, recv_core, merged,
    in_sem, send_sem, halo_sem, xy_sem, z_sem, mis_sem, core_sem, src_sem,
    cross_sem, swap_sem, ready_z, ready_halo, ready_core, ready_src, ready_field,
):
    src = lax.axis_index("src")
    slab = lax.axis_index("slab")
    zl, core = src // 2, src % 2
    zh, px, py = slab // 16, (slab // 4) % 4, slab % 4
    here = px * 4 + py
    hops = (0, 1, 2, 1)
    offsets = sorted(((i, j) for i in range(4) for j in range(4)), key=lambda o: -hops[o[0]] - hops[o[1]])
    plane_peers = [(src, zh * 16 + ((px + i) % 4) * 4 + (py + j) % 4) for i, j in offsets[:-1]]
    z_peer = (src, (1 - zh) * 16 + here)
    sibling = (zl * 2 + 1 - core, slab)
    low_half, high_half = zh == 0, zh == 1
    first = jnp.where(zl < 4, zh, 1 - zh) == 0
    second = jnp.logical_not(first)
    edge = jnp.logical_or(zl == 0, zl == 7)
    beyond = (7 - zl) * 2 + core
    greets_field = jnp.logical_and(first, jnp.logical_or(slab == 15, slab == 16))
    hears_field = jnp.logical_and(second, jnp.logical_or(slab == 15, slab == 16))
    across = (src, 31 - slab)

    loads = [
        pltpu.make_async_copy(pairs_hbm, pairs, in_sem.at[0]),
        pltpu.make_async_copy(field_hbm, fext.at[pl.ds(0, DEPTH)], in_sem.at[1]),
        pltpu.make_async_copy(cond_hbm, cext.at[pl.ds(6, DEPTH)], in_sem.at[2]),
        pltpu.make_async_copy(obs_hbm, obs, in_sem.at[3]),
    ]
    for load in loads:
        load.start()

    barrier = pltpu.get_barrier_semaphore()

    def signal(sem, peer):
        pl.semaphore_signal(sem, inc=1, device_id=peer, device_id_type=MESH)

    for peer in plane_peers:
        signal(barrier, peer)

    @pl.when(first)
    def _():
        signal(barrier, z_peer)

    for at, to in CROSSING:

        @pl.when(jnp.logical_and(edge, slab == at))
        def _():
            signal(barrier, (beyond, to))

    @pl.when(greets_field)
    def _():
        signal(barrier, across)

    for z in range(8):
        after = jnp.where(low_half, z > zl, z < zl)

        @pl.when(after)
        def _():
            signal(barrier, (z * 2 + core, slab))

    @pl.when(core == 1)
    def _():
        signal(barrier, sibling)

    loads[0].wait()
    read_pairs(pairs, index, place_row, lane_row, slab)
    loads[1].wait()
    gather(fext, index, part, slab)
    recv_xy[here] = part[...]

    sent = []

    def send(source, dest, arrival, peer, when=None):
        copy = pltpu.make_async_remote_copy(
            src_ref=source, dst_ref=dest, send_sem=send_sem, recv_sem=arrival,
            device_id=peer, device_id_type=MESH,
        )
        sent.append((copy.wait_send, when))
        if when is None:
            copy.start()
        else:
            pl.when(when)(copy.start)

    def arrived(buffer, arrival):
        pltpu.make_async_copy(buffer, buffer, arrival).wait()

    def wait_for(sem, count):
        @pl.when(count > 0)
        def _():
            pl.semaphore_wait(sem, count)

    def number(flag):
        return flag.astype(jnp.int32)

    crossed = sum(number(slab == to) for _, to in CROSSING) * number(edge)
    crossing = sum(number(slab == at) for at, _ in CROSSING) * number(edge)
    before = jnp.where(low_half, zl, 7 - zl)
    heard = 15 + number(second) + crossed + number(hears_field) + before + (1 - core)
    pl.semaphore_wait(barrier, heard)
    for peer in plane_peers:
        send(part, recv_xy.at[here], xy_sem, peer)

    @pl.when(second)
    def _():
        signal(ready_z, z_peer)

    for at, to in CROSSING:

        @pl.when(jnp.logical_and(edge, slab == to))
        def _():
            signal(ready_halo, (beyond, at))

    @pl.when(jnp.logical_and(hears_field, slab == 15))
    def _():
        signal(ready_field, across)

    for z in range(8):
        earlier = jnp.where(low_half, z < zl, z > zl)

        @pl.when(earlier)
        def _():
            signal(ready_src, (z * 2 + core, slab))

    @pl.when(core == 0)
    def _():
        signal(ready_core, sibling)

    loads[2].wait()
    def cross(blocks):
        for at, to, take, put, k in blocks:
            send(
                cext.at[take + core], cext.at[put + core], cross_sem.at[k], (beyond, to),
                jnp.logical_and(edge, slab == at),
            )

    own = cext.at[pl.ds(6, DEPTH)]
    own_low, own_high = cext.at[pl.ds(6, 2)], cext.at[pl.ds(8, 2)]
    from_1, from_2 = cext.at[pl.ds(2, DEPTH)], cext.at[pl.ds(0, 2)]
    to_1, to_2 = cext.at[pl.ds(10, DEPTH)], cext.at[pl.ds(14, 2)]
    up_1, up_2 = (src, (slab + 1) % 32), (src, (slab + 2) % 32)
    down_1, down_2 = (src, (slab + 31) % 32), (src, (slab + 30) % 32)

    def among(*slabs):
        found = slab == slabs[0]
        for other in slabs[1:]:
            found = jnp.logical_or(found, slab == other)
        return found

    sends_up_1, sends_up_2 = (jnp.logical_not(among(*t)) for t in ((15, 31), (14, 15, 30, 31)))
    sends_down_1, sends_down_2 = (jnp.logical_not(among(*t)) for t in ((0, 16), (0, 1, 16, 17)))
    top = fext.at[pl.ds(DEPTH, 1)]
    bottom = fext.at[pl.ds(0, 1)]
    send(own, to_1, halo_sem.at[1], down_1, sends_down_1)
    send(bottom, top, halo_sem.at[4], down_1, sends_down_1)
    send(bottom, top, halo_sem.at[4], down_1, jnp.logical_and(slab == 16, second))
    send(own_low, to_2, halo_sem.at[3], down_2, sends_down_2)
    send(own, from_1, halo_sem.at[0], up_1, sends_up_1)
    send(own_high, from_2, halo_sem.at[2], up_2, sends_up_2)
    cross(DOWNWARD)
    loads[3].wait()
    read_target(obs, target, src)
    one_hots(place_row, lane_row, row_hot, lane_hot)

    arrived(recv_xy.at[pl.ds(0, 15)], xy_sem)
    zsum[...] = lax.fori_loop(1, 16, lambda k, acc: acc + recv_xy[k], recv_xy[0], unroll=True)
    wait_for(ready_halo, crossing)
    cross(UPWARD)
    wait_for(ready_z, number(first))
    send(zsum, recv_z, z_sem, z_peer)

    held_field = jnp.logical_and(slab == 16, first)
    wait_for(ready_field, number(held_field))
    send(bottom, top, halo_sem.at[4], down_1, held_field)
    wait_for(ready_core, core)
    wait_for(ready_src, 7 - before)

    for _, to, _, put, k in UPWARD + DOWNWARD:
        block = cext.at[put + core]

        @pl.when(slab == to)
        def _():
            arrived(block, cross_sem.at[k])

        send(block, block, swap_sem.at[k], sibling, slab == to)
        for step in range(1, 4):
            z = jnp.where(zl == 0, step, 7 - step)
            send(block, block, cross_sem.at[k], (z * 2 + core, slab), jnp.logical_and(edge, slab == to))
    for _, to, _, put, k in UPWARD + DOWNWARD:

        @pl.when(slab == to)
        def _():
            arrived(cext.at[put + 1 - core], swap_sem.at[k])

    for buffer, arrival, when in (
        (from_1, halo_sem.at[0], jnp.logical_not(among(0, 16))),
        (to_1, halo_sem.at[1], jnp.logical_not(among(15, 31))),
        (from_2, halo_sem.at[2], jnp.logical_not(among(0, 1, 16, 17))),
        (to_2, halo_sem.at[3], jnp.logical_not(among(14, 15, 30, 31))),
    ):

        @pl.when(when)
        def _():
            arrived(buffer, arrival)

    conductivity_terms(cext, coef, diag, invd, cinv, slab)
    field_terms(fext, hu, slab, 0, DEPTH - 1)
    arrived(recv_z, z_sem)
    res = (zsum[...] + recv_z[...]) - target[...]
    for j in range(RROWS):
        res_row[j] = res[j : j + 1, :]
        res_row[RROWS + j] = -res[j : j + 1, :]
    half = jnp.sum(jnp.sum(0.5 * res * res, axis=0, keepdims=True), axis=1, keepdims=True)
    mis[...] = jnp.broadcast_to(half, (1, NX))
    send(mis, mis_core, mis_sem.at[0], sibling)

    spread_residual(res_row, lane_hot, lane_res)
    scatter(row_hot, lane_res, invd, resid)

    arrived(mis_core, mis_sem.at[0])
    mis_sum[...] = mis[...] + mis_core[...]
    recv_mis[zl] = mis_sum[...]
    for k in range(1, 8):
        z = (zl + k) % 8
        send(mis_sum, recv_mis.at[zl], mis_sem.at[1], (z * 2 + core, slab))

    solve(coef, diag, invd, cinv, resid, direct, work, pe, lam)

    @pl.when(slab < 31)
    def _():
        arrived(top, halo_sem.at[4])

    field_terms(fext, hu, slab, DEPTH - 1, DEPTH)
    cell_products(lam, hu, chunks)

    send(chunks.at[1 - core], recv_core, core_sem, sibling)
    arrived(recv_core, core_sem)
    merged[...] = chunks[core] + recv_core[...]
    for z in range(8):
        send(merged.at[z], recv_src.at[zl], src_sem, (z * 2 + core, slab), zl != z)
    recv_src[zl] = merged[zl]
    arrived(recv_mis.at[pl.ds(0, 7)], mis_sem.at[1])
    arrived(recv_src.at[pl.ds(0, 7)], src_sem)
    for wait, when in sent:
        if when is None:
            wait()
        else:
            pl.when(when)(wait)


def finish(recv_src, recv_mis, grad_ref, misfit_ref):
    total, misfit = recv_src[0], recv_mis[0]
    for k in range(1, 8):
        total, misfit = total + recv_src[k], misfit + recv_mis[k]
    grad_ref[...] = total
    misfit_ref[...] = misfit * (1.0 / (GROUPS * RX))


def on_device(conductivity, forward_fields, receiver_pairs, observed):
    field = forward_fields.reshape(DEPTH, NY, NX)
    pairs = jnp.transpose(receiver_pairs[0])
    conductivity, field, pairs, observed = (
        pltpu.with_memory_space_constraint(a, pltpu.HBM) for a in (conductivity, field, pairs, observed)
    )
    plane = (NY, NX)
    any_spec = pl.BlockSpec(memory_space=pltpu.HBM)
    vmem = pl.BlockSpec(memory_space=pltpu.VMEM)
    dma, regular = pltpu.SemaphoreType.DMA, pltpu.SemaphoreType.REGULAR
    received = pl.pallas_call(
        kernel,
        name="adjoint_gradient",
        out_shape=(
            jax.ShapeDtypeStruct((8, 8, NX), F32),
            jax.ShapeDtypeStruct((8, 1, NX), F32),
        ),
        in_specs=[any_spec] * 4,
        out_specs=(vmem, vmem),
        scratch_shapes=[
            pltpu.VMEM((CELLS, *plane), F32),
            pltpu.VMEM((DEPTH + 1, *plane), F32),
            pltpu.VMEM((2, RX), jnp.int32),
            pltpu.VMEM((GROUPS, RX), F32),
            pltpu.VMEM((IDX, NX), jnp.int32),
            pltpu.VMEM((RROWS, NX), F32),
            pltpu.VMEM((RROWS, NX), F32),
            pltpu.VMEM((16, RROWS, NX), F32),
            pltpu.VMEM((RROWS, NX), F32),
            pltpu.VMEM((RROWS, NX), F32),
            pltpu.VMEM((IDX, 1, NX), F32),
            pltpu.VMEM((IDX, 1, NX), F32),
            pltpu.VMEM((IDX, 1, NX), F32),
            pltpu.VMEM((PLANES * NY, IDX * NX), jnp.bfloat16),
            pltpu.VMEM((NX, IDX * NX), jnp.bfloat16),
            pltpu.VMEM((2 * NX, IDX * NX), jnp.bfloat16),
            pltpu.VMEM((3, PLANES, *plane), F32),
            pltpu.VMEM((PLANES, *plane), F32),
            pltpu.VMEM((PLANES, *plane), F32),
            pltpu.VMEM((5, *plane), F32),
            pltpu.VMEM((DEPTH, 7, *plane), F32),
            pltpu.VMEM((PLANES, *plane), F32),
            pltpu.VMEM((PLANES, *plane), F32),
            pltpu.VMEM((PLANES, *plane), F32),
            pltpu.VMEM((PLANES, *plane), F32),
            pltpu.VMEM((PLANES, *plane), F32),
            pltpu.VMEM((1, NX), F32),
            pltpu.VMEM((1, NX), F32),
            pltpu.VMEM((1, NX), F32),
            pltpu.VMEM((2, 8, 8, NX), F32),
            pltpu.VMEM((8, 8, NX), F32),
            pltpu.VMEM((8, 8, NX), F32),
            dma((4,)), dma, dma((5,)), dma, dma, dma((2,)), dma, dma,
            dma((3,)), dma((3,)), regular, regular, regular, regular, regular,
        ],
        compiler_params=pltpu.CompilerParams(
            collective_id=0, has_side_effects=True, vmem_limit_bytes=32 * 1024 * 1024
        ),
    )(conductivity, field, pairs, observed)
    grad, misfit = pl.pallas_call(
        finish,
        name="add_groups",
        out_shape=(jax.ShapeDtypeStruct((8, NX), F32), jax.ShapeDtypeStruct((1, NX), F32)),
        in_specs=[vmem] * 2,
        out_specs=(vmem, vmem),
        compiler_params=pltpu.CompilerParams(vmem_limit_bytes=1024 * 1024),
    )(*received)
    return grad.reshape(DEPTH, 2, NX), misfit[0, 0]


def solution(mesh):
    in_specs = (P("slab", None, None), P("src", "slab", None, None), P("src", None, None), P())
    out_specs = (P("slab", "src", None), P())
    return jax.shard_map(
        on_device, mesh=mesh, in_specs=in_specs, out_specs=out_specs, check_vma=False
    )
```

```python
import functools

import jax
import jax.numpy as jnp
from jax import lax
from jax.experimental import pallas as pl
from jax.experimental.pallas import tpu as pltpu
from jax.sharding import PartitionSpec as P

LOWER = 0.3
UPPER = 2.0
OMEGA = 0.6
THETA = 0.5 * (UPPER + LOWER)
DELTA = 0.5 * (UPPER - LOWER)
RATIO = THETA / DELTA
RHO_A = 1.0 / RATIO
RHO_B = 1.0 / (2.0 * RATIO - RHO_A)
ALPHA = RHO_B * RHO_A
BETA = 2.0 * RHO_B / DELTA

NY, NX = 32, 128
DEPTH = 4
BELOW = 5
PLANES = 15
CELLS = 16
RX = 2000
RROWS = 16
IDX = 2 * RROWS
GROUPS = 16
UPWARD = ((14, 16, 8, 0, 0), (15, 16, 6, 2, 1), (15, 16, 8, 4, 2), (15, 17, 8, 0, 0))
DOWNWARD = ((16, 15, 6, 10, 0), (16, 15, 8, 12, 1), (17, 15, 6, 14, 2), (16, 14, 6, 14, 0))
CROSSING = ((14, 16), (15, 16), (15, 17))
NZ = 128
MESH = pl.DeviceIdType.MESH
F32 = jnp.float32
ONE, TWO, THREE = 1.0 / 16.0, 1.0 / 24.0, 1.0 / 48.0


def lanes():
    return lax.broadcasted_iota(jnp.int32, (NY, NX), 1)


def rows():
    return lax.broadcasted_iota(jnp.int32, (NY, NX), 0)


def next_x(v):
    return jnp.where(lanes() < NX - 1, pltpu.roll(v, NX - 1, 1), 0.0)


def prev_x(v):
    return jnp.where(lanes() > 0, pltpu.roll(v, 1, 1), 0.0)


def next_y(v):
    return jnp.where(rows() < NY - 1, pltpu.roll(v, NY - 1, 0), 0.0)


def prev_y(v):
    return jnp.where(rows() > 0, pltpu.roll(v, 1, 0), 0.0)


def prev2_x(v):
    return jnp.where(lanes() > 1, pltpu.roll(v, 2, 1), 0.0)


def prev2_y(v):
    return jnp.where(rows() > 1, pltpu.roll(v, 2, 0), 0.0)


def forward(v):
    moved = next_x(v)
    sx, dx = v + moved, v - moved
    ms, md = next_y(sx), next_y(dx)
    return sx + ms, sx - ms, dx + md, dx - md


def cell_terms(low, high):
    ss, ds, sd, dd = low
    ss2, ds2, sd2, dd2 = high
    return (ss - ss2, ds + ds2, ds - ds2, sd + sd2, sd - sd2, dd + dd2, dd - dd2)


def scatter_cell(low, high, c1, c2, c3):
    zss, sds, zds, ssd, zsd, sdd, zdd = cell_terms(low, high)
    zss = zss * c1
    sds, zds = sds * c1, zds * c2
    ssd, zsd = ssd * c1, zsd * c2
    sdd, zdd = sdd * c2, zdd * c3
    lower = (zss, sds + zds, ssd + zsd, sdd + zdd)
    upper = (-zss, sds - zds, ssd - zsd, sdd - zdd)
    return lower, upper


def backward(parts):
    ss, ds, sd, dd = parts
    os = (ss + ds) + prev_y(ss - ds)
    od = (sd + dd) + prev_y(sd - dd)
    return (os + od) + prev_x(os - od)


def apply_planes(v_ref, coef, first, last, sink):
    low = forward(v_ref[first - 1])
    mid = forward(v_ref[first])
    _, upper = scatter_cell(low, mid, coef[0, first - 1], coef[1, first - 1], coef[2, first - 1])

    def body(p, carry):
        here, above = carry[:4], carry[4:]
        ahead = forward(v_ref[p + 1])
        lower, upper = scatter_cell(here, ahead, coef[0, p], coef[1, p], coef[2, p])
        sink(p, backward([a + b for a, b in zip(lower, above)]))
        return (*ahead, *upper)

    lax.fori_loop(first, last + 1, body, (*mid, *upper), unroll=True)


def read_pairs(pairs, index, place_row, lane_row, slab):
    index[...] = jnp.full((IDX, NX), 1 << 24, jnp.int32)
    for j in range(RROWS):
        width = min(NX, RX - j * NX)
        for at, end in ((j, 0), (RROWS + j, 1)):
            index[at : at + 1, 0:width] = pairs[end : end + 1, pl.ds(j * NX, width)]
    lane = jnp.bitwise_and(index[...], NX - 1).astype(F32)
    place = (jnp.right_shift(index[...], 7) - (slab * DEPTH - BELOW) * NY).astype(F32)
    for j in range(IDX):
        place_row[j] = place[j : j + 1, :]
        lane_row[j] = lane[j : j + 1, :]


def read_target(obs, target, src):
    target[...] = jnp.zeros((RROWS, NX), F32)
    for j in range(RROWS):
        width = min(NX, RX - j * NX)
        mine = lax.broadcasted_iota(jnp.int32, (GROUPS, width), 0) == src
        target[j : j + 1, 0:width] = jnp.sum(
            jnp.where(mine, obs[:, pl.ds(j * NX, width)], 0.0), axis=0, keepdims=True
        )


def gather(fext, index, part, slab):
    lane = jnp.bitwise_and(index[...], NX - 1)
    line = jnp.right_shift(index[...], 7) - slab * (DEPTH * NY)

    def pick(block, acc):
        values = fext[block // 4, pl.ds((block % 4) * 8, 8), :]
        for k in range(8):
            spread = jnp.broadcast_to(values[k : k + 1, :], (IDX, NX))
            found = jnp.take_along_axis(spread, lane, axis=1, mode="promise_in_bounds")
            acc = jnp.where(line == block * 8 + k, found, acc)
        return acc

    picked = lax.fori_loop(0, DEPTH * NY // 8, pick, jnp.zeros((IDX, NX), F32), unroll=True)
    part[...] = picked[:RROWS] - picked[RROWS:]


def one_hots(place_row, lane_row, row_hot, lane_hot):
    def hot(j, carry):
        columns = pl.ds(pl.multiple_of(j * NX, NX), NX)
        for at, out, size in ((place_row, row_hot, PLANES * NY), (lane_row, lane_hot, NX)):
            spread = jnp.broadcast_to(at[j], (size, NX))
            line_id = lax.broadcasted_iota(jnp.int32, (size, NX), 0).astype(F32)
            out[:, columns] = jnp.where(spread == line_id, 1.0, 0.0).astype(jnp.bfloat16)
        return carry

    lax.fori_loop(0, IDX, hot, 0)


def inside(plane, slab):
    z = slab * DEPTH + plane
    return jnp.logical_and(z >= 0, z < NZ)


def conductivity_terms(cext, coef, diag, invd, cinv, slab):
    def masked_cells(e):
        return jnp.where(inside(e - 6, slab), cext[e], 0.0)

    def around(cells):
        along = cells + prev_x(cells)
        return along + prev_y(along)

    def diagonals(p, below):
        cells = masked_cells(p + 1)
        coef[0, p] = cells * ONE
        coef[1, p] = cells * TWO
        coef[2, p] = cells * THREE
        boxed = around(cells)
        value = (boxed + below) * (1.0 / 3.0)
        keep = inside(p - BELOW, slab)
        diag[p] = jnp.where(keep, value, 0.0)
        invd[p] = jnp.where(keep, 1.0 / jnp.where(keep, value, 1.0), 0.0)
        return boxed

    lax.fori_loop(0, PLANES, diagonals, around(masked_cells(0)), unroll=5)

    even = jnp.logical_and(lanes() % 2 == 0, rows() % 2 == 0)

    def coarse_box(j):
        pair = masked_cells(2 * j + 2) + masked_cells(2 * j + 3)
        pair = pair + next_y(pair)
        pair = jnp.where(even, pair + next_x(pair), 0.0)
        pair = pair + prev2_x(pair)
        return pair + prev2_y(pair)

    def coarse(j, below):
        boxed = coarse_box(j)
        value = (boxed + below) * (0.125 * 2.0 / 3.0)
        keep = jnp.logical_and(even, inside(2 * (j - 2), slab))
        cinv[j - 1] = jnp.where(keep, OMEGA / jnp.where(keep, value, 1.0), 0.0)
        return boxed

    lax.fori_loop(1, 6, coarse, coarse_box(0), unroll=True)


def field_terms(fext, hu, slab, start, stop):
    def terms(p, low):
        high = forward(jnp.where(inside(p + 1, slab), fext[p + 1], 0.0))
        scales = (-ONE, -ONE, -TWO, -ONE, -TWO, -TWO, -THREE)
        for k, (term, scale) in enumerate(zip(cell_terms(low, high), scales)):
            hu[p, k] = term * scale
        return high

    lax.fori_loop(start, stop, terms, forward(fext[start]), unroll=True)


def scatter(res_row, row_hot, lane_hot, invd, resid):
    high_parts, low_parts = [], []
    for j in range(IDX):
        value = jnp.broadcast_to(res_row[j], (16, NX))
        high = value.astype(jnp.bfloat16)
        low = (value - high.astype(F32)).astype(jnp.bfloat16)
        hot = lane_hot[:, j * NX : (j + 1) * NX].reshape(NX // 16, 16, NX)
        high_parts.append((hot * high[None]).reshape(NX, NX))
        low_parts.append((hot * low[None]).reshape(NX, NX))
    by_lane = jnp.concatenate(
        [jnp.concatenate(high_parts, axis=1), jnp.concatenate(low_parts, axis=1)], axis=0
    )
    both = lax.dot_general(
        row_hot[...], by_lane, (((1,), (1,)), ((), ())), preferred_element_type=F32
    )
    resid[...] = (both[:, :NX] + both[:, NX:]).reshape(PLANES, NY, NX) * invd[...]


def solve(coef, diag, invd, cinv, resid, direct, work, pe, lam):
    def first_step(p, applied):
        r = resid[p]
        r1 = r - (applied * (1.0 / THETA)) * invd[p]
        d2 = (ALPHA / THETA) * r + BETA * r1
        resid[p] = r1
        direct[p] = d2
        lam[p] = r * (1.0 / THETA) + d2

    apply_planes(resid, coef, 1, 13, first_step)

    def second_step(p, applied):
        r2 = resid[p] - applied * invd[p]
        resid[p] = r2
        f = diag[p] * r2
        f = f + 0.5 * (prev_x(f) + next_x(f))
        work[p] = f + 0.5 * (prev_y(f) + next_y(f))

    apply_planes(direct, coef, 2, 12, second_step)

    def correct(j):
        p = 2 * j + 3
        c = (work[p] + 0.5 * (work[p - 1] + work[p + 1])) * cinv[j]
        c = c + 0.5 * (prev_y(c) + next_y(c))
        return c + 0.5 * (prev_x(c) + next_x(c))

    def prolong(j, below):
        c = correct(j)
        pe[2 * j + 3] = c
        pe[2 * j + 2] = 0.5 * (below + c)
        return c

    first = correct(0)
    pe[3] = first
    lax.fori_loop(1, 5, prolong, first, unroll=True)

    def third_step(p, applied):
        r3 = resid[p] - applied * invd[p]
        resid[p] = r3
        lam[p] = lam[p] + pe[p] + r3 * (1.0 / THETA)

    apply_planes(pe, coef, 4, 10, third_step)

    def fourth_step(p, applied):
        r3 = resid[p]
        r4 = r3 - (applied * (1.0 / THETA)) * invd[p]
        lam[p] = lam[p] + (ALPHA / THETA) * r3 + BETA * r4

    apply_planes(resid, coef, 5, 9, fourth_step)


def cell_products(lam, hu, chunks):
    low = forward(lam[BELOW])
    for p in range(DEPTH):
        high = forward(lam[BELOW + p + 1])
        total = None
        for k, term in enumerate(cell_terms(low, high)):
            piece = term * hu[p, k]
            total = piece if total is None else total + piece
        low = high
        for z in range(8):
            for c in range(2):
                at = 4 * z + 2 * c
                chunks[c, z, 2 * p : 2 * p + 2, :] = total[at : at + 2, :]


def kernel(
    cond_hbm, field_hbm, pairs_hbm, obs_hbm,
    recv_src, recv_mis,
    cext, fext, pairs, obs, index, target,
    part, recv_xy, zsum, recv_z,
    place_row, lane_row, res_row, row_hot, lane_hot, coef, diag, invd, cinv, hu,
    resid, direct, work, lam, pe,
    mis, mis_core, mis_sum, chunks, recv_core, merged,
    in_sem, send_sem, halo_sem, xy_sem, z_sem, mis_sem, core_sem, src_sem,
    cross_sem, swap_sem, go, ready,
):
    src = lax.axis_index("src")
    slab = lax.axis_index("slab")
    zl, core = src // 2, src % 2
    zh, px, py = slab // 16, (slab // 4) % 4, slab % 4
    here = px * 4 + py
    hops = (0, 1, 2, 1)
    offsets = sorted(((i, j) for i in range(4) for j in range(4)), key=lambda o: -hops[o[0]] - hops[o[1]])
    plane_peers = [(src, zh * 16 + ((px + i) % 4) * 4 + (py + j) % 4) for i, j in offsets[:-1]]
    z_peer = (src, (1 - zh) * 16 + here)
    sibling = (zl * 2 + 1 - core, slab)
    edge = jnp.logical_or(zl == 0, zl == 7)
    beyond = (7 - zl) * 2 + core

    loads = [
        pltpu.make_async_copy(pairs_hbm, pairs, in_sem.at[0]),
        pltpu.make_async_copy(field_hbm, fext.at[pl.ds(0, DEPTH)], in_sem.at[1]),
        pltpu.make_async_copy(cond_hbm, cext.at[pl.ds(6, DEPTH)], in_sem.at[2]),
        pltpu.make_async_copy(obs_hbm, obs, in_sem.at[3]),
    ]
    for load in loads:
        load.start()

    barrier = pltpu.get_barrier_semaphore()

    def signal(sem, peer):
        pl.semaphore_signal(sem, inc=1, device_id=peer, device_id_type=MESH)

    for _, peer in plane_peers:
        signal(barrier, (zl * 2, peer))

    @pl.when(core == 1)
    def _():
        signal(barrier, sibling)

    signal(barrier, (zl * 2 + 1, (1 - zh) * 16 + here))
    for k in range(1, 8):
        signal(barrier, (((zl + k) % 8) * 2 + 1, slab))
    for low, high in CROSSING:
        for at, to in ((low, high), (high, low)):

            @pl.when(jnp.logical_and(edge, slab == at))
            def _():
                signal(barrier, ((7 - zl) * 2 + 1, to))

    @pl.when(slab == 15)
    def _():
        signal(barrier, (zl * 2 + 1, 16))

    loads[0].wait()
    read_pairs(pairs, index, place_row, lane_row, slab)
    loads[1].wait()
    gather(fext, index, part, slab)
    recv_xy[here] = part[...]

    sent = []

    def send(source, dest, arrival, peer, when=None):
        copy = pltpu.make_async_remote_copy(
            src_ref=source, dst_ref=dest, send_sem=send_sem, recv_sem=arrival,
            device_id=peer, device_id_type=MESH,
        )
        sent.append((copy.wait_send, when))
        if when is None:
            copy.start()
        else:
            pl.when(when)(copy.start)

    def arrived(buffer, arrival):
        pltpu.make_async_copy(buffer, buffer, arrival).wait()

    @pl.when(core == 0)
    def _():
        pl.semaphore_wait(barrier, 2 * 15 + 1)
        signal(go, sibling)

    @pl.when(core == 1)
    def _():
        pl.semaphore_wait(go, 1)

    for peer in plane_peers:
        send(part, recv_xy.at[here], xy_sem, peer)

    loads[2].wait()

    def cross(blocks):
        for at, to, take, put, k in blocks:
            send(
                cext.at[take + core], cext.at[put + core], cross_sem.at[k], (beyond, to),
                jnp.logical_and(edge, slab == at),
            )

    own = cext.at[pl.ds(6, DEPTH)]
    own_low, own_high = cext.at[pl.ds(6, 2)], cext.at[pl.ds(8, 2)]
    from_1, from_2 = cext.at[pl.ds(2, DEPTH)], cext.at[pl.ds(0, 2)]
    to_1, to_2 = cext.at[pl.ds(10, DEPTH)], cext.at[pl.ds(14, 2)]
    up_1, up_2 = (src, (slab + 1) % 32), (src, (slab + 2) % 32)
    down_1, down_2 = (src, (slab + 31) % 32), (src, (slab + 30) % 32)

    def among(*slabs):
        found = slab == slabs[0]
        for other in slabs[1:]:
            found = jnp.logical_or(found, slab == other)
        return found

    sends_up_1, sends_up_2 = (jnp.logical_not(among(*t)) for t in ((15, 31), (14, 15, 30, 31)))
    sends_down_1, sends_down_2 = (jnp.logical_not(among(*t)) for t in ((0, 16), (0, 1, 16, 17)))
    top = fext.at[pl.ds(DEPTH, 1)]
    bottom = fext.at[pl.ds(0, 1)]
    send(own, to_1, halo_sem.at[1], down_1, sends_down_1)
    send(bottom, top, halo_sem.at[4], down_1, sends_down_1)
    send(own_low, to_2, halo_sem.at[3], down_2, sends_down_2)
    send(own, from_1, halo_sem.at[0], up_1, sends_up_1)
    send(own_high, from_2, halo_sem.at[2], up_2, sends_up_2)

    crossed = sum((slab == t).astype(jnp.int32) for pair in CROSSING for t in pair)
    far = 1 + 7 + crossed * edge.astype(jnp.int32) + (slab == 16).astype(jnp.int32)

    @pl.when(core == 1)
    def _():
        pl.semaphore_wait(barrier, 2 * far)
        signal(ready, sibling)

    @pl.when(core == 0)
    def _():
        pl.semaphore_wait(ready, 1)

    cross(DOWNWARD + UPWARD)
    send(bottom, top, halo_sem.at[4], down_1, slab == 16)
    loads[3].wait()
    read_target(obs, target, src)
    one_hots(place_row, lane_row, row_hot, lane_hot)

    arrived(recv_xy.at[pl.ds(0, 15)], xy_sem)
    zsum[...] = lax.fori_loop(1, 16, lambda k, acc: acc + recv_xy[k], recv_xy[0], unroll=True)
    send(zsum, recv_z, z_sem, z_peer)

    for _, to, _, put, k in UPWARD + DOWNWARD:
        block = cext.at[put + core]

        @pl.when(slab == to)
        def _():
            arrived(block, cross_sem.at[k])

        send(block, block, swap_sem.at[k], sibling, slab == to)
        for step in range(1, 4):
            z = jnp.where(zl == 0, step, 7 - step)
            send(block, block, cross_sem.at[k], (z * 2 + core, slab), jnp.logical_and(edge, slab == to))
    for _, to, _, put, k in UPWARD + DOWNWARD:

        @pl.when(slab == to)
        def _():
            arrived(cext.at[put + 1 - core], swap_sem.at[k])

    for buffer, arrival, when in (
        (from_1, halo_sem.at[0], jnp.logical_not(among(0, 16))),
        (to_1, halo_sem.at[1], jnp.logical_not(among(15, 31))),
        (from_2, halo_sem.at[2], jnp.logical_not(among(0, 1, 16, 17))),
        (to_2, halo_sem.at[3], jnp.logical_not(among(14, 15, 30, 31))),
    ):

        @pl.when(when)
        def _():
            arrived(buffer, arrival)

    conductivity_terms(cext, coef, diag, invd, cinv, slab)
    field_terms(fext, hu, slab, 0, DEPTH - 1)
    arrived(recv_z, z_sem)
    res = (zsum[...] + recv_z[...]) - target[...]
    for j in range(RROWS):
        res_row[j] = res[j : j + 1, :]
        res_row[RROWS + j] = -res[j : j + 1, :]
    half = jnp.sum(jnp.sum(0.5 * res * res, axis=0, keepdims=True), axis=1, keepdims=True)
    mis[...] = jnp.broadcast_to(half, (1, NX))
    send(mis, mis_core, mis_sem.at[0], sibling)

    scatter(res_row, row_hot, lane_hot, invd, resid)

    arrived(mis_core, mis_sem.at[0])
    mis_sum[...] = mis[...] + mis_core[...]
    recv_mis[zl] = mis_sum[...]
    for k in range(1, 8):
        z = (zl + k) % 8
        send(mis_sum, recv_mis.at[zl], mis_sem.at[1], (z * 2 + core, slab))

    solve(coef, diag, invd, cinv, resid, direct, work, pe, lam)

    @pl.when(slab < 31)
    def _():
        arrived(top, halo_sem.at[4])

    field_terms(fext, hu, slab, DEPTH - 1, DEPTH)
    cell_products(lam, hu, chunks)

    send(chunks.at[1 - core], recv_core, core_sem, sibling)
    arrived(recv_core, core_sem)
    merged[...] = chunks[core] + recv_core[...]
    for z in range(8):
        send(merged.at[z], recv_src.at[zl], src_sem, (z * 2 + core, slab), zl != z)
    recv_src[zl] = merged[zl]
    arrived(recv_mis.at[pl.ds(0, 7)], mis_sem.at[1])
    arrived(recv_src.at[pl.ds(0, 7)], src_sem)
    for wait, when in sent:
        if when is None:
            wait()
        else:
            pl.when(when)(wait)


def finish(recv_src, recv_mis, grad_ref, misfit_ref):
    total, misfit = recv_src[0], recv_mis[0]
    for k in range(1, 8):
        total, misfit = total + recv_src[k], misfit + recv_mis[k]
    grad_ref[...] = total
    misfit_ref[...] = misfit * (1.0 / (GROUPS * RX))


def on_device(conductivity, forward_fields, receiver_pairs, observed):
    field = forward_fields.reshape(DEPTH, NY, NX)
    pairs = jnp.transpose(receiver_pairs[0])
    conductivity, field, pairs, observed = (
        pltpu.with_memory_space_constraint(a, pltpu.HBM) for a in (conductivity, field, pairs, observed)
    )
    plane = (NY, NX)
    any_spec = pl.BlockSpec(memory_space=pltpu.HBM)
    vmem = pl.BlockSpec(memory_space=pltpu.VMEM)
    dma, regular = pltpu.SemaphoreType.DMA, pltpu.SemaphoreType.REGULAR
    received = pl.pallas_call(
        kernel,
        name="adjoint_gradient",
        out_shape=(
            jax.ShapeDtypeStruct((8, 8, NX), F32),
            jax.ShapeDtypeStruct((8, 1, NX), F32),
        ),
        in_specs=[any_spec] * 4,
        out_specs=(vmem, vmem),
        scratch_shapes=[
            pltpu.VMEM((CELLS, *plane), F32),
            pltpu.VMEM((DEPTH + 1, *plane), F32),
            pltpu.VMEM((2, RX), jnp.int32),
            pltpu.VMEM((GROUPS, RX), F32),
            pltpu.VMEM((IDX, NX), jnp.int32),
            pltpu.VMEM((RROWS, NX), F32),
            pltpu.VMEM((RROWS, NX), F32),
            pltpu.VMEM((16, RROWS, NX), F32),
            pltpu.VMEM((RROWS, NX), F32),
            pltpu.VMEM((RROWS, NX), F32),
            pltpu.VMEM((IDX, 1, NX), F32),
            pltpu.VMEM((IDX, 1, NX), F32),
            pltpu.VMEM((IDX, 1, NX), F32),
            pltpu.VMEM((PLANES * NY, IDX * NX), jnp.bfloat16),
            pltpu.VMEM((NX, IDX * NX), jnp.bfloat16),
            pltpu.VMEM((3, PLANES, *plane), F32),
            pltpu.VMEM((PLANES, *plane), F32),
            pltpu.VMEM((PLANES, *plane), F32),
            pltpu.VMEM((5, *plane), F32),
            pltpu.VMEM((DEPTH, 7, *plane), F32),
            pltpu.VMEM((PLANES, *plane), F32),
            pltpu.VMEM((PLANES, *plane), F32),
            pltpu.VMEM((PLANES, *plane), F32),
            pltpu.VMEM((PLANES, *plane), F32),
            pltpu.VMEM((PLANES, *plane), F32),
            pltpu.VMEM((1, NX), F32),
            pltpu.VMEM((1, NX), F32),
            pltpu.VMEM((1, NX), F32),
            pltpu.VMEM((2, 8, 8, NX), F32),
            pltpu.VMEM((8, 8, NX), F32),
            pltpu.VMEM((8, 8, NX), F32),
            dma((4,)), dma, dma((5,)), dma, dma, dma((2,)), dma, dma,
            dma((3,)), dma((3,)), regular, regular,
        ],
        compiler_params=pltpu.CompilerParams(
            collective_id=0, has_side_effects=True, vmem_limit_bytes=32 * 1024 * 1024
        ),
    )(conductivity, field, pairs, observed)
    grad, misfit = pl.pallas_call(
        finish,
        name="add_groups",
        out_shape=(jax.ShapeDtypeStruct((8, NX), F32), jax.ShapeDtypeStruct((1, NX), F32)),
        in_specs=[vmem] * 2,
        out_specs=(vmem, vmem),
        compiler_params=pltpu.CompilerParams(vmem_limit_bytes=1024 * 1024),
    )(*received)
    return grad.reshape(DEPTH, 2, NX), misfit[0, 0]


def solution(mesh):
    in_specs = (P("slab", None, None), P("src", "slab", None, None), P("src", None, None), P())
    out_specs = (P("slab", "src", None), P())
    return jax.shard_map(
        on_device, mesh=mesh, in_specs=in_specs, out_specs=out_specs, check_vma=False
    )
```

```python
import functools

import jax
import jax.numpy as jnp
from jax import lax
from jax.experimental import pallas as pl
from jax.experimental.pallas import tpu as pltpu
from jax.sharding import PartitionSpec as P

LOWER = 0.3
UPPER = 2.0
OMEGA = 0.6
THETA = 0.5 * (UPPER + LOWER)
DELTA = 0.5 * (UPPER - LOWER)
RATIO = THETA / DELTA
RHO_A = 1.0 / RATIO
RHO_B = 1.0 / (2.0 * RATIO - RHO_A)
ALPHA = RHO_B * RHO_A
BETA = 2.0 * RHO_B / DELTA

NY, NX = 32, 128
DEPTH = 4
BELOW = 5
PLANES = 15
CELLS = 16
RX = 2000
RROWS = 16
IDX = 2 * RROWS
GROUPS = 16
UPWARD = ((14, 16, 8, 0, 0), (15, 16, 6, 2, 1), (15, 16, 8, 4, 2), (15, 17, 8, 0, 0))
DOWNWARD = ((16, 15, 6, 10, 0), (16, 15, 8, 12, 1), (17, 15, 6, 14, 2), (16, 14, 6, 14, 0))
CROSSING = ((14, 16), (15, 16), (15, 17))
NZ = 128
MESH = pl.DeviceIdType.MESH
F32 = jnp.float32
ONE, TWO, THREE = 1.0 / 16.0, 1.0 / 24.0, 1.0 / 48.0


def lanes():
    return lax.broadcasted_iota(jnp.int32, (NY, NX), 1)


def rows():
    return lax.broadcasted_iota(jnp.int32, (NY, NX), 0)


def next_x(v):
    return jnp.where(lanes() < NX - 1, pltpu.roll(v, NX - 1, 1), 0.0)


def prev_x(v):
    return jnp.where(lanes() > 0, pltpu.roll(v, 1, 1), 0.0)


def next_y(v):
    return jnp.where(rows() < NY - 1, pltpu.roll(v, NY - 1, 0), 0.0)


def prev_y(v):
    return jnp.where(rows() > 0, pltpu.roll(v, 1, 0), 0.0)


def prev2_x(v):
    return jnp.where(lanes() > 1, pltpu.roll(v, 2, 1), 0.0)


def prev2_y(v):
    return jnp.where(rows() > 1, pltpu.roll(v, 2, 0), 0.0)


def forward(v):
    moved = next_x(v)
    sx, dx = v + moved, v - moved
    ms, md = next_y(sx), next_y(dx)
    return sx + ms, sx - ms, dx + md, dx - md


def cell_terms(low, high):
    ss, ds, sd, dd = low
    ss2, ds2, sd2, dd2 = high
    return (ss - ss2, ds + ds2, ds - ds2, sd + sd2, sd - sd2, dd + dd2, dd - dd2)


def scatter_cell(low, high, c1, c2, c3):
    zss, sds, zds, ssd, zsd, sdd, zdd = cell_terms(low, high)
    zss = zss * c1
    sds, zds = sds * c1, zds * c2
    ssd, zsd = ssd * c1, zsd * c2
    sdd, zdd = sdd * c2, zdd * c3
    lower = (zss, sds + zds, ssd + zsd, sdd + zdd)
    upper = (-zss, sds - zds, ssd - zsd, sdd - zdd)
    return lower, upper


def backward(parts):
    ss, ds, sd, dd = parts
    os = (ss + ds) + prev_y(ss - ds)
    od = (sd + dd) + prev_y(sd - dd)
    return (os + od) + prev_x(os - od)


def apply_planes(v_ref, coef, first, last, sink):
    low = forward(v_ref[first - 1])
    mid = forward(v_ref[first])
    _, upper = scatter_cell(low, mid, coef[0, first - 1], coef[1, first - 1], coef[2, first - 1])

    def body(p, carry):
        here, above = carry[:4], carry[4:]
        ahead = forward(v_ref[p + 1])
        lower, upper = scatter_cell(here, ahead, coef[0, p], coef[1, p], coef[2, p])
        sink(p, backward([a + b for a, b in zip(lower, above)]))
        return (*ahead, *upper)

    lax.fori_loop(first, last + 1, body, (*mid, *upper), unroll=True)


def read_pairs(pairs, index, place_row, lane_row, slab):
    index[...] = jnp.full((IDX, NX), 1 << 24, jnp.int32)
    for j in range(RROWS):
        width = min(NX, RX - j * NX)
        for at, end in ((j, 0), (RROWS + j, 1)):
            index[at : at + 1, 0:width] = pairs[end : end + 1, pl.ds(j * NX, width)]
    lane = jnp.bitwise_and(index[...], NX - 1).astype(F32)
    place = (jnp.right_shift(index[...], 7) - (slab * DEPTH - BELOW) * NY).astype(F32)
    for j in range(IDX):
        place_row[j] = place[j : j + 1, :]
        lane_row[j] = lane[j : j + 1, :]


def read_target(obs, target, src):
    target[...] = jnp.zeros((RROWS, NX), F32)
    for j in range(RROWS):
        width = min(NX, RX - j * NX)
        mine = lax.broadcasted_iota(jnp.int32, (GROUPS, width), 0) == src
        target[j : j + 1, 0:width] = jnp.sum(
            jnp.where(mine, obs[:, pl.ds(j * NX, width)], 0.0), axis=0, keepdims=True
        )


def gather(fext, index, part, slab):
    lane = jnp.bitwise_and(index[...], NX - 1)
    line = jnp.right_shift(index[...], 7) - slab * (DEPTH * NY)

    def pick(block, acc):
        values = fext[block // 4, pl.ds((block % 4) * 8, 8), :]
        for k in range(8):
            spread = jnp.broadcast_to(values[k : k + 1, :], (IDX, NX))
            found = jnp.take_along_axis(spread, lane, axis=1, mode="promise_in_bounds")
            acc = jnp.where(line == block * 8 + k, found, acc)
        return acc

    picked = lax.fori_loop(0, DEPTH * NY // 8, pick, jnp.zeros((IDX, NX), F32), unroll=True)
    part[...] = picked[:RROWS] - picked[RROWS:]


def one_hots(place_row, lane_row, row_hot, lane_hot):
    def hot(j, carry):
        columns = pl.ds(pl.multiple_of(j * NX, NX), NX)
        for at, out, size in ((place_row, row_hot, PLANES * NY), (lane_row, lane_hot, NX)):
            spread = jnp.broadcast_to(at[j], (size, NX))
            line_id = lax.broadcasted_iota(jnp.int32, (size, NX), 0).astype(F32)
            out[:, columns] = jnp.where(spread == line_id, 1.0, 0.0).astype(jnp.bfloat16)
        return carry

    lax.fori_loop(0, IDX, hot, 0)


def inside(plane, slab):
    z = slab * DEPTH + plane
    return jnp.logical_and(z >= 0, z < NZ)


def conductivity_terms(cext, coef, diag, invd, cinv, slab):
    def masked_cells(e):
        return jnp.where(inside(e - 6, slab), cext[e], 0.0)

    def around(cells):
        along = cells + prev_x(cells)
        return along + prev_y(along)

    def diagonals(p, below):
        cells = masked_cells(p + 1)
        coef[0, p] = cells * ONE
        coef[1, p] = cells * TWO
        coef[2, p] = cells * THREE
        boxed = around(cells)
        value = (boxed + below) * (1.0 / 3.0)
        keep = inside(p - BELOW, slab)
        diag[p] = jnp.where(keep, value, 0.0)
        invd[p] = jnp.where(keep, 1.0 / jnp.where(keep, value, 1.0), 0.0)
        return boxed

    lax.fori_loop(0, PLANES, diagonals, around(masked_cells(0)), unroll=5)

    even = jnp.logical_and(lanes() % 2 == 0, rows() % 2 == 0)

    def coarse_box(j):
        pair = masked_cells(2 * j + 2) + masked_cells(2 * j + 3)
        pair = pair + next_y(pair)
        pair = jnp.where(even, pair + next_x(pair), 0.0)
        pair = pair + prev2_x(pair)
        return pair + prev2_y(pair)

    def coarse(j, below):
        boxed = coarse_box(j)
        value = (boxed + below) * (0.125 * 2.0 / 3.0)
        keep = jnp.logical_and(even, inside(2 * (j - 2), slab))
        cinv[j - 1] = jnp.where(keep, OMEGA / jnp.where(keep, value, 1.0), 0.0)
        return boxed

    lax.fori_loop(1, 6, coarse, coarse_box(0), unroll=True)


def field_terms(fext, hu, slab, start, stop):
    def terms(p, low):
        high = forward(jnp.where(inside(p + 1, slab), fext[p + 1], 0.0))
        scales = (-ONE, -ONE, -TWO, -ONE, -TWO, -TWO, -THREE)
        for k, (term, scale) in enumerate(zip(cell_terms(low, high), scales)):
            hu[p, k] = term * scale
        return high

    lax.fori_loop(start, stop, terms, forward(fext[start]), unroll=True)


def scatter(res_row, row_hot, lane_hot, invd, resid):
    high_parts, low_parts = [], []
    for j in range(IDX):
        value = jnp.broadcast_to(res_row[j], (16, NX))
        high = value.astype(jnp.bfloat16)
        low = (value - high.astype(F32)).astype(jnp.bfloat16)
        hot = lane_hot[:, j * NX : (j + 1) * NX].reshape(NX // 16, 16, NX)
        high_parts.append((hot * high[None]).reshape(NX, NX))
        low_parts.append((hot * low[None]).reshape(NX, NX))
    by_lane = jnp.concatenate(
        [jnp.concatenate(high_parts, axis=1), jnp.concatenate(low_parts, axis=1)], axis=0
    )
    both = lax.dot_general(
        row_hot[...], by_lane, (((1,), (1,)), ((), ())), preferred_element_type=F32
    )
    resid[...] = (both[:, :NX] + both[:, NX:]).reshape(PLANES, NY, NX) * invd[...]


def solve(coef, diag, invd, cinv, resid, direct, work, pe, lam):
    def first_step(p, applied):
        r = resid[p]
        r1 = r - (applied * (1.0 / THETA)) * invd[p]
        d2 = (ALPHA / THETA) * r + BETA * r1
        resid[p] = r1
        direct[p] = d2
        lam[p] = r * (1.0 / THETA) + d2

    apply_planes(resid, coef, 1, 13, first_step)

    def second_step(p, applied):
        r2 = resid[p] - applied * invd[p]
        resid[p] = r2
        f = diag[p] * r2
        f = f + 0.5 * (prev_x(f) + next_x(f))
        work[p] = f + 0.5 * (prev_y(f) + next_y(f))

    apply_planes(direct, coef, 2, 12, second_step)

    def correct(j):
        p = 2 * j + 3
        c = (work[p] + 0.5 * (work[p - 1] + work[p + 1])) * cinv[j]
        c = c + 0.5 * (prev_y(c) + next_y(c))
        return c + 0.5 * (prev_x(c) + next_x(c))

    def prolong(j, below):
        c = correct(j)
        pe[2 * j + 3] = c
        pe[2 * j + 2] = 0.5 * (below + c)
        return c

    first = correct(0)
    pe[3] = first
    lax.fori_loop(1, 5, prolong, first, unroll=True)

    def third_step(p, applied):
        r3 = resid[p] - applied * invd[p]
        resid[p] = r3
        lam[p] = lam[p] + pe[p] + r3 * (1.0 / THETA)

    apply_planes(pe, coef, 4, 10, third_step)

    def fourth_step(p, applied):
        r3 = resid[p]
        r4 = r3 - (applied * (1.0 / THETA)) * invd[p]
        lam[p] = lam[p] + (ALPHA / THETA) * r3 + BETA * r4

    apply_planes(resid, coef, 5, 9, fourth_step)


def cell_products(lam, hu, chunks):
    low = forward(lam[BELOW])
    for p in range(DEPTH):
        high = forward(lam[BELOW + p + 1])
        total = None
        for k, term in enumerate(cell_terms(low, high)):
            piece = term * hu[p, k]
            total = piece if total is None else total + piece
        low = high
        for z in range(8):
            for c in range(2):
                at = 4 * z + 2 * c
                chunks[c, z, 2 * p : 2 * p + 2, :] = total[at : at + 2, :]


def kernel(
    cond_hbm, field_hbm, pairs_hbm, obs_hbm,
    recv_src, recv_mis,
    cext, fext, pairs, obs, index, target,
    part, recv_xy, zsum, recv_z,
    place_row, lane_row, res_row, row_hot, lane_hot, coef, diag, invd, cinv, hu,
    resid, direct, work, lam, pe,
    mis, mis_core, mis_sum, chunks, recv_core, merged,
    in_sem, send_sem, sum_sem, halo_sem, xy_sem, z_sem, mis_sem, core_sem, src_sem,
    cross_sem, swap_sem, go, ready,
):
    src = lax.axis_index("src")
    slab = lax.axis_index("slab")
    zl, core = src // 2, src % 2
    zh, px, py = slab // 16, (slab // 4) % 4, slab % 4
    here = px * 4 + py
    hops = (0, 1, 2, 1)
    offsets = sorted(((i, j) for i in range(4) for j in range(4)), key=lambda o: -hops[o[0]] - hops[o[1]])
    plane_peers = [(src, zh * 16 + ((px + i) % 4) * 4 + (py + j) % 4) for i, j in offsets[:-1]]
    sibling = (zl * 2 + 1 - core, slab)
    edge = jnp.logical_or(zl == 0, zl == 7)
    beyond = (7 - zl) * 2 + core

    loads = [
        pltpu.make_async_copy(pairs_hbm, pairs, in_sem.at[0]),
        pltpu.make_async_copy(field_hbm, fext.at[pl.ds(0, DEPTH)], in_sem.at[1]),
        pltpu.make_async_copy(cond_hbm, cext.at[pl.ds(6, DEPTH)], in_sem.at[2]),
        pltpu.make_async_copy(obs_hbm, obs, in_sem.at[3]),
    ]
    for load in loads:
        load.start()

    barrier = pltpu.get_barrier_semaphore()

    def signal(sem, peer):
        pl.semaphore_signal(sem, inc=1, device_id=peer, device_id_type=MESH)

    for peer in plane_peers:
        signal(barrier, peer)

    @pl.when(core == 0)
    def _():
        signal(barrier, sibling)

    signal(barrier, (zl * 2, (1 - zh) * 16 + here))
    for k in range(1, 8):
        signal(barrier, (((zl + k) % 8) * 2, slab))
    for low, high in CROSSING:
        for at, to in ((low, high), (high, low)):

            @pl.when(jnp.logical_and(edge, slab == at))
            def _():
                signal(barrier, ((7 - zl) * 2, to))

    @pl.when(slab == 15)
    def _():
        signal(barrier, (zl * 2, 16))

    loads[0].wait()
    read_pairs(pairs, index, place_row, lane_row, slab)
    loads[1].wait()
    gather(fext, index, part, slab)

    @pl.when(core == 1)
    def _():
        recv_xy[1, here] = part[...]

    sent = []

    def send(source, dest, arrival, peer, when=None):
        copy = pltpu.make_async_remote_copy(
            src_ref=source, dst_ref=dest, send_sem=send_sem, recv_sem=arrival,
            device_id=peer, device_id_type=MESH,
        )
        sent.append((copy.wait_send, when))
        if when is None:
            copy.start()
        else:
            pl.when(when)(copy.start)

    def arrived(buffer, arrival):
        pltpu.make_async_copy(buffer, buffer, arrival).wait()

    @pl.when(core == 1)
    def _():
        pl.semaphore_wait(barrier, 15 + 1)
        signal(go, sibling)

    @pl.when(core == 0)
    def _():
        pl.semaphore_wait(go, 1)

    for _, peer in plane_peers:
        send(part, recv_xy.at[core, here], xy_sem.at[core], (zl * 2 + 1, peer))
    send(part, recv_xy.at[0, here], xy_sem.at[0], sibling, core == 0)

    crossed = sum((slab == t).astype(jnp.int32) for pair in CROSSING for t in pair)
    far = 1 + 7 + crossed * edge.astype(jnp.int32) + (slab == 16).astype(jnp.int32)

    @pl.when(core == 0)
    def _():
        pl.semaphore_wait(barrier, 15 + 2 * far)
        signal(ready, sibling)

    @pl.when(core == 1)
    def _():
        pl.semaphore_wait(ready, 1)

    loads[2].wait()

    def cross(blocks):
        for at, to, take, put, k in blocks:
            send(
                cext.at[take + core], cext.at[put + core], cross_sem.at[k], (beyond, to),
                jnp.logical_and(edge, slab == at),
            )

    own = cext.at[pl.ds(6, DEPTH)]
    own_low, own_high = cext.at[pl.ds(6, 2)], cext.at[pl.ds(8, 2)]
    from_1, from_2 = cext.at[pl.ds(2, DEPTH)], cext.at[pl.ds(0, 2)]
    to_1, to_2 = cext.at[pl.ds(10, DEPTH)], cext.at[pl.ds(14, 2)]
    up_1, up_2 = (src, (slab + 1) % 32), (src, (slab + 2) % 32)
    down_1, down_2 = (src, (slab + 31) % 32), (src, (slab + 30) % 32)

    def among(*slabs):
        found = slab == slabs[0]
        for other in slabs[1:]:
            found = jnp.logical_or(found, slab == other)
        return found

    sends_up_1, sends_up_2 = (jnp.logical_not(among(*t)) for t in ((15, 31), (14, 15, 30, 31)))
    sends_down_1, sends_down_2 = (jnp.logical_not(among(*t)) for t in ((0, 16), (0, 1, 16, 17)))
    top = fext.at[pl.ds(DEPTH, 1)]
    bottom = fext.at[pl.ds(0, 1)]
    send(own, to_1, halo_sem.at[1], down_1, sends_down_1)
    send(bottom, top, halo_sem.at[4], down_1, sends_down_1)
    send(own_low, to_2, halo_sem.at[3], down_2, sends_down_2)
    send(own, from_1, halo_sem.at[0], up_1, sends_up_1)
    send(own_high, from_2, halo_sem.at[2], up_2, sends_up_2)

    cross(DOWNWARD + UPWARD)
    loads[3].wait()
    read_target(obs, target, src)
    one_hots(place_row, lane_row, row_hot, lane_hot)

    def add_plane(k):
        return lax.fori_loop(1, 16, lambda i, acc: acc + recv_xy[k, i], recv_xy[k, 0], unroll=True)

    def send_sum(source, to, slot):
        return pltpu.make_async_remote_copy(
            src_ref=source, dst_ref=to[0], send_sem=sum_sem.at[slot], recv_sem=to[1],
            device_id=to[2], device_id_type=MESH,
        )

    other_half = (1 - zh) * 16 + here
    sums = [
        send_sum(zsum.at[1], (recv_z, z_sem.at[1], (zl * 2, other_half)), 0),
        send_sum(zsum.at[1], (zsum.at[0], z_sem.at[0], sibling), 1),
        send_sum(zsum.at[0], (recv_z, z_sem.at[1], (zl * 2 + 1, other_half)), 2),
    ]

    @pl.when(core == 1)
    def _():
        arrived(recv_xy.at[0], xy_sem.at[0])
        zsum[1] = add_plane(0)
        sums[0].start()
        sums[1].start()
        arrived(recv_xy.at[1, pl.ds(0, 15)], xy_sem.at[1])
        zsum[0] = add_plane(1)
        sums[2].start()

    send(bottom, top, halo_sem.at[4], down_1, slab == 16)

    for _, to, _, put, k in UPWARD + DOWNWARD:
        block = cext.at[put + core]

        @pl.when(slab == to)
        def _():
            arrived(block, cross_sem.at[k])

        send(block, block, swap_sem.at[k], sibling, slab == to)
        for step in range(1, 4):
            z = jnp.where(zl == 0, step, 7 - step)
            send(block, block, cross_sem.at[k], (z * 2 + core, slab), jnp.logical_and(edge, slab == to))
    for _, to, _, put, k in UPWARD + DOWNWARD:

        @pl.when(slab == to)
        def _():
            arrived(cext.at[put + 1 - core], swap_sem.at[k])

    for buffer, arrival, when in (
        (from_1, halo_sem.at[0], jnp.logical_not(among(0, 16))),
        (to_1, halo_sem.at[1], jnp.logical_not(among(15, 31))),
        (from_2, halo_sem.at[2], jnp.logical_not(among(0, 1, 16, 17))),
        (to_2, halo_sem.at[3], jnp.logical_not(among(14, 15, 30, 31))),
    ):

        @pl.when(when)
        def _():
            arrived(buffer, arrival)

    conductivity_terms(cext, coef, diag, invd, cinv, slab)
    field_terms(fext, hu, slab, 0, DEPTH - 1)

    @pl.when(core == 0)
    def _():
        arrived(zsum.at[0], z_sem.at[0])

    arrived(recv_z, z_sem.at[1])
    res = (zsum[0] + recv_z[...]) - target[...]
    for j in range(RROWS):
        res_row[j] = res[j : j + 1, :]
        res_row[RROWS + j] = -res[j : j + 1, :]
    half = jnp.sum(jnp.sum(0.5 * res * res, axis=0, keepdims=True), axis=1, keepdims=True)
    mis[...] = jnp.broadcast_to(half, (1, NX))
    send(mis, mis_core, mis_sem.at[0], sibling)

    scatter(res_row, row_hot, lane_hot, invd, resid)

    arrived(mis_core, mis_sem.at[0])
    mis_sum[...] = mis[...] + mis_core[...]
    recv_mis[zl] = mis_sum[...]
    for k in range(1, 8):
        z = (zl + k) % 8
        send(mis_sum, recv_mis.at[zl], mis_sem.at[1], (z * 2 + core, slab))

    solve(coef, diag, invd, cinv, resid, direct, work, pe, lam)

    @pl.when(slab < 31)
    def _():
        arrived(top, halo_sem.at[4])

    field_terms(fext, hu, slab, DEPTH - 1, DEPTH)
    cell_products(lam, hu, chunks)

    send(chunks.at[1 - core], recv_core, core_sem, sibling)
    arrived(recv_core, core_sem)
    merged[...] = chunks[core] + recv_core[...]
    for z in range(8):
        send(merged.at[z], recv_src.at[zl], src_sem, (z * 2 + core, slab), zl != z)
    recv_src[zl] = merged[zl]
    arrived(recv_mis.at[pl.ds(0, 7)], mis_sem.at[1])
    arrived(recv_src.at[pl.ds(0, 7)], src_sem)

    @pl.when(core == 1)
    def _():
        for copy in sums:
            copy.wait_send()

    for wait, when in sent:
        if when is None:
            wait()
        else:
            pl.when(when)(wait)


def finish(recv_src, recv_mis, grad_ref, misfit_ref):
    total, misfit = recv_src[0], recv_mis[0]
    for k in range(1, 8):
        total, misfit = total + recv_src[k], misfit + recv_mis[k]
    grad_ref[...] = total
    misfit_ref[...] = misfit * (1.0 / (GROUPS * RX))


def on_device(conductivity, forward_fields, receiver_pairs, observed):
    field = forward_fields.reshape(DEPTH, NY, NX)
    pairs = jnp.transpose(receiver_pairs[0])
    conductivity, field, pairs, observed = (
        pltpu.with_memory_space_constraint(a, pltpu.HBM) for a in (conductivity, field, pairs, observed)
    )
    plane = (NY, NX)
    any_spec = pl.BlockSpec(memory_space=pltpu.HBM)
    vmem = pl.BlockSpec(memory_space=pltpu.VMEM)
    dma, regular = pltpu.SemaphoreType.DMA, pltpu.SemaphoreType.REGULAR
    received = pl.pallas_call(
        kernel,
        name="adjoint_gradient",
        out_shape=(
            jax.ShapeDtypeStruct((8, 8, NX), F32),
            jax.ShapeDtypeStruct((8, 1, NX), F32),
        ),
        in_specs=[any_spec] * 4,
        out_specs=(vmem, vmem),
        scratch_shapes=[
            pltpu.VMEM((CELLS, *plane), F32),
            pltpu.VMEM((DEPTH + 1, *plane), F32),
            pltpu.VMEM((2, RX), jnp.int32),
            pltpu.VMEM((GROUPS, RX), F32),
            pltpu.VMEM((IDX, NX), jnp.int32),
            pltpu.VMEM((RROWS, NX), F32),
            pltpu.VMEM((RROWS, NX), F32),
            pltpu.VMEM((2, 16, RROWS, NX), F32),
            pltpu.VMEM((2, RROWS, NX), F32),
            pltpu.VMEM((RROWS, NX), F32),
            pltpu.VMEM((IDX, 1, NX), F32),
            pltpu.VMEM((IDX, 1, NX), F32),
            pltpu.VMEM((IDX, 1, NX), F32),
            pltpu.VMEM((PLANES * NY, IDX * NX), jnp.bfloat16),
            pltpu.VMEM((NX, IDX * NX), jnp.bfloat16),
            pltpu.VMEM((3, PLANES, *plane), F32),
            pltpu.VMEM((PLANES, *plane), F32),
            pltpu.VMEM((PLANES, *plane), F32),
            pltpu.VMEM((5, *plane), F32),
            pltpu.VMEM((DEPTH, 7, *plane), F32),
            pltpu.VMEM((PLANES, *plane), F32),
            pltpu.VMEM((PLANES, *plane), F32),
            pltpu.VMEM((PLANES, *plane), F32),
            pltpu.VMEM((PLANES, *plane), F32),
            pltpu.VMEM((PLANES, *plane), F32),
            pltpu.VMEM((1, NX), F32),
            pltpu.VMEM((1, NX), F32),
            pltpu.VMEM((1, NX), F32),
            pltpu.VMEM((2, 8, 8, NX), F32),
            pltpu.VMEM((8, 8, NX), F32),
            pltpu.VMEM((8, 8, NX), F32),
            dma((4,)), dma, dma((3,)), dma((5,)), dma((2,)), dma((2,)), dma((2,)), dma, dma,
            dma((3,)), dma((3,)), regular, regular,
        ],
        compiler_params=pltpu.CompilerParams(
            collective_id=0, has_side_effects=True, vmem_limit_bytes=32 * 1024 * 1024
        ),
    )(conductivity, field, pairs, observed)
    grad, misfit = pl.pallas_call(
        finish,
        name="add_groups",
        out_shape=(jax.ShapeDtypeStruct((8, NX), F32), jax.ShapeDtypeStruct((1, NX), F32)),
        in_specs=[vmem] * 2,
        out_specs=(vmem, vmem),
        compiler_params=pltpu.CompilerParams(vmem_limit_bytes=1024 * 1024),
    )(*received)
    return grad.reshape(DEPTH, 2, NX), misfit[0, 0]


def solution(mesh):
    in_specs = (P("slab", None, None), P("src", "slab", None, None), P("src", None, None), P())
    out_specs = (P("slab", "src", None), P())
    return jax.shard_map(
        on_device, mesh=mesh, in_specs=in_specs, out_specs=out_specs, check_vma=False
    )
```

```python
import functools

import jax
import jax.numpy as jnp
from jax import lax
from jax.experimental import pallas as pl
from jax.experimental.pallas import tpu as pltpu
from jax.sharding import PartitionSpec as P

LOWER = 0.3
UPPER = 2.0
OMEGA = 0.6
THETA = 0.5 * (UPPER + LOWER)
DELTA = 0.5 * (UPPER - LOWER)
RATIO = THETA / DELTA
RHO_A = 1.0 / RATIO
RHO_B = 1.0 / (2.0 * RATIO - RHO_A)
ALPHA = RHO_B * RHO_A
BETA = 2.0 * RHO_B / DELTA

NY, NX = 32, 128
DEPTH = 4
BELOW = 5
PLANES = 15
CELLS = 16
RX = 2000
RROWS = 16
IDX = 2 * RROWS
GROUPS = 16
UPWARD = ((14, 16, 8, 0, 0), (15, 16, 6, 2, 1), (15, 16, 8, 4, 2), (15, 17, 8, 0, 0))
DOWNWARD = ((16, 15, 6, 10, 0), (16, 15, 8, 12, 1), (17, 15, 6, 14, 2), (16, 14, 6, 14, 0))
CROSSING = ((14, 16), (15, 16), (15, 17))
NZ = 128
MESH = pl.DeviceIdType.MESH
F32 = jnp.float32
ONE, TWO, THREE = 1.0 / 16.0, 1.0 / 24.0, 1.0 / 48.0


def lanes():
    return lax.broadcasted_iota(jnp.int32, (NY, NX), 1)


def rows():
    return lax.broadcasted_iota(jnp.int32, (NY, NX), 0)


def next_x(v):
    return jnp.where(lanes() < NX - 1, pltpu.roll(v, NX - 1, 1), 0.0)


def prev_x(v):
    return jnp.where(lanes() > 0, pltpu.roll(v, 1, 1), 0.0)


def next_y(v):
    return jnp.where(rows() < NY - 1, pltpu.roll(v, NY - 1, 0), 0.0)


def prev_y(v):
    return jnp.where(rows() > 0, pltpu.roll(v, 1, 0), 0.0)


def prev2_x(v):
    return jnp.where(lanes() > 1, pltpu.roll(v, 2, 1), 0.0)


def prev2_y(v):
    return jnp.where(rows() > 1, pltpu.roll(v, 2, 0), 0.0)


def forward(v):
    moved = next_x(v)
    sx, dx = v + moved, v - moved
    ms, md = next_y(sx), next_y(dx)
    return sx + ms, sx - ms, dx + md, dx - md


def cell_terms(low, high):
    ss, ds, sd, dd = low
    ss2, ds2, sd2, dd2 = high
    return (ss - ss2, ds + ds2, ds - ds2, sd + sd2, sd - sd2, dd + dd2, dd - dd2)


def scatter_cell(low, high, c1, c2, c3):
    zss, sds, zds, ssd, zsd, sdd, zdd = cell_terms(low, high)
    zss = zss * c1
    sds, zds = sds * c1, zds * c2
    ssd, zsd = ssd * c1, zsd * c2
    sdd, zdd = sdd * c2, zdd * c3
    lower = (zss, sds + zds, ssd + zsd, sdd + zdd)
    upper = (-zss, sds - zds, ssd - zsd, sdd - zdd)
    return lower, upper


def backward(parts):
    ss, ds, sd, dd = parts
    os = (ss + ds) + prev_y(ss - ds)
    od = (sd + dd) + prev_y(sd - dd)
    return (os + od) + prev_x(os - od)


def apply_planes(v_ref, coef, first, last, sink):
    low = forward(v_ref[first - 1])
    mid = forward(v_ref[first])
    _, upper = scatter_cell(low, mid, coef[0, first - 1], coef[1, first - 1], coef[2, first - 1])

    def body(p, carry):
        here, above = carry[:4], carry[4:]
        ahead = forward(v_ref[p + 1])
        lower, upper = scatter_cell(here, ahead, coef[0, p], coef[1, p], coef[2, p])
        sink(p, backward([a + b for a, b in zip(lower, above)]))
        return (*ahead, *upper)

    lax.fori_loop(first, last + 1, body, (*mid, *upper), unroll=True)


def read_pairs(pairs, index, place_row, lane_row, slab):
    index[...] = jnp.full((IDX, NX), 1 << 24, jnp.int32)
    for j in range(RROWS):
        width = min(NX, RX - j * NX)
        for at, end in ((j, 0), (RROWS + j, 1)):
            index[at : at + 1, 0:width] = pairs[end : end + 1, pl.ds(j * NX, width)]
    lane = jnp.bitwise_and(index[...], NX - 1).astype(F32)
    place = (jnp.right_shift(index[...], 7) - (slab * DEPTH - BELOW) * NY).astype(F32)
    for j in range(IDX):
        place_row[j] = place[j : j + 1, :]
        lane_row[j] = lane[j : j + 1, :]


def read_target(obs, target, src):
    target[...] = jnp.zeros((RROWS, NX), F32)
    for j in range(RROWS):
        width = min(NX, RX - j * NX)
        mine = lax.broadcasted_iota(jnp.int32, (GROUPS, width), 0) == src
        target[j : j + 1, 0:width] = jnp.sum(
            jnp.where(mine, obs[:, pl.ds(j * NX, width)], 0.0), axis=0, keepdims=True
        )


def gather(fext, index, part, slab):
    lane = jnp.bitwise_and(index[...], NX - 1)
    line = jnp.right_shift(index[...], 7) - slab * (DEPTH * NY)

    def pick(block, acc):
        values = fext[block // 4, pl.ds((block % 4) * 8, 8), :]
        for k in range(8):
            spread = jnp.broadcast_to(values[k : k + 1, :], (IDX, NX))
            found = jnp.take_along_axis(spread, lane, axis=1, mode="promise_in_bounds")
            acc = jnp.where(line == block * 8 + k, found, acc)
        return acc

    picked = lax.fori_loop(0, DEPTH * NY // 8, pick, jnp.zeros((IDX, NX), F32), unroll=True)
    part[...] = picked[:RROWS] - picked[RROWS:]


def one_hots(place_row, lane_row, row_hot, lane_hot):
    def hot(j, carry):
        columns = pl.ds(pl.multiple_of(j * NX, NX), NX)
        for at, out, size in ((place_row, row_hot, PLANES * NY), (lane_row, lane_hot, NX)):
            spread = jnp.broadcast_to(at[j], (size, NX))
            line_id = lax.broadcasted_iota(jnp.int32, (size, NX), 0).astype(F32)
            out[:, columns] = jnp.where(spread == line_id, 1.0, 0.0).astype(jnp.bfloat16)
        return carry

    lax.fori_loop(0, IDX, hot, 0)


def inside(plane, slab):
    z = slab * DEPTH + plane
    return jnp.logical_and(z >= 0, z < NZ)


def conductivity_terms(cext, coef, diag, invd, cinv, slab):
    def masked_cells(e):
        return jnp.where(inside(e - 6, slab), cext[e], 0.0)

    def around(cells):
        along = cells + prev_x(cells)
        return along + prev_y(along)

    def diagonals(p, below):
        cells = masked_cells(p + 1)
        coef[0, p] = cells * ONE
        coef[1, p] = cells * TWO
        coef[2, p] = cells * THREE
        boxed = around(cells)
        value = (boxed + below) * (1.0 / 3.0)
        keep = inside(p - BELOW, slab)
        diag[p] = jnp.where(keep, value, 0.0)
        invd[p] = jnp.where(keep, 1.0 / jnp.where(keep, value, 1.0), 0.0)
        return boxed

    lax.fori_loop(0, PLANES, diagonals, around(masked_cells(0)), unroll=5)

    even = jnp.logical_and(lanes() % 2 == 0, rows() % 2 == 0)

    def coarse_box(j):
        pair = masked_cells(2 * j + 2) + masked_cells(2 * j + 3)
        pair = pair + next_y(pair)
        pair = jnp.where(even, pair + next_x(pair), 0.0)
        pair = pair + prev2_x(pair)
        return pair + prev2_y(pair)

    def coarse(j, below):
        boxed = coarse_box(j)
        value = (boxed + below) * (0.125 * 2.0 / 3.0)
        keep = jnp.logical_and(even, inside(2 * (j - 2), slab))
        cinv[j - 1] = jnp.where(keep, OMEGA / jnp.where(keep, value, 1.0), 0.0)
        return boxed

    lax.fori_loop(1, 6, coarse, coarse_box(0), unroll=True)


def field_terms(fext, hu, slab, start, stop):
    def terms(p, low):
        high = forward(jnp.where(inside(p + 1, slab), fext[p + 1], 0.0))
        scales = (-ONE, -ONE, -TWO, -ONE, -TWO, -TWO, -THREE)
        for k, (term, scale) in enumerate(zip(cell_terms(low, high), scales)):
            hu[p, k] = term * scale
        return high

    lax.fori_loop(start, stop, terms, forward(fext[start]), unroll=True)


def scatter(res_row, row_hot, lane_hot, invd, resid):
    high_parts, low_parts = [], []
    for j in range(IDX):
        value = jnp.broadcast_to(res_row[j], (16, NX))
        high = value.astype(jnp.bfloat16)
        low = (value - high.astype(F32)).astype(jnp.bfloat16)
        hot = lane_hot[:, j * NX : (j + 1) * NX].reshape(NX // 16, 16, NX)
        high_parts.append((hot * high[None]).reshape(NX, NX))
        low_parts.append((hot * low[None]).reshape(NX, NX))
    by_lane = jnp.concatenate(
        [jnp.concatenate(high_parts, axis=1), jnp.concatenate(low_parts, axis=1)], axis=0
    )
    both = lax.dot_general(
        row_hot[...], by_lane, (((1,), (1,)), ((), ())), preferred_element_type=F32
    )
    resid[...] = (both[:, :NX] + both[:, NX:]).reshape(PLANES, NY, NX) * invd[...]


def solve(coef, diag, invd, cinv, resid, direct, work, pe, lam):
    def first_step(p, applied):
        r = resid[p]
        r1 = r - (applied * (1.0 / THETA)) * invd[p]
        d2 = (ALPHA / THETA) * r + BETA * r1
        resid[p] = r1
        direct[p] = d2
        lam[p] = r * (1.0 / THETA) + d2

    apply_planes(resid, coef, 1, 13, first_step)

    def second_step(p, applied):
        r2 = resid[p] - applied * invd[p]
        resid[p] = r2
        work[p] = diag[p] * r2

    apply_planes(direct, coef, 2, 12, second_step)

    def correct(j):
        p = 2 * j + 3
        c = work[p] + 0.5 * (work[p - 1] + work[p + 1])
        c = c + 0.5 * (prev_y(c) + next_y(c))
        c = (c + 0.5 * (prev_x(c) + next_x(c))) * cinv[j]
        c = c + 0.5 * (prev_y(c) + next_y(c))
        return c + 0.5 * (prev_x(c) + next_x(c))

    def prolong(j, below):
        c = correct(j)
        pe[2 * j + 3] = c
        pe[2 * j + 2] = 0.5 * (below + c)
        return c

    first = correct(0)
    pe[3] = first
    lax.fori_loop(1, 5, prolong, first, unroll=True)

    def third_step(p, applied):
        r3 = resid[p] - applied * invd[p]
        resid[p] = r3
        lam[p] = lam[p] + pe[p] + r3 * (1.0 / THETA)

    apply_planes(pe, coef, 4, 10, third_step)

    def fourth_step(p, applied):
        r3 = resid[p]
        r4 = r3 - (applied * (1.0 / THETA)) * invd[p]
        lam[p] = lam[p] + (ALPHA / THETA) * r3 + BETA * r4

    apply_planes(resid, coef, 5, 9, fourth_step)


def cell_products(lam, hu, chunks):
    low = forward(lam[BELOW])
    for p in range(DEPTH):
        high = forward(lam[BELOW + p + 1])
        total = None
        for k, term in enumerate(cell_terms(low, high)):
            piece = term * hu[p, k]
            total = piece if total is None else total + piece
        low = high
        for z in range(8):
            for c in range(2):
                at = 4 * z + 2 * c
                chunks[c, z, 2 * p : 2 * p + 2, :] = total[at : at + 2, :]


def kernel(
    cond_hbm, field_hbm, pairs_hbm, obs_hbm,
    recv_src, recv_mis,
    cext, fext, pairs, obs, index, target,
    part, recv_xy, zsum, recv_z,
    place_row, lane_row, res_row, row_hot, lane_hot, coef, diag, invd, cinv, hu,
    resid, direct, work, lam, pe,
    mis, chunks,
    in_sem, send_sem, sum_sem, halo_sem, xy_sem, z_sem, mis_sem, src_sem,
    cross_sem, swap_sem, go, ready,
):
    src = lax.axis_index("src")
    slab = lax.axis_index("slab")
    zl, core = src // 2, src % 2
    zh, px, py = slab // 16, (slab // 4) % 4, slab % 4
    here = px * 4 + py
    hops = (0, 1, 2, 1)
    offsets = sorted(((i, j) for i in range(4) for j in range(4)), key=lambda o: -hops[o[0]] - hops[o[1]])
    plane_peers = [(src, zh * 16 + ((px + i) % 4) * 4 + (py + j) % 4) for i, j in offsets[:-1]]
    sibling = (zl * 2 + 1 - core, slab)
    edge = jnp.logical_or(zl == 0, zl == 7)
    beyond = (7 - zl) * 2 + core

    loads = [
        pltpu.make_async_copy(pairs_hbm, pairs, in_sem.at[0]),
        pltpu.make_async_copy(field_hbm, fext.at[pl.ds(0, DEPTH)], in_sem.at[1]),
        pltpu.make_async_copy(cond_hbm, cext.at[pl.ds(6, DEPTH)], in_sem.at[2]),
        pltpu.make_async_copy(obs_hbm, obs, in_sem.at[3]),
    ]
    for load in loads:
        load.start()

    barrier = pltpu.get_barrier_semaphore()

    def signal(sem, peer):
        pl.semaphore_signal(sem, inc=1, device_id=peer, device_id_type=MESH)

    for peer in plane_peers:
        signal(barrier, peer)

    @pl.when(core == 0)
    def _():
        signal(barrier, sibling)

    signal(barrier, (zl * 2, (1 - zh) * 16 + here))
    for k in range(1, 8):
        signal(barrier, (((zl + k) % 8) * 2, slab))
    for low, high in CROSSING:
        for at, to in ((low, high), (high, low)):

            @pl.when(jnp.logical_and(edge, slab == at))
            def _():
                signal(barrier, ((7 - zl) * 2, to))

    @pl.when(slab == 15)
    def _():
        signal(barrier, (zl * 2, 16))

    loads[0].wait()
    read_pairs(pairs, index, place_row, lane_row, slab)
    loads[1].wait()
    gather(fext, index, part, slab)

    @pl.when(core == 1)
    def _():
        recv_xy[1, here] = part[...]

    sent = []

    def send(source, dest, arrival, peer, when=None):
        copy = pltpu.make_async_remote_copy(
            src_ref=source, dst_ref=dest, send_sem=send_sem, recv_sem=arrival,
            device_id=peer, device_id_type=MESH,
        )
        sent.append((copy.wait_send, when))
        if when is None:
            copy.start()
        else:
            pl.when(when)(copy.start)

    def arrived(buffer, arrival):
        pltpu.make_async_copy(buffer, buffer, arrival).wait()

    @pl.when(core == 1)
    def _():
        pl.semaphore_wait(barrier, 15 + 1)
        signal(go, sibling)

    @pl.when(core == 0)
    def _():
        pl.semaphore_wait(go, 1)

    for _, peer in plane_peers:
        send(part, recv_xy.at[core, here], xy_sem.at[core], (zl * 2 + 1, peer))
    send(part, recv_xy.at[0, here], xy_sem.at[0], sibling, core == 0)

    crossed = sum((slab == t).astype(jnp.int32) for pair in CROSSING for t in pair)
    far = 1 + 7 + crossed * edge.astype(jnp.int32) + (slab == 16).astype(jnp.int32)

    @pl.when(core == 0)
    def _():
        pl.semaphore_wait(barrier, 15 + 2 * far)
        signal(ready, sibling)

    @pl.when(core == 1)
    def _():
        pl.semaphore_wait(ready, 1)

    loads[2].wait()

    def cross(blocks):
        for at, to, take, put, k in blocks:
            send(
                cext.at[take + core], cext.at[put + core], cross_sem.at[k], (beyond, to),
                jnp.logical_and(edge, slab == at),
            )

    own = cext.at[pl.ds(6, DEPTH)]
    own_low, own_high = cext.at[pl.ds(6, 2)], cext.at[pl.ds(8, 2)]
    from_1, from_2 = cext.at[pl.ds(2, DEPTH)], cext.at[pl.ds(0, 2)]
    to_1, to_2 = cext.at[pl.ds(10, DEPTH)], cext.at[pl.ds(14, 2)]
    up_1, up_2 = (src, (slab + 1) % 32), (src, (slab + 2) % 32)
    down_1, down_2 = (src, (slab + 31) % 32), (src, (slab + 30) % 32)

    def among(*slabs):
        found = slab == slabs[0]
        for other in slabs[1:]:
            found = jnp.logical_or(found, slab == other)
        return found

    sends_up_1, sends_up_2 = (jnp.logical_not(among(*t)) for t in ((15, 31), (14, 15, 30, 31)))
    sends_down_1, sends_down_2 = (jnp.logical_not(among(*t)) for t in ((0, 16), (0, 1, 16, 17)))
    top = fext.at[pl.ds(DEPTH, 1)]
    bottom = fext.at[pl.ds(0, 1)]
    send(own, to_1, halo_sem.at[1], down_1, sends_down_1)
    send(bottom, top, halo_sem.at[4], down_1, sends_down_1)
    send(own_low, to_2, halo_sem.at[3], down_2, sends_down_2)
    send(own, from_1, halo_sem.at[0], up_1, sends_up_1)
    send(own_high, from_2, halo_sem.at[2], up_2, sends_up_2)

    cross(DOWNWARD + UPWARD)
    loads[3].wait()
    read_target(obs, target, src)
    one_hots(place_row, lane_row, row_hot, lane_hot)

    def add_plane(k):
        return lax.fori_loop(1, 16, lambda i, acc: acc + recv_xy[k, i], recv_xy[k, 0], unroll=True)

    def send_sum(source, to, slot):
        return pltpu.make_async_remote_copy(
            src_ref=source, dst_ref=to[0], send_sem=sum_sem.at[slot], recv_sem=to[1],
            device_id=to[2], device_id_type=MESH,
        )

    other_half = (1 - zh) * 16 + here
    sums = [
        send_sum(zsum.at[1], (recv_z, z_sem.at[1], (zl * 2, other_half)), 0),
        send_sum(zsum.at[1], (zsum.at[0], z_sem.at[0], sibling), 1),
        send_sum(zsum.at[0], (recv_z, z_sem.at[1], (zl * 2 + 1, other_half)), 2),
    ]

    @pl.when(core == 1)
    def _():
        arrived(recv_xy.at[0], xy_sem.at[0])
        zsum[1] = add_plane(0)
        sums[0].start()
        sums[1].start()
        arrived(recv_xy.at[1, pl.ds(0, 15)], xy_sem.at[1])
        zsum[0] = add_plane(1)
        sums[2].start()

    send(bottom, top, halo_sem.at[4], down_1, slab == 16)

    for _, to, _, put, k in UPWARD + DOWNWARD:
        block = cext.at[put + core]

        @pl.when(slab == to)
        def _():
            arrived(block, cross_sem.at[k])

        send(block, block, swap_sem.at[k], sibling, slab == to)
        for step in range(1, 4):
            z = jnp.where(zl == 0, step, 7 - step)
            send(block, block, cross_sem.at[k], (z * 2 + core, slab), jnp.logical_and(edge, slab == to))
    for _, to, _, put, k in UPWARD + DOWNWARD:

        @pl.when(slab == to)
        def _():
            arrived(cext.at[put + 1 - core], swap_sem.at[k])

    for buffer, arrival, when in (
        (from_1, halo_sem.at[0], jnp.logical_not(among(0, 16))),
        (to_1, halo_sem.at[1], jnp.logical_not(among(15, 31))),
        (from_2, halo_sem.at[2], jnp.logical_not(among(0, 1, 16, 17))),
        (to_2, halo_sem.at[3], jnp.logical_not(among(14, 15, 30, 31))),
    ):

        @pl.when(when)
        def _():
            arrived(buffer, arrival)

    conductivity_terms(cext, coef, diag, invd, cinv, slab)
    field_terms(fext, hu, slab, 0, DEPTH - 1)

    @pl.when(core == 0)
    def _():
        arrived(zsum.at[0], z_sem.at[0])

    arrived(recv_z, z_sem.at[1])
    res = (zsum[0] + recv_z[...]) - target[...]
    for j in range(RROWS):
        res_row[j] = res[j : j + 1, :]
        res_row[RROWS + j] = -res[j : j + 1, :]
    scatter(res_row, row_hot, lane_hot, invd, resid)

    half = jnp.sum(jnp.sum(0.5 * res * res, axis=0, keepdims=True), axis=1, keepdims=True)
    mis[...] = jnp.broadcast_to(half, (1, NX))
    recv_mis[src] = mis[...]
    for z in range(8):
        for c in (1, 0):
            send(mis, recv_mis.at[src], mis_sem, (z * 2 + c, slab), src != z * 2 + c)

    solve(coef, diag, invd, cinv, resid, direct, work, pe, lam)

    @pl.when(slab < 31)
    def _():
        arrived(top, halo_sem.at[4])

    field_terms(fext, hu, slab, DEPTH - 1, DEPTH)
    cell_products(lam, hu, chunks)

    for z in range(8):
        for c in (1, 0):
            send(chunks.at[c, z], recv_src.at[src], src_sem, (z * 2 + c, slab), src != z * 2 + c)
    recv_src[src] = chunks[core, zl]
    arrived(recv_mis.at[pl.ds(0, 15)], mis_sem)
    arrived(recv_src.at[pl.ds(0, 15)], src_sem)

    @pl.when(core == 1)
    def _():
        for copy in sums:
            copy.wait_send()

    for wait, when in sent:
        if when is None:
            wait()
        else:
            pl.when(when)(wait)


def finish(recv_src, recv_mis, grad_ref, misfit_ref):
    total, misfit = recv_src[0], recv_mis[0]
    for k in range(1, GROUPS):
        total, misfit = total + recv_src[k], misfit + recv_mis[k]
    grad_ref[...] = total
    misfit_ref[...] = misfit * (1.0 / (GROUPS * RX))


def on_device(conductivity, forward_fields, receiver_pairs, observed):
    field = forward_fields.reshape(DEPTH, NY, NX)
    pairs = jnp.transpose(receiver_pairs[0])
    conductivity, field, pairs, observed = (
        pltpu.with_memory_space_constraint(a, pltpu.HBM) for a in (conductivity, field, pairs, observed)
    )
    plane = (NY, NX)
    any_spec = pl.BlockSpec(memory_space=pltpu.HBM)
    vmem = pl.BlockSpec(memory_space=pltpu.VMEM)
    dma, regular = pltpu.SemaphoreType.DMA, pltpu.SemaphoreType.REGULAR
    received = pl.pallas_call(
        kernel,
        name="adjoint_gradient",
        out_shape=(
            jax.ShapeDtypeStruct((GROUPS, 8, NX), F32),
            jax.ShapeDtypeStruct((GROUPS, 1, NX), F32),
        ),
        in_specs=[any_spec] * 4,
        out_specs=(vmem, vmem),
        scratch_shapes=[
            pltpu.VMEM((CELLS, *plane), F32),
            pltpu.VMEM((DEPTH + 1, *plane), F32),
            pltpu.VMEM((2, RX), jnp.int32),
            pltpu.VMEM((GROUPS, RX), F32),
            pltpu.VMEM((IDX, NX), jnp.int32),
            pltpu.VMEM((RROWS, NX), F32),
            pltpu.VMEM((RROWS, NX), F32),
            pltpu.VMEM((2, 16, RROWS, NX), F32),
            pltpu.VMEM((2, RROWS, NX), F32),
            pltpu.VMEM((RROWS, NX), F32),
            pltpu.VMEM((IDX, 1, NX), F32),
            pltpu.VMEM((IDX, 1, NX), F32),
            pltpu.VMEM((IDX, 1, NX), F32),
            pltpu.VMEM((PLANES * NY, IDX * NX), jnp.bfloat16),
            pltpu.VMEM((NX, IDX * NX), jnp.bfloat16),
            pltpu.VMEM((3, PLANES, *plane), F32),
            pltpu.VMEM((PLANES, *plane), F32),
            pltpu.VMEM((PLANES, *plane), F32),
            pltpu.VMEM((5, *plane), F32),
            pltpu.VMEM((DEPTH, 7, *plane), F32),
            pltpu.VMEM((PLANES, *plane), F32),
            pltpu.VMEM((PLANES, *plane), F32),
            pltpu.VMEM((PLANES, *plane), F32),
            pltpu.VMEM((PLANES, *plane), F32),
            pltpu.VMEM((PLANES, *plane), F32),
            pltpu.VMEM((1, NX), F32),
            pltpu.VMEM((2, 8, 8, NX), F32),
            dma((4,)), dma, dma((3,)), dma((5,)), dma((2,)), dma((2,)), dma, dma,
            dma((3,)), dma((3,)), regular, regular,
        ],
        compiler_params=pltpu.CompilerParams(
            collective_id=0, has_side_effects=True, vmem_limit_bytes=32 * 1024 * 1024
        ),
    )(conductivity, field, pairs, observed)
    grad, misfit = pl.pallas_call(
        finish,
        name="add_groups",
        out_shape=(jax.ShapeDtypeStruct((8, NX), F32), jax.ShapeDtypeStruct((1, NX), F32)),
        in_specs=[vmem] * 2,
        out_specs=(vmem, vmem),
        compiler_params=pltpu.CompilerParams(vmem_limit_bytes=1024 * 1024),
    )(*received)
    return grad.reshape(DEPTH, 2, NX), misfit[0, 0]


def solution(mesh):
    in_specs = (P("slab", None, None), P("src", "slab", None, None), P("src", None, None), P())
    out_specs = (P("slab", "src", None), P())
    return jax.shard_map(
        on_device, mesh=mesh, in_specs=in_specs, out_specs=out_specs, check_vma=False
    )
```

```python
import functools

import jax
import jax.numpy as jnp
from jax import lax
from jax.experimental import pallas as pl
from jax.experimental.pallas import tpu as pltpu
from jax.sharding import PartitionSpec as P

LOWER = 0.3
UPPER = 2.0
OMEGA = 0.6
THETA = 0.5 * (UPPER + LOWER)
DELTA = 0.5 * (UPPER - LOWER)
RATIO = THETA / DELTA
RHO_A = 1.0 / RATIO
RHO_B = 1.0 / (2.0 * RATIO - RHO_A)
ALPHA = RHO_B * RHO_A
BETA = 2.0 * RHO_B / DELTA

NY, NX = 32, 128
DEPTH = 4
BELOW = 5
PLANES = 15
CELLS = 16
RX = 2000
RROWS = 16
IDX = 2 * RROWS
GROUPS = 16
UPWARD = ((14, 16, 8, 0, 0), (15, 16, 6, 2, 1), (15, 16, 8, 4, 2), (15, 17, 8, 0, 0))
DOWNWARD = ((16, 15, 6, 10, 0), (16, 15, 8, 12, 1), (17, 15, 6, 14, 2), (16, 14, 6, 14, 0))
CROSSING = ((14, 16), (15, 16), (15, 17))
NZ = 128
MESH = pl.DeviceIdType.MESH
F32 = jnp.float32
ONE, TWO, THREE = 1.0 / 16.0, 1.0 / 24.0, 1.0 / 48.0


def lanes():
    return lax.broadcasted_iota(jnp.int32, (NY, NX), 1)


def rows():
    return lax.broadcasted_iota(jnp.int32, (NY, NX), 0)


def next_x(v):
    return jnp.where(lanes() < NX - 1, pltpu.roll(v, NX - 1, 1), 0.0)


def prev_x(v):
    return jnp.where(lanes() > 0, pltpu.roll(v, 1, 1), 0.0)


def next_y(v):
    return jnp.where(rows() < NY - 1, pltpu.roll(v, NY - 1, 0), 0.0)


def prev_y(v):
    return jnp.where(rows() > 0, pltpu.roll(v, 1, 0), 0.0)


def prev2_x(v):
    return jnp.where(lanes() > 1, pltpu.roll(v, 2, 1), 0.0)


def prev2_y(v):
    return jnp.where(rows() > 1, pltpu.roll(v, 2, 0), 0.0)


def forward(v):
    moved = next_x(v)
    sx, dx = v + moved, v - moved
    ms, md = next_y(sx), next_y(dx)
    return sx + ms, sx - ms, dx + md, dx - md


def cell_terms(low, high):
    ss, ds, sd, dd = low
    ss2, ds2, sd2, dd2 = high
    return (ss - ss2, ds + ds2, ds - ds2, sd + sd2, sd - sd2, dd + dd2, dd - dd2)


def scatter_cell(low, high, c1, c2, c3):
    zss, sds, zds, ssd, zsd, sdd, zdd = cell_terms(low, high)
    zss = zss * c1
    sds, zds = sds * c1, zds * c2
    ssd, zsd = ssd * c1, zsd * c2
    sdd, zdd = sdd * c2, zdd * c3
    lower = (zss, sds + zds, ssd + zsd, sdd + zdd)
    upper = (-zss, sds - zds, ssd - zsd, sdd - zdd)
    return lower, upper


def backward(parts):
    ss, ds, sd, dd = parts
    os = (ss + ds) + prev_y(ss - ds)
    od = (sd + dd) + prev_y(sd - dd)
    return (os + od) + prev_x(os - od)


def apply_planes(v_ref, coef, first, last, sink):
    low = forward(v_ref[first - 1])
    mid = forward(v_ref[first])
    _, upper = scatter_cell(low, mid, coef[0, first - 1], coef[1, first - 1], coef[2, first - 1])

    def body(p, carry):
        here, above = carry[:4], carry[4:]
        ahead = forward(v_ref[p + 1])
        lower, upper = scatter_cell(here, ahead, coef[0, p], coef[1, p], coef[2, p])
        sink(p, backward([a + b for a, b in zip(lower, above)]))
        return (*ahead, *upper)

    lax.fori_loop(first, last + 1, body, (*mid, *upper), unroll=True)


def read_pairs(pairs, index, place_row, lane_row, slab):
    index[...] = jnp.full((IDX, NX), 1 << 24, jnp.int32)
    for j in range(RROWS):
        width = min(NX, RX - j * NX)
        for at, end in ((j, 0), (RROWS + j, 1)):
            index[at : at + 1, 0:width] = pairs[end : end + 1, pl.ds(j * NX, width)]
    lane = jnp.bitwise_and(index[...], NX - 1).astype(F32)
    place = (jnp.right_shift(index[...], 7) - (slab * DEPTH - BELOW) * NY).astype(F32)
    for j in range(IDX):
        place_row[j] = place[j : j + 1, :]
        lane_row[j] = lane[j : j + 1, :]


def read_target(obs, target, src):
    target[...] = jnp.zeros((RROWS, NX), F32)
    for j in range(RROWS):
        width = min(NX, RX - j * NX)
        mine = lax.broadcasted_iota(jnp.int32, (GROUPS, width), 0) == src
        target[j : j + 1, 0:width] = jnp.sum(
            jnp.where(mine, obs[:, pl.ds(j * NX, width)], 0.0), axis=0, keepdims=True
        )


def gather(fext, index, part, slab):
    lane = jnp.bitwise_and(index[...], NX - 1)
    line = jnp.right_shift(index[...], 7) - slab * (DEPTH * NY)

    def pick(block, acc):
        values = fext[block // 4, pl.ds((block % 4) * 8, 8), :]
        for k in range(8):
            spread = jnp.broadcast_to(values[k : k + 1, :], (IDX, NX))
            found = jnp.take_along_axis(spread, lane, axis=1, mode="promise_in_bounds")
            acc = jnp.where(line == block * 8 + k, found, acc)
        return acc

    picked = lax.fori_loop(0, DEPTH * NY // 8, pick, jnp.zeros((IDX, NX), F32), unroll=True)
    part[...] = picked[:RROWS] - picked[RROWS:]


def one_hots(place_row, lane_row, row_hot, lane_hot):
    def hot(j, carry):
        columns = pl.ds(pl.multiple_of(j * NX, NX), NX)
        for at, out, size in ((place_row, row_hot, PLANES * NY), (lane_row, lane_hot, NX)):
            spread = jnp.broadcast_to(at[j], (size, NX))
            line_id = lax.broadcasted_iota(jnp.int32, (size, NX), 0).astype(F32)
            out[:, columns] = jnp.where(spread == line_id, 1.0, 0.0).astype(jnp.bfloat16)
        return carry

    lax.fori_loop(0, IDX, hot, 0)


def inside(plane, slab):
    z = slab * DEPTH + plane
    return jnp.logical_and(z >= 0, z < NZ)


def conductivity_terms(cext, coef, diag, invd, cinv, slab):
    def masked_cells(e):
        return jnp.where(inside(e - 6, slab), cext[e], 0.0)

    def around(cells):
        along = cells + prev_x(cells)
        return along + prev_y(along)

    def diagonals(p, below):
        cells = masked_cells(p + 1)
        coef[0, p] = cells * ONE
        coef[1, p] = cells * TWO
        coef[2, p] = cells * THREE
        boxed = around(cells)
        value = (boxed + below) * (1.0 / 3.0)
        keep = inside(p - BELOW, slab)
        diag[p] = jnp.where(keep, value, 0.0)
        invd[p] = jnp.where(keep, 1.0 / jnp.where(keep, value, 1.0), 0.0)
        return boxed

    lax.fori_loop(0, PLANES, diagonals, around(masked_cells(0)), unroll=5)

    even = jnp.logical_and(lanes() % 2 == 0, rows() % 2 == 0)

    def coarse_box(j):
        pair = masked_cells(2 * j + 2) + masked_cells(2 * j + 3)
        pair = pair + next_y(pair)
        pair = jnp.where(even, pair + next_x(pair), 0.0)
        pair = pair + prev2_x(pair)
        return pair + prev2_y(pair)

    def coarse(j, below):
        boxed = coarse_box(j)
        value = (boxed + below) * (0.125 * 2.0 / 3.0)
        keep = jnp.logical_and(even, inside(2 * (j - 2), slab))
        cinv[j - 1] = jnp.where(keep, OMEGA / jnp.where(keep, value, 1.0), 0.0)
        return boxed

    lax.fori_loop(1, 6, coarse, coarse_box(0), unroll=True)


def field_terms(fext, hu, slab, start, stop):
    def terms(p, low):
        high = forward(jnp.where(inside(p + 1, slab), fext[p + 1], 0.0))
        scales = (-ONE, -ONE, -TWO, -ONE, -TWO, -TWO, -THREE)
        for k, (term, scale) in enumerate(zip(cell_terms(low, high), scales)):
            hu[p, k] = term * scale
        return high

    lax.fori_loop(start, stop, terms, forward(fext[start]), unroll=True)


def scatter(res_row, row_hot, lane_hot, invd, resid):
    high_parts, low_parts = [], []
    for j in range(IDX):
        value = jnp.broadcast_to(res_row[j], (16, NX))
        high = value.astype(jnp.bfloat16)
        low = (value - high.astype(F32)).astype(jnp.bfloat16)
        hot = lane_hot[:, j * NX : (j + 1) * NX].reshape(NX // 16, 16, NX)
        high_parts.append((hot * high[None]).reshape(NX, NX))
        low_parts.append((hot * low[None]).reshape(NX, NX))
    by_lane = jnp.concatenate(
        [jnp.concatenate(high_parts, axis=1), jnp.concatenate(low_parts, axis=1)], axis=0
    )
    both = lax.dot_general(
        row_hot[...], by_lane, (((1,), (1,)), ((), ())), preferred_element_type=F32
    )
    resid[...] = (both[:, :NX] + both[:, NX:]).reshape(PLANES, NY, NX) * invd[...]


def solve(coef, diag, invd, cinv, resid, direct, work, pe, lam):
    def first_step(p, applied):
        r = resid[p]
        r1 = r - (applied * (1.0 / THETA)) * invd[p]
        d2 = (ALPHA / THETA) * r + BETA * r1
        resid[p] = r1
        direct[p] = d2
        lam[p] = r * (1.0 / THETA) + d2

    apply_planes(resid, coef, 1, 13, first_step)

    def second_step(p, applied):
        r2 = resid[p] - applied * invd[p]
        resid[p] = r2
        work[p] = diag[p] * r2

    apply_planes(direct, coef, 2, 12, second_step)

    def correct(j):
        p = 2 * j + 3
        c = work[p] + 0.5 * (work[p - 1] + work[p + 1])
        c = c + 0.5 * (prev_y(c) + next_y(c))
        c = (c + 0.5 * (prev_x(c) + next_x(c))) * cinv[j]
        c = c + 0.5 * (prev_y(c) + next_y(c))
        return c + 0.5 * (prev_x(c) + next_x(c))

    def prolong(j, below):
        c = correct(j)
        pe[2 * j + 3] = c
        pe[2 * j + 2] = 0.5 * (below + c)
        return c

    first = correct(0)
    pe[3] = first
    lax.fori_loop(1, 5, prolong, first, unroll=True)

    def third_step(p, applied):
        r3 = resid[p] - applied * invd[p]
        resid[p] = r3
        lam[p] = lam[p] + pe[p] + r3 * (1.0 / THETA)

    apply_planes(pe, coef, 4, 10, third_step)

    def fourth_step(p, applied):
        r3 = resid[p]
        r4 = r3 - (applied * (1.0 / THETA)) * invd[p]
        lam[p] = lam[p] + (ALPHA / THETA) * r3 + BETA * r4

    apply_planes(resid, coef, 5, 9, fourth_step)


def cell_products(lam, hu, chunks):
    low = forward(lam[BELOW])
    for p in range(DEPTH):
        high = forward(lam[BELOW + p + 1])
        total = None
        for k, term in enumerate(cell_terms(low, high)):
            piece = term * hu[p, k]
            total = piece if total is None else total + piece
        low = high
        for z in range(8):
            for c in range(2):
                at = 4 * z + 2 * c
                chunks[c, z, 2 * p : 2 * p + 2, :] = total[at : at + 2, :]


def kernel(
    cond_hbm, field_hbm, pairs_hbm, obs_hbm,
    recv_src, recv_mis,
    cext, fext, pairs, obs, index, target,
    part, recv_xy, zsum, recv_z,
    place_row, lane_row, res_row, row_hot, lane_hot, coef, diag, invd, cinv, hu,
    resid, direct, work, lam, pe,
    mis, chunks,
    in_sem, send_sem, sum_sem, halo_sem, xy_sem, z_sem, mis_sem, src_sem,
    cross_sem, swap_sem, go, ready,
):
    src = lax.axis_index("src")
    slab = lax.axis_index("slab")
    zl, core = src // 2, src % 2
    zh, px, py = slab // 16, (slab // 4) % 4, slab % 4
    here = px * 4 + py
    hops = (0, 1, 2, 1)
    offsets = sorted(((i, j) for i in range(4) for j in range(4)), key=lambda o: -hops[o[0]] - hops[o[1]])
    plane_peers = [(src, zh * 16 + ((px + i) % 4) * 4 + (py + j) % 4) for i, j in offsets[:-1]]
    sibling = (zl * 2 + 1 - core, slab)
    edge = jnp.logical_or(zl == 0, zl == 7)
    beyond = (7 - zl) * 2 + core

    loads = [
        pltpu.make_async_copy(pairs_hbm, pairs, in_sem.at[0]),
        pltpu.make_async_copy(field_hbm, fext.at[pl.ds(0, DEPTH)], in_sem.at[1]),
        pltpu.make_async_copy(cond_hbm, cext.at[pl.ds(6, DEPTH)], in_sem.at[2]),
        pltpu.make_async_copy(obs_hbm, obs, in_sem.at[3]),
    ]
    for load in loads:
        load.start()

    barrier = pltpu.get_barrier_semaphore()

    def signal(sem, peer):
        pl.semaphore_signal(sem, inc=1, device_id=peer, device_id_type=MESH)

    for peer in plane_peers:
        signal(barrier, peer)

    @pl.when(core == 0)
    def _():
        signal(barrier, sibling)

    signal(barrier, (zl * 2, (1 - zh) * 16 + here))
    for k in range(1, 8):
        signal(barrier, (((zl + k) % 8) * 2, slab))
    for low, high in CROSSING:
        for at, to in ((low, high), (high, low)):

            @pl.when(jnp.logical_and(edge, slab == at))
            def _():
                signal(barrier, ((7 - zl) * 2, to))

    @pl.when(slab == 15)
    def _():
        signal(barrier, (zl * 2, 16))

    loads[0].wait()
    read_pairs(pairs, index, place_row, lane_row, slab)
    loads[1].wait()
    gather(fext, index, part, slab)

    @pl.when(core == 1)
    def _():
        recv_xy[1, here] = part[...]

    sent = []

    def send(source, dest, arrival, peer, when=None):
        copy = pltpu.make_async_remote_copy(
            src_ref=source, dst_ref=dest, send_sem=send_sem, recv_sem=arrival,
            device_id=peer, device_id_type=MESH,
        )
        sent.append((copy.wait_send, when))
        if when is None:
            copy.start()
        else:
            pl.when(when)(copy.start)

    def arrived(buffer, arrival):
        pltpu.make_async_copy(buffer, buffer, arrival).wait()

    @pl.when(core == 1)
    def _():
        pl.semaphore_wait(barrier, 15 + 1)
        signal(go, sibling)

    @pl.when(core == 0)
    def _():
        pl.semaphore_wait(go, 1)

    for _, peer in plane_peers:
        send(part, recv_xy.at[core, here], xy_sem.at[core], (zl * 2 + 1, peer))
    send(part, recv_xy.at[0, here], xy_sem.at[0], sibling, core == 0)

    crossed = sum((slab == t).astype(jnp.int32) for pair in CROSSING for t in pair)
    far = 1 + 7 + crossed * edge.astype(jnp.int32) + (slab == 16).astype(jnp.int32)

    @pl.when(core == 0)
    def _():
        pl.semaphore_wait(barrier, 15 + 2 * far)
        signal(ready, sibling)

    @pl.when(core == 1)
    def _():
        pl.semaphore_wait(ready, 1)

    loads[2].wait()

    def cross(blocks):
        for at, to, take, put, k in blocks:
            send(
                cext.at[take + core], cext.at[put + core], cross_sem.at[k], (beyond, to),
                jnp.logical_and(edge, slab == at),
            )

    own = cext.at[pl.ds(6, DEPTH)]
    own_low, own_high = cext.at[pl.ds(6, 2)], cext.at[pl.ds(8, 2)]
    from_1, from_2 = cext.at[pl.ds(2, DEPTH)], cext.at[pl.ds(0, 2)]
    to_1, to_2 = cext.at[pl.ds(10, DEPTH)], cext.at[pl.ds(14, 2)]
    up_1, up_2 = (src, (slab + 1) % 32), (src, (slab + 2) % 32)
    down_1, down_2 = (src, (slab + 31) % 32), (src, (slab + 30) % 32)

    def among(*slabs):
        found = slab == slabs[0]
        for other in slabs[1:]:
            found = jnp.logical_or(found, slab == other)
        return found

    sends_up_1, sends_up_2 = (jnp.logical_not(among(*t)) for t in ((15, 31), (14, 15, 30, 31)))
    sends_down_1, sends_down_2 = (jnp.logical_not(among(*t)) for t in ((0, 16), (0, 1, 16, 17)))
    top = fext.at[pl.ds(DEPTH, 1)]
    bottom = fext.at[pl.ds(0, 1)]
    cross(DOWNWARD + UPWARD)
    send(own, to_1, halo_sem.at[1], down_1, sends_down_1)
    send(bottom, top, halo_sem.at[4], down_1, sends_down_1)
    send(own_low, to_2, halo_sem.at[3], down_2, sends_down_2)
    send(own, from_1, halo_sem.at[0], up_1, sends_up_1)
    send(own_high, from_2, halo_sem.at[2], up_2, sends_up_2)

    loads[3].wait()
    read_target(obs, target, src)

    @pl.when(among(14, 15))
    def _():
        one_hots(place_row, lane_row, row_hot, lane_hot)

    def add_plane(k):
        return lax.fori_loop(1, 16, lambda i, acc: acc + recv_xy[k, i], recv_xy[k, 0], unroll=True)

    def send_sum(source, to, slot):
        return pltpu.make_async_remote_copy(
            src_ref=source, dst_ref=to[0], send_sem=sum_sem.at[slot], recv_sem=to[1],
            device_id=to[2], device_id_type=MESH,
        )

    other_half = (1 - zh) * 16 + here
    sums = [
        send_sum(zsum.at[1], (recv_z, z_sem.at[1], (zl * 2, other_half)), 0),
        send_sum(zsum.at[1], (zsum.at[0], z_sem.at[0], sibling), 1),
        send_sum(zsum.at[0], (recv_z, z_sem.at[1], (zl * 2 + 1, other_half)), 2),
    ]

    @pl.when(core == 1)
    def _():
        arrived(recv_xy.at[0], xy_sem.at[0])
        zsum[1] = add_plane(0)
        sums[0].start()
        sums[1].start()
        arrived(recv_xy.at[1, pl.ds(0, 15)], xy_sem.at[1])
        zsum[0] = add_plane(1)
        sums[2].start()

    send(bottom, top, halo_sem.at[4], down_1, slab == 16)

    for _, to, _, put, k in UPWARD + DOWNWARD:

        @pl.when(slab == to)
        def _():
            arrived(cext.at[put + core], cross_sem.at[k])

    for _, to, _, put, k in UPWARD + DOWNWARD:
        block = cext.at[put + core]
        send(block, block, swap_sem.at[k], sibling, slab == to)
    for step in (3, 2, 1):
        z = jnp.where(zl == 0, step, 7 - step)
        for _, to, _, put, k in UPWARD + DOWNWARD:
            block = cext.at[put + core]
            send(block, block, cross_sem.at[k], (z * 2 + core, slab), jnp.logical_and(edge, slab == to))
    for _, to, _, put, k in UPWARD + DOWNWARD:

        @pl.when(slab == to)
        def _():
            arrived(cext.at[put + 1 - core], swap_sem.at[k])

    @pl.when(jnp.logical_not(among(14, 15)))
    def _():
        one_hots(place_row, lane_row, row_hot, lane_hot)

    for buffer, arrival, when in (
        (from_1, halo_sem.at[0], jnp.logical_not(among(0, 16))),
        (to_1, halo_sem.at[1], jnp.logical_not(among(15, 31))),
        (from_2, halo_sem.at[2], jnp.logical_not(among(0, 1, 16, 17))),
        (to_2, halo_sem.at[3], jnp.logical_not(among(14, 15, 30, 31))),
    ):

        @pl.when(when)
        def _():
            arrived(buffer, arrival)

    conductivity_terms(cext, coef, diag, invd, cinv, slab)
    field_terms(fext, hu, slab, 0, DEPTH - 1)

    @pl.when(core == 0)
    def _():
        arrived(zsum.at[0], z_sem.at[0])

    arrived(recv_z, z_sem.at[1])
    res = (zsum[0] + recv_z[...]) - target[...]
    for j in range(RROWS):
        res_row[j] = res[j : j + 1, :]
        res_row[RROWS + j] = -res[j : j + 1, :]
    scatter(res_row, row_hot, lane_hot, invd, resid)

    half = jnp.sum(jnp.sum(0.5 * res * res, axis=0, keepdims=True), axis=1, keepdims=True)
    mis[...] = jnp.broadcast_to(half, (1, NX))
    recv_mis[src] = mis[...]
    for z in range(8):
        for c in (1, 0):
            send(mis, recv_mis.at[src], mis_sem, (z * 2 + c, slab), src != z * 2 + c)

    solve(coef, diag, invd, cinv, resid, direct, work, pe, lam)

    @pl.when(slab < 31)
    def _():
        arrived(top, halo_sem.at[4])

    field_terms(fext, hu, slab, DEPTH - 1, DEPTH)
    cell_products(lam, hu, chunks)

    for z in range(8):
        for c in (1, 0):
            send(chunks.at[c, z], recv_src.at[src], src_sem, (z * 2 + c, slab), src != z * 2 + c)
    recv_src[src] = chunks[core, zl]
    arrived(recv_mis.at[pl.ds(0, 15)], mis_sem)
    arrived(recv_src.at[pl.ds(0, 15)], src_sem)

    @pl.when(core == 1)
    def _():
        for copy in sums:
            copy.wait_send()

    for wait, when in sent:
        if when is None:
            wait()
        else:
            pl.when(when)(wait)


def finish(recv_src, recv_mis, grad_ref, misfit_ref):
    total, misfit = recv_src[0], recv_mis[0]
    for k in range(1, GROUPS):
        total, misfit = total + recv_src[k], misfit + recv_mis[k]
    grad_ref[...] = total
    misfit_ref[...] = misfit * (1.0 / (GROUPS * RX))


def on_device(conductivity, forward_fields, receiver_pairs, observed):
    field = forward_fields.reshape(DEPTH, NY, NX)
    pairs = jnp.transpose(receiver_pairs[0])
    conductivity, field, pairs, observed = (
        pltpu.with_memory_space_constraint(a, pltpu.HBM) for a in (conductivity, field, pairs, observed)
    )
    plane = (NY, NX)
    any_spec = pl.BlockSpec(memory_space=pltpu.HBM)
    vmem = pl.BlockSpec(memory_space=pltpu.VMEM)
    dma, regular = pltpu.SemaphoreType.DMA, pltpu.SemaphoreType.REGULAR
    received = pl.pallas_call(
        kernel,
        name="adjoint_gradient",
        out_shape=(
            jax.ShapeDtypeStruct((GROUPS, 8, NX), F32),
            jax.ShapeDtypeStruct((GROUPS, 1, NX), F32),
        ),
        in_specs=[any_spec] * 4,
        out_specs=(vmem, vmem),
        scratch_shapes=[
            pltpu.VMEM((CELLS, *plane), F32),
            pltpu.VMEM((DEPTH + 1, *plane), F32),
            pltpu.VMEM((2, RX), jnp.int32),
            pltpu.VMEM((GROUPS, RX), F32),
            pltpu.VMEM((IDX, NX), jnp.int32),
            pltpu.VMEM((RROWS, NX), F32),
            pltpu.VMEM((RROWS, NX), F32),
            pltpu.VMEM((2, 16, RROWS, NX), F32),
            pltpu.VMEM((2, RROWS, NX), F32),
            pltpu.VMEM((RROWS, NX), F32),
            pltpu.VMEM((IDX, 1, NX), F32),
            pltpu.VMEM((IDX, 1, NX), F32),
            pltpu.VMEM((IDX, 1, NX), F32),
            pltpu.VMEM((PLANES * NY, IDX * NX), jnp.bfloat16),
            pltpu.VMEM((NX, IDX * NX), jnp.bfloat16),
            pltpu.VMEM((3, PLANES, *plane), F32),
            pltpu.VMEM((PLANES, *plane), F32),
            pltpu.VMEM((PLANES, *plane), F32),
            pltpu.VMEM((5, *plane), F32),
            pltpu.VMEM((DEPTH, 7, *plane), F32),
            pltpu.VMEM((PLANES, *plane), F32),
            pltpu.VMEM((PLANES, *plane), F32),
            pltpu.VMEM((PLANES, *plane), F32),
            pltpu.VMEM((PLANES, *plane), F32),
            pltpu.VMEM((PLANES, *plane), F32),
            pltpu.VMEM((1, NX), F32),
            pltpu.VMEM((2, 8, 8, NX), F32),
            dma((4,)), dma, dma((3,)), dma((5,)), dma((2,)), dma((2,)), dma, dma,
            dma((3,)), dma((3,)), regular, regular,
        ],
        compiler_params=pltpu.CompilerParams(
            collective_id=0, has_side_effects=True, vmem_limit_bytes=32 * 1024 * 1024
        ),
    )(conductivity, field, pairs, observed)
    grad, misfit = pl.pallas_call(
        finish,
        name="add_groups",
        out_shape=(jax.ShapeDtypeStruct((8, NX), F32), jax.ShapeDtypeStruct((1, NX), F32)),
        in_specs=[vmem] * 2,
        out_specs=(vmem, vmem),
        compiler_params=pltpu.CompilerParams(vmem_limit_bytes=1024 * 1024),
    )(*received)
    return grad.reshape(DEPTH, 2, NX), misfit[0, 0]


def solution(mesh):
    in_specs = (P("slab", None, None), P("src", "slab", None, None), P("src", None, None), P())
    out_specs = (P("slab", "src", None), P())
    return jax.shard_map(
        on_device, mesh=mesh, in_specs=in_specs, out_specs=out_specs, check_vma=False
    )
```

```python
import functools

import jax
import jax.numpy as jnp
from jax import lax
from jax.experimental import pallas as pl
from jax.experimental.pallas import tpu as pltpu
from jax.sharding import PartitionSpec as P

LOWER = 0.3
UPPER = 2.0
OMEGA = 0.6
THETA = 0.5 * (UPPER + LOWER)
DELTA = 0.5 * (UPPER - LOWER)
RATIO = THETA / DELTA
RHO_A = 1.0 / RATIO
RHO_B = 1.0 / (2.0 * RATIO - RHO_A)
ALPHA = RHO_B * RHO_A
BETA = 2.0 * RHO_B / DELTA

NY, NX = 32, 128
DEPTH = 4
BELOW = 5
PLANES = 15
CELLS = 16
RX = 2000
RROWS = 16
IDX = 2 * RROWS
GROUPS = 16
UPWARD = ((14, 16, 8, 0, 0), (15, 16, 6, 2, 1), (15, 16, 8, 4, 2), (15, 17, 8, 0, 0))
DOWNWARD = ((16, 15, 6, 10, 0), (16, 15, 8, 12, 1), (17, 15, 6, 14, 2), (16, 14, 6, 14, 0))
CROSSING = ((14, 16), (15, 16), (15, 17))
NZ = 128
MESH = pl.DeviceIdType.MESH
F32 = jnp.float32
ONE, TWO, THREE = 1.0 / 16.0, 1.0 / 24.0, 1.0 / 48.0


def lanes():
    return lax.broadcasted_iota(jnp.int32, (NY, NX), 1)


def rows():
    return lax.broadcasted_iota(jnp.int32, (NY, NX), 0)


def next_x(v):
    return jnp.where(lanes() < NX - 1, pltpu.roll(v, NX - 1, 1), 0.0)


def prev_x(v):
    return jnp.where(lanes() > 0, pltpu.roll(v, 1, 1), 0.0)


def next_y(v):
    return jnp.where(rows() < NY - 1, pltpu.roll(v, NY - 1, 0), 0.0)


def prev_y(v):
    return jnp.where(rows() > 0, pltpu.roll(v, 1, 0), 0.0)


def prev2_x(v):
    return jnp.where(lanes() > 1, pltpu.roll(v, 2, 1), 0.0)


def prev2_y(v):
    return jnp.where(rows() > 1, pltpu.roll(v, 2, 0), 0.0)


def forward(v):
    moved = next_x(v)
    sx, dx = v + moved, v - moved
    ms, md = next_y(sx), next_y(dx)
    return sx + ms, sx - ms, dx + md, dx - md


def cell_terms(low, high):
    ss, ds, sd, dd = low
    ss2, ds2, sd2, dd2 = high
    return (ss - ss2, ds + ds2, ds - ds2, sd + sd2, sd - sd2, dd + dd2, dd - dd2)


def scatter_cell(low, high, c1, c2, c3):
    zss, sds, zds, ssd, zsd, sdd, zdd = cell_terms(low, high)
    zss = zss * c1
    sds, zds = sds * c1, zds * c2
    ssd, zsd = ssd * c1, zsd * c2
    sdd, zdd = sdd * c2, zdd * c3
    lower = (zss, sds + zds, ssd + zsd, sdd + zdd)
    upper = (-zss, sds - zds, ssd - zsd, sdd - zdd)
    return lower, upper


def backward(parts):
    ss, ds, sd, dd = parts
    os = (ss + ds) + prev_y(ss - ds)
    od = (sd + dd) + prev_y(sd - dd)
    return (os + od) + prev_x(os - od)


def apply_planes(v_ref, coef, first, last, sink):
    low = forward(v_ref[first - 1])
    mid = forward(v_ref[first])
    _, upper = scatter_cell(low, mid, coef[0, first - 1], coef[1, first - 1], coef[2, first - 1])

    def body(p, carry):
        here, above = carry[:4], carry[4:]
        ahead = forward(v_ref[p + 1])
        lower, upper = scatter_cell(here, ahead, coef[0, p], coef[1, p], coef[2, p])
        sink(p, backward([a + b for a, b in zip(lower, above)]))
        return (*ahead, *upper)

    lax.fori_loop(first, last + 1, body, (*mid, *upper), unroll=True)


def read_pairs(pairs, index, place_row, lane_row, slab):
    index[...] = jnp.full((IDX, NX), 1 << 24, jnp.int32)
    for j in range(RROWS):
        width = min(NX, RX - j * NX)
        for at, end in ((j, 0), (RROWS + j, 1)):
            index[at : at + 1, 0:width] = pairs[end : end + 1, pl.ds(j * NX, width)]
    lane = jnp.bitwise_and(index[...], NX - 1).astype(F32)
    place = (jnp.right_shift(index[...], 7) - (slab * DEPTH - BELOW) * NY).astype(F32)
    for j in range(IDX):
        place_row[j] = place[j : j + 1, :]
        lane_row[j] = lane[j : j + 1, :]


def read_target(obs, target, src):
    target[...] = jnp.zeros((RROWS, NX), F32)
    for j in range(RROWS):
        width = min(NX, RX - j * NX)
        mine = lax.broadcasted_iota(jnp.int32, (GROUPS, width), 0) == src
        target[j : j + 1, 0:width] = jnp.sum(
            jnp.where(mine, obs[:, pl.ds(j * NX, width)], 0.0), axis=0, keepdims=True
        )


def gather(fext, index, part, slab):
    lane = jnp.bitwise_and(index[...], NX - 1)
    line = jnp.right_shift(index[...], 7) - slab * (DEPTH * NY)

    def pick(block, acc):
        values = fext[block // 4, pl.ds((block % 4) * 8, 8), :]
        for k in range(8):
            spread = jnp.broadcast_to(values[k : k + 1, :], (IDX, NX))
            found = jnp.take_along_axis(spread, lane, axis=1, mode="promise_in_bounds")
            acc = jnp.where(line == block * 8 + k, found, acc)
        return acc

    picked = lax.fori_loop(0, DEPTH * NY // 8, pick, jnp.zeros((IDX, NX), F32), unroll=True)
    part[...] = picked[:RROWS] - picked[RROWS:]


def one_hots(place_row, lane_row, row_hot, lane_hot):
    def hot(j, carry):
        columns = pl.ds(pl.multiple_of(j * NX, NX), NX)
        for at, out, size in ((place_row, row_hot, PLANES * NY), (lane_row, lane_hot, NX)):
            spread = jnp.broadcast_to(at[j], (size, NX))
            line_id = lax.broadcasted_iota(jnp.int32, (size, NX), 0).astype(F32)
            out[:, columns] = jnp.where(spread == line_id, 1.0, 0.0).astype(jnp.bfloat16)
        return carry

    lax.fori_loop(0, IDX, hot, 0)


def inside(plane, slab):
    z = slab * DEPTH + plane
    return jnp.logical_and(z >= 0, z < NZ)


def conductivity_terms(cext, coef, diag, invd, cinv, slab):
    def masked_cells(e):
        return jnp.where(inside(e - 6, slab), cext[e], 0.0)

    def around(cells):
        along = cells + prev_x(cells)
        return along + prev_y(along)

    def diagonals(p, below):
        cells = masked_cells(p + 1)
        coef[0, p] = cells * ONE
        coef[1, p] = cells * TWO
        coef[2, p] = cells * THREE
        boxed = around(cells)
        value = (boxed + below) * (1.0 / 3.0)
        keep = inside(p - BELOW, slab)
        diag[p] = jnp.where(keep, value, 0.0)
        invd[p] = jnp.where(keep, 1.0 / jnp.where(keep, value, 1.0), 0.0)
        return boxed

    lax.fori_loop(0, PLANES, diagonals, around(masked_cells(0)), unroll=5)

    even = jnp.logical_and(lanes() % 2 == 0, rows() % 2 == 0)

    def coarse_box(j):
        pair = masked_cells(2 * j + 2) + masked_cells(2 * j + 3)
        pair = pair + next_y(pair)
        pair = jnp.where(even, pair + next_x(pair), 0.0)
        pair = pair + prev2_x(pair)
        return pair + prev2_y(pair)

    def coarse(j, below):
        boxed = coarse_box(j)
        value = (boxed + below) * (0.125 * 2.0 / 3.0)
        keep = jnp.logical_and(even, inside(2 * (j - 2), slab))
        cinv[j - 1] = jnp.where(keep, OMEGA / jnp.where(keep, value, 1.0), 0.0)
        return boxed

    lax.fori_loop(1, 6, coarse, coarse_box(0), unroll=True)


def field_terms(fext, hu, slab, start, stop):
    def terms(p, low):
        high = forward(jnp.where(inside(p + 1, slab), fext[p + 1], 0.0))
        scales = (-ONE, -ONE, -TWO, -ONE, -TWO, -TWO, -THREE)
        for k, (term, scale) in enumerate(zip(cell_terms(low, high), scales)):
            hu[p, k] = term * scale
        return high

    lax.fori_loop(start, stop, terms, forward(fext[start]), unroll=True)


def scatter(res_row, row_hot, lane_hot, invd, resid):
    high_parts, low_parts = [], []
    for j in range(IDX):
        value = jnp.broadcast_to(res_row[j], (16, NX))
        high = value.astype(jnp.bfloat16)
        low = (value - high.astype(F32)).astype(jnp.bfloat16)
        hot = lane_hot[:, j * NX : (j + 1) * NX].reshape(NX // 16, 16, NX)
        high_parts.append((hot * high[None]).reshape(NX, NX))
        low_parts.append((hot * low[None]).reshape(NX, NX))
    by_lane = jnp.concatenate(
        [jnp.concatenate(high_parts, axis=1), jnp.concatenate(low_parts, axis=1)], axis=0
    )
    both = lax.dot_general(
        row_hot[...], by_lane, (((1,), (1,)), ((), ())), preferred_element_type=F32
    )
    resid[...] = (both[:, :NX] + both[:, NX:]).reshape(PLANES, NY, NX) * invd[...]


def solve(coef, diag, invd, cinv, resid, direct, work, pe, lam):
    def first_step(p, applied):
        r = resid[p]
        r1 = r - (applied * (1.0 / THETA)) * invd[p]
        d2 = (ALPHA / THETA) * r + BETA * r1
        resid[p] = r1
        direct[p] = d2
        lam[p] = r * (1.0 / THETA) + d2

    apply_planes(resid, coef, 1, 13, first_step)

    def second_step(p, applied):
        r2 = resid[p] - applied * invd[p]
        resid[p] = r2
        work[p] = diag[p] * r2

    apply_planes(direct, coef, 2, 12, second_step)

    def correct(j):
        p = 2 * j + 3
        c = work[p] + 0.5 * (work[p - 1] + work[p + 1])
        c = c + 0.5 * (prev_y(c) + next_y(c))
        c = (c + 0.5 * (prev_x(c) + next_x(c))) * cinv[j]
        c = c + 0.5 * (prev_y(c) + next_y(c))
        return c + 0.5 * (prev_x(c) + next_x(c))

    def prolong(j, below):
        c = correct(j)
        pe[2 * j + 3] = c
        pe[2 * j + 2] = 0.5 * (below + c)
        return c

    first = correct(0)
    pe[3] = first
    lax.fori_loop(1, 5, prolong, first, unroll=True)

    def third_step(p, applied):
        r3 = resid[p] - applied * invd[p]
        resid[p] = r3
        lam[p] = lam[p] + pe[p] + r3 * (1.0 / THETA)

    apply_planes(pe, coef, 4, 10, third_step)

    def fourth_step(p, applied):
        r3 = resid[p]
        r4 = r3 - (applied * (1.0 / THETA)) * invd[p]
        lam[p] = lam[p] + (ALPHA / THETA) * r3 + BETA * r4

    apply_planes(resid, coef, 5, 9, fourth_step)


def cell_products(lam, hu, chunks):
    low = forward(lam[BELOW])
    for p in range(DEPTH):
        high = forward(lam[BELOW + p + 1])
        total = None
        for k, term in enumerate(cell_terms(low, high)):
            piece = term * hu[p, k]
            total = piece if total is None else total + piece
        low = high
        for z in range(8):
            for c in range(2):
                at = 4 * z + 2 * c
                chunks[c, z, 2 * p : 2 * p + 2, :] = total[at : at + 2, :]


def kernel(
    cond_hbm, field_hbm, pairs_hbm, obs_hbm,
    recv_src, recv_mis,
    cext, fext, pairs, obs, index, target,
    part, recv_xy, zsum, recv_z,
    place_row, lane_row, res_row, row_hot, lane_hot, coef, diag, invd, cinv, hu,
    resid, direct, work, lam, pe,
    mis, chunks,
    in_sem, send_sem, sum_sem, halo_sem, xy_sem, z_sem, mis_sem, src_sem,
    cross_sem, swap_sem, go, ready,
):
    src = lax.axis_index("src")
    slab = lax.axis_index("slab")
    zl, core = src // 2, src % 2
    zh, px, py = slab // 16, (slab // 4) % 4, slab % 4
    here = px * 4 + py
    hops = (0, 1, 2, 1)
    offsets = sorted(((i, j) for i in range(4) for j in range(4)), key=lambda o: -hops[o[0]] - hops[o[1]])
    plane_peers = [(src, zh * 16 + ((px + i) % 4) * 4 + (py + j) % 4) for i, j in offsets[:-1]]
    sibling = (zl * 2 + 1 - core, slab)
    edge = jnp.logical_or(zl == 0, zl == 7)
    beyond = (7 - zl) * 2 + core

    barrier = pltpu.get_barrier_semaphore()

    def signal(sem, peer):
        pl.semaphore_signal(sem, inc=1, device_id=peer, device_id_type=MESH)

    for peer in reversed(plane_peers):
        signal(barrier, peer)

    @pl.when(core == 0)
    def _():
        signal(barrier, sibling)

    loads = [
        pltpu.make_async_copy(pairs_hbm, pairs, in_sem.at[0]),
        pltpu.make_async_copy(field_hbm, fext.at[pl.ds(0, DEPTH)], in_sem.at[1]),
        pltpu.make_async_copy(cond_hbm, cext.at[pl.ds(6, DEPTH)], in_sem.at[2]),
        pltpu.make_async_copy(obs_hbm, obs, in_sem.at[3]),
    ]
    for load in loads:
        load.start()

    signal(barrier, (zl * 2, (1 - zh) * 16 + here))
    for k in range(1, 8):
        signal(barrier, (((zl + k) % 8) * 2, slab))
    for low, high in CROSSING:
        for at, to in ((low, high), (high, low)):

            @pl.when(jnp.logical_and(edge, slab == at))
            def _():
                signal(barrier, ((7 - zl) * 2, to))

    @pl.when(slab == 15)
    def _():
        signal(barrier, (zl * 2, 16))

    loads[0].wait()
    read_pairs(pairs, index, place_row, lane_row, slab)
    loads[1].wait()
    gather(fext, index, part, slab)

    @pl.when(core == 1)
    def _():
        recv_xy[1, here] = part[...]

    sent = []

    def send(source, dest, arrival, peer, when=None):
        copy = pltpu.make_async_remote_copy(
            src_ref=source, dst_ref=dest, send_sem=send_sem, recv_sem=arrival,
            device_id=peer, device_id_type=MESH,
        )
        sent.append((copy.wait_send, when))
        if when is None:
            copy.start()
        else:
            pl.when(when)(copy.start)

    def arrived(buffer, arrival):
        pltpu.make_async_copy(buffer, buffer, arrival).wait()

    @pl.when(core == 1)
    def _():
        pl.semaphore_wait(barrier, 15 + 1)
        signal(go, sibling)

    @pl.when(core == 0)
    def _():
        pl.semaphore_wait(go, 1)

    for _, peer in plane_peers:
        send(part, recv_xy.at[core, here], xy_sem.at[core], (zl * 2 + 1, peer))
    send(part, recv_xy.at[0, here], xy_sem.at[0], sibling, core == 0)

    crossed = sum((slab == t).astype(jnp.int32) for pair in CROSSING for t in pair)
    far = 1 + 7 + crossed * edge.astype(jnp.int32) + (slab == 16).astype(jnp.int32)

    @pl.when(core == 0)
    def _():
        pl.semaphore_wait(barrier, 15 + 2 * far)
        signal(ready, sibling)

    @pl.when(core == 1)
    def _():
        pl.semaphore_wait(ready, 1)

    loads[2].wait()

    def cross(blocks):
        for at, to, take, put, k in blocks:
            send(
                cext.at[take + core], cext.at[put + core], cross_sem.at[k], (beyond, to),
                jnp.logical_and(edge, slab == at),
            )

    own = cext.at[pl.ds(6, DEPTH)]
    own_low, own_high = cext.at[pl.ds(6, 2)], cext.at[pl.ds(8, 2)]
    from_1, from_2 = cext.at[pl.ds(2, DEPTH)], cext.at[pl.ds(0, 2)]
    to_1, to_2 = cext.at[pl.ds(10, DEPTH)], cext.at[pl.ds(14, 2)]
    up_1, up_2 = (src, (slab + 1) % 32), (src, (slab + 2) % 32)
    down_1, down_2 = (src, (slab + 31) % 32), (src, (slab + 30) % 32)

    def among(*slabs):
        found = slab == slabs[0]
        for other in slabs[1:]:
            found = jnp.logical_or(found, slab == other)
        return found

    sends_up_1, sends_up_2 = (jnp.logical_not(among(*t)) for t in ((15, 31), (14, 15, 30, 31)))
    sends_down_1, sends_down_2 = (jnp.logical_not(among(*t)) for t in ((0, 16), (0, 1, 16, 17)))
    top = fext.at[pl.ds(DEPTH, 1)]
    bottom = fext.at[pl.ds(0, 1)]
    cross(DOWNWARD + UPWARD)
    send(own, to_1, halo_sem.at[1], down_1, sends_down_1)
    send(bottom, top, halo_sem.at[4], down_1, sends_down_1)
    send(own_low, to_2, halo_sem.at[3], down_2, sends_down_2)
    send(own, from_1, halo_sem.at[0], up_1, sends_up_1)
    send(own_high, from_2, halo_sem.at[2], up_2, sends_up_2)

    loads[3].wait()
    read_target(obs, target, src)

    @pl.when(among(14, 15))
    def _():
        one_hots(place_row, lane_row, row_hot, lane_hot)

    def add_plane(k):
        return lax.fori_loop(1, 16, lambda i, acc: acc + recv_xy[k, i], recv_xy[k, 0], unroll=True)

    def send_sum(source, to, slot):
        return pltpu.make_async_remote_copy(
            src_ref=source, dst_ref=to[0], send_sem=sum_sem.at[slot], recv_sem=to[1],
            device_id=to[2], device_id_type=MESH,
        )

    other_half = (1 - zh) * 16 + here
    sums = [
        send_sum(zsum.at[1], (recv_z, z_sem.at[1], (zl * 2, other_half)), 0),
        send_sum(zsum.at[1], (zsum.at[0], z_sem.at[0], sibling), 1),
        send_sum(zsum.at[0], (recv_z, z_sem.at[1], (zl * 2 + 1, other_half)), 2),
    ]

    @pl.when(core == 1)
    def _():
        arrived(recv_xy.at[0], xy_sem.at[0])
        zsum[1] = add_plane(0)
        sums[0].start()
        sums[1].start()
        arrived(recv_xy.at[1, pl.ds(0, 15)], xy_sem.at[1])
        zsum[0] = add_plane(1)
        sums[2].start()

    send(bottom, top, halo_sem.at[4], down_1, slab == 16)

    for _, to, _, put, k in UPWARD + DOWNWARD:

        @pl.when(slab == to)
        def _():
            arrived(cext.at[put + core], cross_sem.at[k])

    for _, to, _, put, k in UPWARD + DOWNWARD:
        block = cext.at[put + core]
        send(block, block, swap_sem.at[k], sibling, slab == to)
    for step in (4, 3, 2, 1):
        z = jnp.where(zl == 0, step, 7 - step)
        serves = edge if step < 3 else zl == 7
        for _, to, _, put, k in UPWARD + DOWNWARD:
            block = cext.at[put + core]
            send(block, block, cross_sem.at[k], (z * 2 + core, slab), jnp.logical_and(serves, slab == to))
    for _, to, _, put, k in UPWARD + DOWNWARD:

        @pl.when(slab == to)
        def _():
            arrived(cext.at[put + 1 - core], swap_sem.at[k])

    @pl.when(jnp.logical_not(among(14, 15)))
    def _():
        one_hots(place_row, lane_row, row_hot, lane_hot)

    for buffer, arrival, when in (
        (from_1, halo_sem.at[0], jnp.logical_not(among(0, 16))),
        (to_1, halo_sem.at[1], jnp.logical_not(among(15, 31))),
        (from_2, halo_sem.at[2], jnp.logical_not(among(0, 1, 16, 17))),
        (to_2, halo_sem.at[3], jnp.logical_not(among(14, 15, 30, 31))),
    ):

        @pl.when(when)
        def _():
            arrived(buffer, arrival)

    conductivity_terms(cext, coef, diag, invd, cinv, slab)
    field_terms(fext, hu, slab, 0, DEPTH - 1)

    @pl.when(core == 0)
    def _():
        arrived(zsum.at[0], z_sem.at[0])

    arrived(recv_z, z_sem.at[1])
    res = (zsum[0] + recv_z[...]) - target[...]
    for j in range(RROWS):
        res_row[j] = res[j : j + 1, :]
        res_row[RROWS + j] = -res[j : j + 1, :]
    scatter(res_row, row_hot, lane_hot, invd, resid)

    half = jnp.sum(jnp.sum(0.5 * res * res, axis=0, keepdims=True), axis=1, keepdims=True)
    mis[...] = jnp.broadcast_to(half, (1, NX))
    recv_mis[src] = mis[...]

    solve(coef, diag, invd, cinv, resid, direct, work, pe, lam)

    @pl.when(slab < 31)
    def _():
        arrived(top, halo_sem.at[4])

    field_terms(fext, hu, slab, DEPTH - 1, DEPTH)
    cell_products(lam, hu, chunks)

    for z in range(8):
        for c in (1, 0):
            other = src != z * 2 + c
            send(chunks.at[c, z], recv_src.at[src], src_sem, (z * 2 + c, slab), other)
            send(mis, recv_mis.at[src], mis_sem, (z * 2 + c, slab), other)
    recv_src[src] = chunks[core, zl]
    arrived(recv_mis.at[pl.ds(0, 15)], mis_sem)
    arrived(recv_src.at[pl.ds(0, 15)], src_sem)

    @pl.when(core == 1)
    def _():
        for copy in sums:
            copy.wait_send()

    for wait, when in sent:
        if when is None:
            wait()
        else:
            pl.when(when)(wait)


def finish(recv_src, recv_mis, grad_ref, misfit_ref):
    total, misfit = recv_src[0], recv_mis[0]
    for k in range(1, GROUPS):
        total, misfit = total + recv_src[k], misfit + recv_mis[k]
    grad_ref[...] = total
    misfit_ref[...] = misfit * (1.0 / (GROUPS * RX))


def on_device(conductivity, forward_fields, receiver_pairs, observed):
    field = forward_fields.reshape(DEPTH, NY, NX)
    pairs = jnp.transpose(receiver_pairs[0])
    conductivity, field, pairs, observed = (
        pltpu.with_memory_space_constraint(a, pltpu.HBM) for a in (conductivity, field, pairs, observed)
    )
    plane = (NY, NX)
    any_spec = pl.BlockSpec(memory_space=pltpu.HBM)
    vmem = pl.BlockSpec(memory_space=pltpu.VMEM)
    dma, regular = pltpu.SemaphoreType.DMA, pltpu.SemaphoreType.REGULAR
    received = pl.pallas_call(
        kernel,
        name="adjoint_gradient",
        out_shape=(
            jax.ShapeDtypeStruct((GROUPS, 8, NX), F32),
            jax.ShapeDtypeStruct((GROUPS, 1, NX), F32),
        ),
        in_specs=[any_spec] * 4,
        out_specs=(vmem, vmem),
        scratch_shapes=[
            pltpu.VMEM((CELLS, *plane), F32),
            pltpu.VMEM((DEPTH + 1, *plane), F32),
            pltpu.VMEM((2, RX), jnp.int32),
            pltpu.VMEM((GROUPS, RX), F32),
            pltpu.VMEM((IDX, NX), jnp.int32),
            pltpu.VMEM((RROWS, NX), F32),
            pltpu.VMEM((RROWS, NX), F32),
            pltpu.VMEM((2, 16, RROWS, NX), F32),
            pltpu.VMEM((2, RROWS, NX), F32),
            pltpu.VMEM((RROWS, NX), F32),
            pltpu.VMEM((IDX, 1, NX), F32),
            pltpu.VMEM((IDX, 1, NX), F32),
            pltpu.VMEM((IDX, 1, NX), F32),
            pltpu.VMEM((PLANES * NY, IDX * NX), jnp.bfloat16),
            pltpu.VMEM((NX, IDX * NX), jnp.bfloat16),
            pltpu.VMEM((3, PLANES, *plane), F32),
            pltpu.VMEM((PLANES, *plane), F32),
            pltpu.VMEM((PLANES, *plane), F32),
            pltpu.VMEM((5, *plane), F32),
            pltpu.VMEM((DEPTH, 7, *plane), F32),
            pltpu.VMEM((PLANES, *plane), F32),
            pltpu.VMEM((PLANES, *plane), F32),
            pltpu.VMEM((PLANES, *plane), F32),
            pltpu.VMEM((PLANES, *plane), F32),
            pltpu.VMEM((PLANES, *plane), F32),
            pltpu.VMEM((1, NX), F32),
            pltpu.VMEM((2, 8, 8, NX), F32),
            dma((4,)), dma, dma((3,)), dma((5,)), dma((2,)), dma((2,)), dma, dma,
            dma((3,)), dma((3,)), regular, regular,
        ],
        compiler_params=pltpu.CompilerParams(
            collective_id=0, has_side_effects=True, vmem_limit_bytes=32 * 1024 * 1024
        ),
    )(conductivity, field, pairs, observed)
    grad, misfit = pl.pallas_call(
        finish,
        name="add_groups",
        out_shape=(jax.ShapeDtypeStruct((8, NX), F32), jax.ShapeDtypeStruct((1, NX), F32)),
        in_specs=[vmem] * 2,
        out_specs=(vmem, vmem),
        compiler_params=pltpu.CompilerParams(vmem_limit_bytes=1024 * 1024),
    )(*received)
    return grad.reshape(DEPTH, 2, NX), misfit[0, 0]


def solution(mesh):
    in_specs = (P("slab", None, None), P("src", "slab", None, None), P("src", None, None), P())
    out_specs = (P("slab", "src", None), P())
    return jax.shard_map(
        on_device, mesh=mesh, in_specs=in_specs, out_specs=out_specs, check_vma=False
    )
```

```python
import functools

import jax
import jax.numpy as jnp
from jax import lax
from jax.experimental import pallas as pl
from jax.experimental.pallas import tpu as pltpu
from jax.sharding import PartitionSpec as P

LOWER = 0.3
UPPER = 2.0
OMEGA = 0.6
THETA = 0.5 * (UPPER + LOWER)
DELTA = 0.5 * (UPPER - LOWER)
RATIO = THETA / DELTA
RHO_A = 1.0 / RATIO
RHO_B = 1.0 / (2.0 * RATIO - RHO_A)
ALPHA = RHO_B * RHO_A
BETA = 2.0 * RHO_B / DELTA

NY, NX = 32, 128
DEPTH = 4
BELOW = 5
PLANES = 15
CELLS = 16
RX = 2000
RROWS = 16
IDX = 2 * RROWS
GROUPS = 16
UPWARD = ((14, 16, 8, 0, 0), (15, 16, 6, 2, 1), (15, 16, 8, 4, 2), (15, 17, 8, 0, 0))
DOWNWARD = ((16, 15, 6, 10, 0), (16, 15, 8, 12, 1), (17, 15, 6, 14, 2), (16, 14, 6, 14, 0))
CROSSING = ((14, 16), (15, 16), (15, 17))
NZ = 128
MESH = pl.DeviceIdType.MESH
F32 = jnp.float32
ONE, TWO, THREE = 1.0 / 16.0, 1.0 / 24.0, 1.0 / 48.0


def lanes():
    return lax.broadcasted_iota(jnp.int32, (NY, NX), 1)


def rows():
    return lax.broadcasted_iota(jnp.int32, (NY, NX), 0)


def next_x(v):
    return jnp.where(lanes() < NX - 1, pltpu.roll(v, NX - 1, 1), 0.0)


def prev_x(v):
    return jnp.where(lanes() > 0, pltpu.roll(v, 1, 1), 0.0)


def next_y(v):
    return jnp.where(rows() < NY - 1, pltpu.roll(v, NY - 1, 0), 0.0)


def prev_y(v):
    return jnp.where(rows() > 0, pltpu.roll(v, 1, 0), 0.0)


def prev2_x(v):
    return jnp.where(lanes() > 1, pltpu.roll(v, 2, 1), 0.0)


def prev2_y(v):
    return jnp.where(rows() > 1, pltpu.roll(v, 2, 0), 0.0)


def forward(v):
    moved = next_x(v)
    sx, dx = v + moved, v - moved
    ms, md = next_y(sx), next_y(dx)
    return sx + ms, sx - ms, dx + md, dx - md


def cell_terms(low, high):
    ss, ds, sd, dd = low
    ss2, ds2, sd2, dd2 = high
    return (ss - ss2, ds + ds2, ds - ds2, sd + sd2, sd - sd2, dd + dd2, dd - dd2)


def scatter_cell(low, high, c1, c2, c3):
    zss, sds, zds, ssd, zsd, sdd, zdd = cell_terms(low, high)
    zss = zss * c1
    sds, zds = sds * c1, zds * c2
    ssd, zsd = ssd * c1, zsd * c2
    sdd, zdd = sdd * c2, zdd * c3
    lower = (zss, sds + zds, ssd + zsd, sdd + zdd)
    upper = (-zss, sds - zds, ssd - zsd, sdd - zdd)
    return lower, upper


def backward(parts):
    ss, ds, sd, dd = parts
    os = (ss + ds) + prev_y(ss - ds)
    od = (sd + dd) + prev_y(sd - dd)
    return (os + od) + prev_x(os - od)


def apply_planes(v_ref, coef, first, last, sink):
    low = forward(v_ref[first - 1])
    mid = forward(v_ref[first])
    _, upper = scatter_cell(low, mid, coef[0, first - 1], coef[1, first - 1], coef[2, first - 1])

    def body(p, carry):
        here, above = carry[:4], carry[4:]
        ahead = forward(v_ref[p + 1])
        lower, upper = scatter_cell(here, ahead, coef[0, p], coef[1, p], coef[2, p])
        sink(p, backward([a + b for a, b in zip(lower, above)]))
        return (*ahead, *upper)

    lax.fori_loop(first, last + 1, body, (*mid, *upper), unroll=True)


def read_pairs(pairs, index, place_row, lane_row, slab):
    index[...] = jnp.full((IDX, NX), 1 << 24, jnp.int32)
    for j in range(RROWS):
        width = min(NX, RX - j * NX)
        for at, end in ((j, 0), (RROWS + j, 1)):
            index[at : at + 1, 0:width] = pairs[end : end + 1, pl.ds(j * NX, width)]
    lane = jnp.bitwise_and(index[...], NX - 1).astype(F32)
    place = (jnp.right_shift(index[...], 7) - (slab * DEPTH - BELOW) * NY).astype(F32)
    for j in range(IDX):
        place_row[j] = place[j : j + 1, :]
        lane_row[j] = lane[j : j + 1, :]


def read_target(obs, target, src):
    target[...] = jnp.zeros((RROWS, NX), F32)
    for j in range(RROWS):
        width = min(NX, RX - j * NX)
        mine = lax.broadcasted_iota(jnp.int32, (GROUPS, width), 0) == src
        target[j : j + 1, 0:width] = jnp.sum(
            jnp.where(mine, obs[:, pl.ds(j * NX, width)], 0.0), axis=0, keepdims=True
        )


def gather(fext, index, part, slab):
    lane = jnp.bitwise_and(index[...], NX - 1)
    line = jnp.right_shift(index[...], 7) - slab * (DEPTH * NY)

    def pick(block, acc):
        values = fext[block // 4, pl.ds((block % 4) * 8, 8), :]
        for k in range(8):
            spread = jnp.broadcast_to(values[k : k + 1, :], (IDX, NX))
            found = jnp.take_along_axis(spread, lane, axis=1, mode="promise_in_bounds")
            acc = jnp.where(line == block * 8 + k, found, acc)
        return acc

    picked = lax.fori_loop(0, DEPTH * NY // 8, pick, jnp.zeros((IDX, NX), F32), unroll=True)
    part[...] = picked[:RROWS] - picked[RROWS:]


def one_hots(place_row, lane_row, row_hot, lane_hot):
    def hot(j, carry):
        columns = pl.ds(pl.multiple_of(j * NX, NX), NX)
        for at, out, size in ((place_row, row_hot, PLANES * NY), (lane_row, lane_hot, NX)):
            spread = jnp.broadcast_to(at[j], (size, NX))
            line_id = lax.broadcasted_iota(jnp.int32, (size, NX), 0).astype(F32)
            out[:, columns] = jnp.where(spread == line_id, 1.0, 0.0).astype(jnp.bfloat16)
        return carry

    lax.fori_loop(0, IDX, hot, 0)


def inside(plane, slab):
    z = slab * DEPTH + plane
    return jnp.logical_and(z >= 0, z < NZ)


def conductivity_terms(cext, coef, diag, invd, cinv, slab):
    def masked_cells(e):
        return jnp.where(inside(e - 6, slab), cext[e], 0.0)

    def around(cells):
        along = cells + prev_x(cells)
        return along + prev_y(along)

    def diagonals(p, below):
        cells = masked_cells(p + 1)
        coef[0, p] = cells * ONE
        coef[1, p] = cells * TWO
        coef[2, p] = cells * THREE
        boxed = around(cells)
        value = (boxed + below) * (1.0 / 3.0)
        keep = inside(p - BELOW, slab)
        diag[p] = jnp.where(keep, value, 0.0)
        invd[p] = jnp.where(keep, 1.0 / jnp.where(keep, value, 1.0), 0.0)
        return boxed

    lax.fori_loop(0, PLANES, diagonals, around(masked_cells(0)), unroll=5)

    even = jnp.logical_and(lanes() % 2 == 0, rows() % 2 == 0)

    def coarse_box(j):
        pair = masked_cells(2 * j + 2) + masked_cells(2 * j + 3)
        pair = pair + next_y(pair)
        pair = jnp.where(even, pair + next_x(pair), 0.0)
        pair = pair + prev2_x(pair)
        return pair + prev2_y(pair)

    def coarse(j, below):
        boxed = coarse_box(j)
        value = (boxed + below) * (0.125 * 2.0 / 3.0)
        keep = jnp.logical_and(even, inside(2 * (j - 2), slab))
        cinv[j - 1] = jnp.where(keep, OMEGA / jnp.where(keep, value, 1.0), 0.0)
        return boxed

    lax.fori_loop(1, 6, coarse, coarse_box(0), unroll=True)


def field_terms(fext, hu, slab, start, stop):
    def terms(p, low):
        high = forward(jnp.where(inside(p + 1, slab), fext[p + 1], 0.0))
        scales = (-ONE, -ONE, -TWO, -ONE, -TWO, -TWO, -THREE)
        for k, (term, scale) in enumerate(zip(cell_terms(low, high), scales)):
            hu[p, k] = term * scale
        return high

    lax.fori_loop(start, stop, terms, forward(fext[start]), unroll=True)


def scatter(res_row, row_hot, lane_hot, invd, resid):
    high_parts, low_parts = [], []
    for j in range(IDX):
        value = jnp.broadcast_to(res_row[j], (16, NX))
        high = value.astype(jnp.bfloat16)
        low = (value - high.astype(F32)).astype(jnp.bfloat16)
        hot = lane_hot[:, j * NX : (j + 1) * NX].reshape(NX // 16, 16, NX)
        high_parts.append((hot * high[None]).reshape(NX, NX))
        low_parts.append((hot * low[None]).reshape(NX, NX))
    by_lane = jnp.concatenate(
        [jnp.concatenate(high_parts, axis=1), jnp.concatenate(low_parts, axis=1)], axis=0
    )
    both = lax.dot_general(
        row_hot[...], by_lane, (((1,), (1,)), ((), ())), preferred_element_type=F32
    )
    resid[...] = (both[:, :NX] + both[:, NX:]).reshape(PLANES, NY, NX) * invd[...]


def solve(coef, diag, invd, cinv, resid, direct, work, pe, lam):
    def first_step(p, applied):
        r = resid[p]
        r1 = r - (applied * (1.0 / THETA)) * invd[p]
        d2 = (ALPHA / THETA) * r + BETA * r1
        resid[p] = r1
        direct[p] = d2
        lam[p] = r * (1.0 / THETA) + d2

    apply_planes(resid, coef, 1, 13, first_step)

    def second_step(p, applied):
        r2 = resid[p] - applied * invd[p]
        resid[p] = r2
        work[p] = diag[p] * r2

    apply_planes(direct, coef, 2, 12, second_step)

    def correct(j):
        p = 2 * j + 3
        c = work[p] + 0.5 * (work[p - 1] + work[p + 1])
        c = c + 0.5 * (prev_y(c) + next_y(c))
        c = (c + 0.5 * (prev_x(c) + next_x(c))) * cinv[j]
        c = c + 0.5 * (prev_y(c) + next_y(c))
        return c + 0.5 * (prev_x(c) + next_x(c))

    def prolong(j, below):
        c = correct(j)
        pe[2 * j + 3] = c
        pe[2 * j + 2] = 0.5 * (below + c)
        return c

    first = correct(0)
    pe[3] = first
    lax.fori_loop(1, 5, prolong, first, unroll=True)

    def third_step(p, applied):
        r3 = resid[p] - applied * invd[p]
        resid[p] = r3
        lam[p] = lam[p] + pe[p] + r3 * (1.0 / THETA)

    apply_planes(pe, coef, 4, 10, third_step)

    def fourth_step(p, applied):
        r3 = resid[p]
        r4 = r3 - (applied * (1.0 / THETA)) * invd[p]
        lam[p] = lam[p] + (ALPHA / THETA) * r3 + BETA * r4

    apply_planes(resid, coef, 5, 9, fourth_step)


def cell_products(lam, hu, chunks):
    low = forward(lam[BELOW])
    for p in range(DEPTH):
        high = forward(lam[BELOW + p + 1])
        total = None
        for k, term in enumerate(cell_terms(low, high)):
            piece = term * hu[p, k]
            total = piece if total is None else total + piece
        low = high
        for z in range(8):
            for c in range(2):
                at = 4 * z + 2 * c
                chunks[c, z, 2 * p : 2 * p + 2, :] = total[at : at + 2, :]


def kernel(
    cond_hbm, field_hbm, pairs_hbm, obs_hbm,
    recv_src, recv_mis,
    cext, fext, pairs, obs, index, target,
    part, recv_xy, zsum, recv_z,
    place_row, lane_row, res_row, row_hot, lane_hot, coef, diag, invd, cinv, hu,
    resid, direct, work, lam, pe,
    mis, chunks,
    in_sem, send_sem, sum_sem, halo_sem, xy_sem, z_sem, mis_sem, src_sem,
    cross_sem, swap_sem, go, ready,
):
    src = lax.axis_index("src")
    slab = lax.axis_index("slab")
    zl, core = src // 2, src % 2
    zh, px, py = slab // 16, (slab // 4) % 4, slab % 4
    here = px * 4 + py
    hops = (0, 1, 2, 1)
    offsets = sorted(((i, j) for i in range(4) for j in range(4)), key=lambda o: -hops[o[0]] - hops[o[1]])
    plane_peers = [(src, zh * 16 + ((px + i) % 4) * 4 + (py + j) % 4) for i, j in offsets[:-1]]
    sibling = (zl * 2 + 1 - core, slab)
    edge = jnp.logical_or(zl == 0, zl == 7)
    beyond = (7 - zl) * 2 + core

    barrier = pltpu.get_barrier_semaphore()

    def signal(sem, peer):
        pl.semaphore_signal(sem, inc=1, device_id=peer, device_id_type=MESH)

    for peer in reversed(plane_peers):
        signal(barrier, peer)

    @pl.when(core == 0)
    def _():
        signal(barrier, sibling)

    loads = [
        pltpu.make_async_copy(pairs_hbm, pairs, in_sem.at[0]),
        pltpu.make_async_copy(field_hbm, fext.at[pl.ds(0, DEPTH)], in_sem.at[1]),
        pltpu.make_async_copy(cond_hbm, cext.at[pl.ds(6, DEPTH)], in_sem.at[2]),
        pltpu.make_async_copy(obs_hbm, obs, in_sem.at[3]),
    ]
    for load in loads:
        load.start()

    signal(barrier, (zl * 2, (1 - zh) * 16 + here))
    for k in range(1, 8):
        signal(barrier, (((zl + k) % 8) * 2, slab))
    for low, high in CROSSING:
        for at, to in ((low, high), (high, low)):

            @pl.when(jnp.logical_and(edge, slab == at))
            def _():
                signal(barrier, ((7 - zl) * 2, to))

    @pl.when(slab == 15)
    def _():
        signal(barrier, (zl * 2, 16))

    loads[0].wait()
    read_pairs(pairs, index, place_row, lane_row, slab)
    loads[1].wait()
    gather(fext, index, part, slab)

    @pl.when(core == 1)
    def _():
        recv_xy[1, here] = part[...]

    sent = []

    def send(source, dest, arrival, peer, when=None):
        copy = pltpu.make_async_remote_copy(
            src_ref=source, dst_ref=dest, send_sem=send_sem, recv_sem=arrival,
            device_id=peer, device_id_type=MESH,
        )
        sent.append((copy.wait_send, when))
        if when is None:
            copy.start()
        else:
            pl.when(when)(copy.start)

    def arrived(buffer, arrival):
        pltpu.make_async_copy(buffer, buffer, arrival).wait()

    @pl.when(core == 1)
    def _():
        pl.semaphore_wait(barrier, 15 + 1)
        signal(go, sibling)

    @pl.when(core == 0)
    def _():
        pl.semaphore_wait(go, 1)

    for _, peer in plane_peers:
        send(part, recv_xy.at[core, here], xy_sem.at[core], (zl * 2 + 1, peer))
    send(part, recv_xy.at[0, here], xy_sem.at[0], sibling, core == 0)

    crossed = sum((slab == t).astype(jnp.int32) for pair in CROSSING for t in pair)
    far = 1 + 7 + crossed * edge.astype(jnp.int32) + (slab == 16).astype(jnp.int32)

    @pl.when(core == 0)
    def _():
        pl.semaphore_wait(barrier, 15 + 2 * far)
        signal(ready, sibling)

    @pl.when(core == 1)
    def _():
        pl.semaphore_wait(ready, 1)

    loads[2].wait()

    def cross(blocks):
        for at, to, take, put, k in blocks:
            send(
                cext.at[take + core], cext.at[put + core], cross_sem.at[k], (beyond, to),
                jnp.logical_and(edge, slab == at),
            )

    own = cext.at[pl.ds(6, DEPTH)]
    own_low, own_high = cext.at[pl.ds(6, 2)], cext.at[pl.ds(8, 2)]
    from_1, from_2 = cext.at[pl.ds(2, DEPTH)], cext.at[pl.ds(0, 2)]
    to_1, to_2 = cext.at[pl.ds(10, DEPTH)], cext.at[pl.ds(14, 2)]
    up_1, up_2 = (src, (slab + 1) % 32), (src, (slab + 2) % 32)
    down_1, down_2 = (src, (slab + 31) % 32), (src, (slab + 30) % 32)

    def among(*slabs):
        found = slab == slabs[0]
        for other in slabs[1:]:
            found = jnp.logical_or(found, slab == other)
        return found

    sends_up_1, sends_up_2 = (jnp.logical_not(among(*t)) for t in ((15, 31), (14, 15, 30, 31)))
    sends_down_1, sends_down_2 = (jnp.logical_not(among(*t)) for t in ((0, 16), (0, 1, 16, 17)))
    top = fext.at[pl.ds(DEPTH, 1)]
    bottom = fext.at[pl.ds(0, 1)]
    cross(DOWNWARD + UPWARD)
    send(own, to_1, halo_sem.at[1], down_1, sends_down_1)
    send(bottom, top, halo_sem.at[4], down_1, sends_down_1)
    send(own_low, to_2, halo_sem.at[3], down_2, sends_down_2)
    send(own, from_1, halo_sem.at[0], up_1, sends_up_1)
    send(own_high, from_2, halo_sem.at[2], up_2, sends_up_2)

    loads[3].wait()
    read_target(obs, target, src)

    @pl.when(among(14, 15))
    def _():
        one_hots(place_row, lane_row, row_hot, lane_hot)

    def add_plane(k):
        return lax.fori_loop(1, 16, lambda i, acc: acc + recv_xy[k, i], recv_xy[k, 0], unroll=True)

    def send_sum(source, to, slot):
        return pltpu.make_async_remote_copy(
            src_ref=source, dst_ref=to[0], send_sem=sum_sem.at[slot], recv_sem=to[1],
            device_id=to[2], device_id_type=MESH,
        )

    other_half = (1 - zh) * 16 + here
    sums = [
        send_sum(zsum.at[1], (recv_z, z_sem.at[1], (zl * 2, other_half)), 0),
        send_sum(zsum.at[1], (zsum.at[0], z_sem.at[0], sibling), 1),
        send_sum(zsum.at[0], (recv_z, z_sem.at[1], (zl * 2 + 1, other_half)), 2),
    ]

    @pl.when(core == 1)
    def _():
        arrived(recv_xy.at[0], xy_sem.at[0])
        zsum[1] = add_plane(0)
        sums[0].start()
        sums[1].start()
        arrived(recv_xy.at[1, pl.ds(0, 15)], xy_sem.at[1])
        zsum[0] = add_plane(1)
        sums[2].start()

    send(bottom, top, halo_sem.at[4], down_1, slab == 16)

    for _, to, _, put, k in UPWARD + DOWNWARD:

        @pl.when(slab == to)
        def _():
            arrived(cext.at[put + core], cross_sem.at[k])

    for _, to, _, put, k in UPWARD + DOWNWARD:
        block = cext.at[put + core]
        send(block, block, swap_sem.at[k], sibling, slab == to)
    for step in (4, 3, 2, 1):
        z = jnp.where(zl == 0, step, 7 - step)
        serves = edge if step < 3 else zl == 7
        for _, to, _, put, k in UPWARD + DOWNWARD:
            block = cext.at[put + core]
            send(block, block, cross_sem.at[k], (z * 2 + core, slab), jnp.logical_and(serves, slab == to))
    for _, to, _, put, k in UPWARD + DOWNWARD:

        @pl.when(slab == to)
        def _():
            arrived(cext.at[put + 1 - core], swap_sem.at[k])

    @pl.when(jnp.logical_not(among(14, 15)))
    def _():
        one_hots(place_row, lane_row, row_hot, lane_hot)

    for buffer, arrival, when in (
        (from_1, halo_sem.at[0], jnp.logical_not(among(0, 16))),
        (to_1, halo_sem.at[1], jnp.logical_not(among(15, 31))),
        (from_2, halo_sem.at[2], jnp.logical_not(among(0, 1, 16, 17))),
        (to_2, halo_sem.at[3], jnp.logical_not(among(14, 15, 30, 31))),
    ):

        @pl.when(when)
        def _():
            arrived(buffer, arrival)

    conductivity_terms(cext, coef, diag, invd, cinv, slab)
    field_terms(fext, hu, slab, 0, DEPTH - 1)

    @pl.when(jnp.logical_not(among(15, 31)))
    def _():
        arrived(top, halo_sem.at[4])

    @pl.when(slab != 15)
    def _():
        field_terms(fext, hu, slab, DEPTH - 1, DEPTH)


    @pl.when(core == 0)
    def _():
        arrived(zsum.at[0], z_sem.at[0])

    arrived(recv_z, z_sem.at[1])
    res = (zsum[0] + recv_z[...]) - target[...]
    for j in range(RROWS):
        res_row[j] = res[j : j + 1, :]
        res_row[RROWS + j] = -res[j : j + 1, :]
    scatter(res_row, row_hot, lane_hot, invd, resid)

    half = jnp.sum(jnp.sum(0.5 * res * res, axis=0, keepdims=True), axis=1, keepdims=True)
    mis[...] = jnp.broadcast_to(half, (1, NX))
    recv_mis[src] = mis[...]

    solve(coef, diag, invd, cinv, resid, direct, work, pe, lam)

    @pl.when(slab == 15)
    def _():
        arrived(top, halo_sem.at[4])
        field_terms(fext, hu, slab, DEPTH - 1, DEPTH)

    cell_products(lam, hu, chunks)

    for z in range(8):
        for c in (1, 0):
            other = src != z * 2 + c
            send(chunks.at[c, z], recv_src.at[src], src_sem, (z * 2 + c, slab), other)
            send(mis, recv_mis.at[src], mis_sem, (z * 2 + c, slab), other)
    recv_src[src] = chunks[core, zl]
    arrived(recv_mis.at[pl.ds(0, 15)], mis_sem)
    arrived(recv_src.at[pl.ds(0, 15)], src_sem)

    @pl.when(core == 1)
    def _():
        for copy in sums:
            copy.wait_send()

    for wait, when in sent:
        if when is None:
            wait()
        else:
            pl.when(when)(wait)


def finish(recv_src, recv_mis, grad_ref, misfit_ref):
    total, misfit = recv_src[0], recv_mis[0]
    for k in range(1, GROUPS):
        total, misfit = total + recv_src[k], misfit + recv_mis[k]
    grad_ref[...] = total
    misfit_ref[...] = misfit * (1.0 / (GROUPS * RX))


def on_device(conductivity, forward_fields, receiver_pairs, observed):
    field = forward_fields.reshape(DEPTH, NY, NX)
    pairs = jnp.transpose(receiver_pairs[0])
    conductivity, field, pairs, observed = (
        pltpu.with_memory_space_constraint(a, pltpu.HBM) for a in (conductivity, field, pairs, observed)
    )
    plane = (NY, NX)
    any_spec = pl.BlockSpec(memory_space=pltpu.HBM)
    vmem = pl.BlockSpec(memory_space=pltpu.VMEM)
    dma, regular = pltpu.SemaphoreType.DMA, pltpu.SemaphoreType.REGULAR
    received = pl.pallas_call(
        kernel,
        name="adjoint_gradient",
        out_shape=(
            jax.ShapeDtypeStruct((GROUPS, 8, NX), F32),
            jax.ShapeDtypeStruct((GROUPS, 1, NX), F32),
        ),
        in_specs=[any_spec] * 4,
        out_specs=(vmem, vmem),
        scratch_shapes=[
            pltpu.VMEM((CELLS, *plane), F32),
            pltpu.VMEM((DEPTH + 1, *plane), F32),
            pltpu.VMEM((2, RX), jnp.int32),
            pltpu.VMEM((GROUPS, RX), F32),
            pltpu.VMEM((IDX, NX), jnp.int32),
            pltpu.VMEM((RROWS, NX), F32),
            pltpu.VMEM((RROWS, NX), F32),
            pltpu.VMEM((2, 16, RROWS, NX), F32),
            pltpu.VMEM((2, RROWS, NX), F32),
            pltpu.VMEM((RROWS, NX), F32),
            pltpu.VMEM((IDX, 1, NX), F32),
            pltpu.VMEM((IDX, 1, NX), F32),
            pltpu.VMEM((IDX, 1, NX), F32),
            pltpu.VMEM((PLANES * NY, IDX * NX), jnp.bfloat16),
            pltpu.VMEM((NX, IDX * NX), jnp.bfloat16),
            pltpu.VMEM((3, PLANES, *plane), F32),
            pltpu.VMEM((PLANES, *plane), F32),
            pltpu.VMEM((PLANES, *plane), F32),
            pltpu.VMEM((5, *plane), F32),
            pltpu.VMEM((DEPTH, 7, *plane), F32),
            pltpu.VMEM((PLANES, *plane), F32),
            pltpu.VMEM((PLANES, *plane), F32),
            pltpu.VMEM((PLANES, *plane), F32),
            pltpu.VMEM((PLANES, *plane), F32),
            pltpu.VMEM((PLANES, *plane), F32),
            pltpu.VMEM((1, NX), F32),
            pltpu.VMEM((2, 8, 8, NX), F32),
            dma((4,)), dma, dma((3,)), dma((5,)), dma((2,)), dma((2,)), dma, dma,
            dma((3,)), dma((3,)), regular, regular,
        ],
        compiler_params=pltpu.CompilerParams(
            collective_id=0, has_side_effects=True, vmem_limit_bytes=32 * 1024 * 1024
        ),
    )(conductivity, field, pairs, observed)
    grad, misfit = pl.pallas_call(
        finish,
        name="add_groups",
        out_shape=(jax.ShapeDtypeStruct((8, NX), F32), jax.ShapeDtypeStruct((1, NX), F32)),
        in_specs=[vmem] * 2,
        out_specs=(vmem, vmem),
        compiler_params=pltpu.CompilerParams(vmem_limit_bytes=1024 * 1024),
    )(*received)
    return grad.reshape(DEPTH, 2, NX), misfit[0, 0]


def solution(mesh):
    in_specs = (P("slab", None, None), P("src", "slab", None, None), P("src", None, None), P())
    out_specs = (P("slab", "src", None), P())
    return jax.shard_map(
        on_device, mesh=mesh, in_specs=in_specs, out_specs=out_specs, check_vma=False
    )
```
